32 devices in a mesh: section: 2 (over core), dp: 16 (over z, y, x).
Axes of the slice: x: 2, y: 2, z: 4, core: 2. Of those that a mesh axis runs over, the one named last changes fastest.
Arguments:
- hidden: bfloat16 [16384, 768], P('dp'), may hold values from -6 to 6
- segment_ids: int32 [32, 512], P('dp'), may hold values from 0 to 3, never falling along the last dimension, each value on 1 to 256 neighbouring positions
- cotangent: bfloat16 [2, 16384, 768], P('section', 'dp'), may hold values from -6 to 6
- w_qkv: bfloat16 [2, 768, 2304], P('section'), may hold values from -0.21875 to 0.21875
- w_out: bfloat16 [2, 768, 768], P('section'), may hold values from -2.5 to 2.5
- w_up: bfloat16 [2, 768, 3072], P('section'), may hold values from -0.21875 to 0.21875
- w_down: bfloat16 [2, 3072, 768], P('section'), may hold values from -0.109375 to 0.109375
- biases: float32 [2, 6, 768], P('section'), may hold values from -3 to 3
- gains: float32 [2, 2, 768], P('section'), may hold values from 0.25 to 1.75
- up_bias: float32 [2, 3072], P('section'), may hold values from -3 to 3
Outputs:
- states: bfloat16 [2, 16384, 768], P('section', 'dp')
- grad_input: float32 [16384, 768], P('dp')
- grad_w_qkv: float32 [2, 768, 2304], P('section', 'dp')
- grad_w_out: float32 [2, 768, 768], P('section', 'dp')
- grad_w_up: float32 [2, 768, 3072], P('section', 'dp')
- grad_w_down: float32 [2, 3072, 768], P('section', 'dp')
- grad_biases: float32 [2, 6, 768], P('section', None, 'dp')
- grad_gains: float32 [2, 2, 768], P('section', None, 'dp')
- grad_up_bias: float32 [2, 3072], P('section', 'dp')
The draws below stay inside these ranges and needn't reach their ends.
Inputs may be any that keep to these rules, and one draw needn't show every extreme that they name: `segment_ids`: in every sequence the ids run through 0 to 3 without falling, each document 1 to 256 tokens, one exactly 256.
All inputs are finite; a program needn't handle non-finite values.
Results may differ from the reference program's by a relative error of at most 0.015.
Values may be sent and summed in bfloat16 or wider, within the bound.
A program may use at most 256 MiB of HBM per device.

```python
import math
import jax
import jax.numpy as jnp
import numpy as np
from jax import lax

D = 768
HEADS = 12
FF = 3072
SEQ_LEN = 512
DOCS = 4
MOST = 256
SEQS = 32
TOKENS = 16384


def strengthened(values, rng, source, target, shards_of, factor):
    def block_of(position):
        return (jnp.arange(values.shape[position]) // (values.shape[position] // shards_of)).reshape((-1,) + (1,) * (values.ndim - 1 - position))

    first = jax.random.permutation(rng, shards_of)[block_of(target)]
    second = (block_of(target) + shards_of // 2) % shards_of
    return jnp.where((block_of(source) == first) | (block_of(source) == second), factor * values, values)


def steps_of(rng, shape, cuts, smallest, high):
    def one(position, shards_of):
        steps = jax.random.uniform(jax.random.fold_in(jax.random.fold_in(rng, 6), position), (shards_of,), jnp.float32, smallest / len(cuts), high / len(cuts))
        return jnp.repeat(jnp.exp(steps), shape[position] // shards_of).reshape((-1,) + (1,) * (len(shape) - position - 1))

    factor_of = one(*cuts[0])
    for cut in cuts[1:]:
        factor_of = factor_of * one(*cut)
    return factor_of


def split_up(amount, total, reach, lean):
    weights = [(1 << 20) // math.isqrt(standing ** lean) + 1 for standing in range(2, amount + 1)]
    rest, holding = total - reach - (amount - 1), [1] * (amount - 1)
    while rest > 0:
        candidates = [i for i in range(amount - 1) if holding[i] < reach]
        whole, left = sum([weights[i] for i in candidates]), rest
        for i in candidates:
            more = min(reach - holding[i], max(1, left * weights[i] // whole), rest)
            holding[i] = holding[i] + more
            rest = rest - more
    return np.array([reach] + holding)


def uneven(own_key, count, total, most, lean):
    if count == 2:
        one = jax.random.randint(own_key, (), max(1, total - most), min(most, total - 1) + 1)
        return jnp.stack([one, total - one])
    lengths = jnp.asarray(split_up(count, total, most, lean), jnp.int32)
    pairs = (count - 1) // 2
    source_of, sink = lengths[1:1 + 2 * pairs:2], lengths[2:2 + 2 * pairs:2]
    slack = jnp.minimum(source_of - 1, most - sink)
    moved = jax.random.randint(jax.random.fold_in(own_key, 1), (pairs,), 0, 1 << 20) % (slack + 1)
    lengths = lengths.at[1:1 + 2 * pairs:2].set(source_of - moved).at[2:2 + 2 * pairs:2].set(sink + moved)
    return lengths[jax.random.permutation(jax.random.fold_in(own_key, 2), count)]


def gaussian(rng, shape, width, most, split=(), dtype=jnp.bfloat16):
    entries = jax.random.normal(rng, shape, jnp.float32) * width
    if len(split) > 0:
        entries = steps_of(rng, shape, split, -0.22, 0.18) * entries
    return jnp.clip(entries, min=-most, max=most).astype(dtype)


def noise_with(stream_key, shape, deviation, bound, cuts, heavy, held_as=jnp.bfloat16):
    result = deviation * jax.random.normal(stream_key, shape, jnp.float32)
    if cuts:
        result = result * steps_of(stream_key, shape, cuts, -0.22, 0.18)
    return jnp.clip(strengthened(result, jax.random.fold_in(stream_key, 3), *heavy), -bound, bound).astype(held_as)


def setup_inputs(seed: int = 0) -> dict:
    arg_keys = jax.random.split(jax.random.key(seed), 11)
    return {
        "hidden": noise_with(arg_keys[0], (TOKENS, D), 1.0, 6.0, ((0, 16),), (0, 1, 16, 2.0)),
        "segment_ids": jax.vmap(lambda own: jnp.searchsorted(jnp.cumsum(uneven(own, DOCS, SEQ_LEN, MOST, 1)), jnp.arange(SEQ_LEN), side="right"))(jax.random.split(arg_keys[1], SEQS)).reshape((SEQS, SEQ_LEN)).astype(jnp.int32),
        "cotangent": noise_with(arg_keys[2], (2, TOKENS, D), 1.0, 6.0, ((0, 2), (1, 16)), (1, 2, 16, 2.0)),
        "w_qkv": gaussian(arg_keys[3], (2, D, 3 * D), D ** -0.5, 0.21875, ((0, 2),)),
        "w_out": gaussian(arg_keys[4], (2, D, D), (D * DOCS // SEQ_LEN) ** -0.5, 2.5, ((0, 2),)),
        "w_up": gaussian(arg_keys[5], (2, D, FF), D ** -0.5, 0.21875, ((0, 2),)),
        "w_down": gaussian(arg_keys[6], (2, FF, D), FF ** -0.5, 0.109375, ((0, 2),)),
        "biases": gaussian(arg_keys[7], (2, 6, D), 0.5, 3.0, ((0, 2),), jnp.float32),
        "gains": jnp.clip(1.0 + 0.15 * jax.random.normal(arg_keys[8], (2, 2, D), jnp.float32), 0.25, 1.75),
        "up_bias": gaussian(arg_keys[9], (2, FF), 0.5, 3.0, ((0, 2),), jnp.float32),
    }


norm_eps = 1e-12
masked_score = -1e+30

@jax.custom_vjp
def low(v):
    return lax.optimization_barrier(v.astype(jnp.bfloat16)).astype(jnp.float32)

@jax.custom_vjp
def low_back(v):
    return v

def low_keep(v):
    return (low(v), None)

def low_pass(kept, grad):
    return (grad,)

def back_keep(v):
    return (v, None)

def back_low(kept, grad):
    return (low(grad),)
low.defvjp(low_keep, low_pass)
low_back.defvjp(back_keep, back_low)

def product(left_side, right_side):
    return jnp.matmul(left_side, right_side, precision=lax.Precision.HIGHEST)

def norm_rows(residue):
    centered = residue - lax.optimization_barrier(jnp.mean(residue, axis=-1, keepdims=True))
    return centered * lax.rsqrt(lax.optimization_barrier(jnp.mean(centered * centered, axis=-1, keepdims=True)) + norm_eps)

def attend_seq(operands):
    queries, key_rows, value_rows, segments = operands
    length = queries.shape[0]
    query_per_head = queries.reshape(length, HEADS, -1)
    key_per_head = key_rows.reshape(length, HEADS, -1)
    value_per_head = value_rows.reshape(length, HEADS, -1)
    score_scale = query_per_head.shape[-1] ** (-0.5)
    unscaled_scores = jnp.einsum('syn,byn->ysb', query_per_head, key_per_head, precision=lax.Precision.HIGHEST) * score_scale
    same_doc = segments[:, None] == segments[None, :]
    scores = low_back(jnp.where(same_doc[None], unscaled_scores, masked_score))
    maximum = lax.optimization_barrier(jnp.max(scores, axis=-1, keepdims=True))
    attention_weight = jnp.exp(scores - maximum)
    attention_probs = low(attention_weight / lax.optimization_barrier(jnp.sum(attention_weight, axis=-1, keepdims=True)))
    attention_result = jnp.einsum('zea,azq->ezq', attention_probs, value_per_head, precision=lax.Precision.HIGHEST)
    return low_back(low(attention_result.reshape(length, -1)))

def block_apply(inputs, segments, params):
    w_qkv, w_out, w_up, w_down, biases, gains, up_bias = params
    projected = low_back(product(inputs, w_qkv))
    queries = low(projected[..., :D] + biases[0])
    key_rows = low(projected[..., D:2 * D])
    value_rows = low(projected[..., 2 * D:] + biases[1])
    attention_result = lax.map(jax.checkpoint(attend_seq), (queries, key_rows, value_rows, segments))
    mixed_out = low_back(product(attention_result, w_out)) + biases[2]
    hidden = norm_rows(inputs + mixed_out) * gains[0] + biases[3]
    preact = low_back(product(low(hidden), w_up)) + up_bias
    active = low(jax.nn.gelu(preact, approximate=False))
    ffn_out = low_back(product(active, w_down)) + biases[4]
    return norm_rows(hidden + ffn_out) * gains[1] + biases[5]

def two_blocks(inputs, segments, params):
    first_params = tuple((member[0] for member in params))
    head_params = tuple((member[1] for member in params))
    first_out = block_apply(inputs, segments, first_params)
    positions = jnp.arange(segments.shape[-1])
    is_first = (positions == 0) | (segments != jnp.roll(segments, 1, axis=-1))
    head_in = jnp.where(is_first[..., None], low_back(low(first_out)), inputs)
    head_out = block_apply(head_in, segments, head_params)
    return (first_out, head_out)

def reference(hidden, segment_ids, cotangent, w_qkv, w_out, w_up, w_down, biases, gains, up_bias):
    params = tuple((member.astype(jnp.float32) for member in (w_qkv, w_out, w_up, w_down, biases, gains, up_bias)))
    seq_total = segment_ids.shape[0]
    group_size = math.gcd(seq_total, max(1, 4096 // SEQ_LEN))
    step_count = seq_total // group_size
    inputs = hidden.astype(jnp.float32).reshape(step_count, group_size, SEQ_LEN, D)
    segments = segment_ids.reshape(step_count, group_size, SEQ_LEN)
    cot_pair = cotangent.astype(jnp.float32).reshape(2, step_count, group_size, SEQ_LEN, D)

    def scan_step(running, sliced):
        group_in, group_seg, grad_first, grad_head = sliced

        def forward(values_in, weights_in):
            return two_blocks(values_in, group_seg, weights_in)
        outputs, pullback = jax.vjp(forward, group_in, params)
        grad_in, grad_params = pullback((grad_first, grad_head))
        running = jax.tree.map(jnp.add, running, grad_params)
        return (running, (outputs[0].astype(jnp.bfloat16), outputs[1].astype(jnp.bfloat16), grad_in))
    zeros_start = jax.tree.map(jnp.zeros_like, params)
    totals, (first_states, head_states, grad_input) = lax.scan(scan_step, zeros_start, (inputs, segments, cot_pair[0], cot_pair[1]))
    states = jnp.stack([first_states.reshape(-1, D), head_states.reshape(-1, D)])
    return (states, grad_input.reshape(-1, D), totals[0], totals[1], totals[2], totals[3], totals[4], totals[5], totals[6])
```

```python
import functools

import jax
import jax.numpy as jnp
from jax import lax
from jax.experimental import pallas as pl
from jax.experimental.pallas import tpu as pltpu
from jax.sharding import PartitionSpec as P

HEADS = 12
HEAD = 64
NORM_EPS = 1e-12
MASKED = -1e30
INV_ROOT_TWO = 0.7071067811865476
INV_ROOT_TAU = 0.3989422804014327
MESH = pl.DeviceIdType.MESH
BF = jnp.bfloat16
F32 = jnp.float32
TILE = 256
ROWS = 128
VMEM_BYTES = 60 * 1024 * 1024


def dot_nn(a, b):
    return lax.dot_general(a, b, (((1,), (0,)), ((), ())), preferred_element_type=F32)


def dot_nt(a, b):
    return lax.dot_general(a, b, (((1,), (1,)), ((), ())), preferred_element_type=F32)


def dot_tn(a, b):
    return lax.dot_general(a, b, (((0,), (0,)), ((), ())), preferred_element_type=F32)


def loop(count, body):
    def step(i, carry):
        body(i)
        return carry

    lax.fori_loop(0, count, step, 0)


def tile_of(i, size=TILE):
    return pl.ds(pl.multiple_of(i * size, size), size)


class Weights:
    def __init__(self, block, pairs, targets, sems):
        self.waits = []
        own = lax.axis_index("section") == block
        for n, ((mine, theirs), target) in enumerate(zip(pairs, targets)):
            sem = sems.at[n]

            @pl.when(own)
            def _():
                pltpu.make_async_copy(mine, target, sem).start()

            @pl.when(jnp.logical_not(own))
            def _():
                pltpu.make_async_copy(theirs, target, sem).start()

            self.waits.append(pltpu.make_async_copy(mine, target, sem))

    def wait(self, n):
        self.waits[n].wait()


def normed_rows(residue):
    centered = residue - jnp.mean(residue, axis=-1, keepdims=True)
    inv = lax.rsqrt(jnp.mean(centered * centered, axis=-1, keepdims=True) + NORM_EPS)
    return centered * inv, inv


def lane_masks(shape):
    lane = lax.broadcasted_iota(jnp.int32, shape, 1)
    return (lane < HEAD, lane >= HEAD)


def forward_kernel(
    block,
    x_ref, segr_ref, segc_ref, first_ref, qkvb_ref, small_ref, upb_ref,
    wqkv_m, wqkv_t, wout_m, wout_t, wup_m, wup_t, wdown_m, wdown_t,
    qkv_ref, o_ref, lse_ref, n1_ref, inv1_ref, hlow_ref, g_ref, slope_ref, n2_ref, inv2_ref, y_ref, x1_ref,
    wqkv, wout, wup, wdown, mask_ref, res_ref, h_ref, sems,
):
    rows, width = x_ref.shape
    hidden_width = wup.shape[1]
    weights = Weights(
        block,
        ((wqkv_m, wqkv_t), (wout_m, wout_t), (wup_m, wup_t), (wdown_m, wdown_t)),
        (wqkv, wout, wup, wdown),
        sems,
    )
    mask_ref[...] = jnp.where(segc_ref[...] == segr_ref[...], 0.0, MASKED)
    weights.wait(0)
    x = x_ref[...]

    def project(j):
        cols = tile_of(j)
        scale = jnp.where(j < width // TILE, HEAD ** -0.5, 1.0)
        qkv_ref[:, cols] = ((dot_nn(x_ref[...], wqkv[:, cols]) + qkvb_ref[:, cols]) * scale).astype(BF)

    loop(3 * width // TILE, project)

    def attend(pair):
        queries = qkv_ref[:, tile_of(pair, 128)]
        keys = qkv_ref[:, pl.ds(pl.multiple_of(width + pair * 128, 128), 128)]
        values = qkv_ref[:, pl.ds(pl.multiple_of(2 * width + pair * 128, 128), 128)]
        masks = lane_masks((rows, 128))
        parts = []
        for h in range(2):
            scores = dot_nt(keys, jnp.where(masks[h], queries, jnp.zeros_like(queries))) + mask_ref[...]
            top = jnp.max(scores, axis=0, keepdims=True)
            weight = jnp.exp(scores - top)
            total = jnp.sum(weight, axis=0, keepdims=True)
            lse_ref[pair, pl.ds(h, 1), :] = top + jnp.log(total)
            result = dot_tn(values, weight.astype(BF))
            parts.append(result[h * HEAD : (h + 1) * HEAD] * (1.0 / total))
        o_ref[:, tile_of(pair, 128)] = jnp.concatenate(parts, axis=0).T.astype(BF)

    loop(HEADS // 2, attend)
    weights.wait(1)

    def mix(j):
        cols = tile_of(j)
        res_ref[:, cols] = x_ref[:, cols].astype(F32) + (dot_nn(o_ref[...], wout[:, cols]) + small_ref[2:3, cols])

    loop(width // TILE, mix)

    def norm_one(i):
        r = tile_of(i, ROWS)
        normed, inv = normed_rows(res_ref[r, :])
        n1_ref[r, :] = normed
        inv1_ref[r, :] = jnp.broadcast_to(inv, (ROWS, 128))
        h = normed * small_ref[6:7, :] + small_ref[3:4, :]
        h_ref[r, :] = h
        hlow_ref[r, :] = h.astype(BF)

    loop(rows // ROWS, norm_one)
    weights.wait(2)

    def widen(j):
        cols = tile_of(j)
        z = dot_nn(hlow_ref[...], wup[:, cols]) + upb_ref[:, cols]
        half = 0.5 * (1.0 + lax.erf(z * INV_ROOT_TWO))
        g_ref[:, cols] = (z * half).astype(BF)
        slope_ref[:, cols] = (half + z * jnp.exp(-0.5 * z * z) * INV_ROOT_TAU).astype(BF)

    loop(hidden_width // TILE, widen)
    weights.wait(3)

    def narrow(j):
        cols = tile_of(j)
        res_ref[:, cols] = h_ref[:, cols] + (dot_nn(g_ref[...], wdown[:, cols]) + small_ref[4:5, cols])

    loop(width // TILE, narrow)

    def norm_two(i):
        r = tile_of(i, ROWS)
        normed, inv = normed_rows(res_ref[r, :])
        n2_ref[r, :] = normed
        inv2_ref[r, :] = jnp.broadcast_to(inv, (ROWS, 128))
        y = (normed * small_ref[7:8, :] + small_ref[5:6, :]).astype(BF)
        y_ref[r, :] = y
        x1_ref[r, :] = jnp.where(first_ref[r, :] > 0.5, y.astype(F32), x_ref[r, :].astype(F32)).astype(BF)

    loop(rows // ROWS, norm_two)


def norm_back(gradient, normed, inv):
    return inv * (
        gradient
        - jnp.mean(gradient, axis=-1, keepdims=True)
        - normed * jnp.mean(gradient * normed, axis=-1, keepdims=True)
    )


def column_sum(v):
    return jnp.sum(v, axis=0, keepdims=True)


def backward_kernel(
    block,
    cot_ref, dnext_ref, segr_ref, segc_ref, first_ref, small_ref,
    qkv_ref, o_ref, lse_ref, n1_ref, inv1_ref, slope_ref, n2_ref, inv2_ref,
    wqkv_m, wqkv_t, wout_m, wout_t, wup_m, wup_t, wdown_m, wdown_t,
    dx_ref, dproj_ref, da_ref, dz_ref, df_ref, dsmall_ref, dup_ref,
    wqkv, wout, wup, wdown, mask_ref, dr_ref, dh_ref, do_ref, sems,
):
    rows, width = cot_ref.shape
    hidden_width = wup.shape[1]
    weights = Weights(
        block,
        ((wdown_m, wdown_t), (wup_m, wup_t), (wout_m, wout_t), (wqkv_m, wqkv_t)),
        (wdown, wup, wout, wqkv),
        sems,
    )
    mask_ref[...] = jnp.where(segc_ref[...] == segr_ref[...], 0.0, MASKED)
    dsmall_ref[...] = jnp.zeros_like(dsmall_ref)

    def norm_two(i):
        r = tile_of(i, ROWS)
        gradient = cot_ref[r, :].astype(F32)
        if block == 0:
            back = dnext_ref[r, :].astype(BF).astype(F32)
            gradient = gradient + jnp.where(first_ref[r, :] > 0.5, back, 0.0)
        normed = n2_ref[r, :]
        dr = norm_back(gradient * small_ref[7:8, :], normed, inv2_ref[r, 0:1])
        dr_ref[r, :] = dr
        df_ref[r, :] = dr.astype(BF)
        dsmall_ref[7:8, :] += column_sum(gradient * normed)
        dsmall_ref[5:6, :] += column_sum(gradient)
        dsmall_ref[4:5, :] += column_sum(dr)

    loop(rows // ROWS, norm_two)
    weights.wait(0)

    def narrow(j):
        cols = tile_of(j)
        dz = dot_nt(df_ref[...], wdown[cols, :]) * slope_ref[:, cols].astype(F32)
        dup_ref[:, cols] = column_sum(dz)
        dz_ref[:, cols] = dz.astype(BF)

    loop(hidden_width // TILE, narrow)
    weights.wait(1)

    def widen(j):
        cols = tile_of(j)
        dh_ref[:, cols] = dr_ref[:, cols] + dot_nt(dz_ref[...], wup[cols, :])

    loop(width // TILE, widen)

    def norm_one(i):
        r = tile_of(i, ROWS)
        gradient = dh_ref[r, :]
        normed = n1_ref[r, :]
        dr = norm_back(gradient * small_ref[6:7, :], normed, inv1_ref[r, 0:1])
        dr_ref[r, :] = dr
        da_ref[r, :] = dr.astype(BF)
        dsmall_ref[6:7, :] += column_sum(gradient * normed)
        dsmall_ref[3:4, :] += column_sum(gradient)
        dsmall_ref[2:3, :] += column_sum(dr)

    loop(rows // ROWS, norm_one)
    weights.wait(2)

    def mix(j):
        cols = tile_of(j)
        do_ref[:, cols] = dot_nt(da_ref[...], wout[cols, :]).astype(BF)

    loop(width // TILE, mix)

    def attend(pair):
        here = tile_of(pair, 128)
        key_cols = pl.ds(pl.multiple_of(width + pair * 128, 128), 128)
        value_cols = pl.ds(pl.multiple_of(2 * width + pair * 128, 128), 128)
        queries, keys, values = qkv_ref[:, here], qkv_ref[:, key_cols], qkv_ref[:, value_cols]
        grad = do_ref[:, here]
        masks = lane_masks((rows, 128))
        dq, dk, dv = [], 0.0, 0.0
        for h in range(2):
            head_queries = jnp.where(masks[h], queries, jnp.zeros_like(queries))
            head_grad = jnp.where(masks[h], grad, jnp.zeros_like(grad))
            scores = dot_nt(keys, head_queries) + mask_ref[...]
            weight = jnp.exp(scores - lse_ref[pair, pl.ds(h, 1), :])
            dweight = dot_nt(values, head_grad)
            delta = jnp.sum(weight * dweight, axis=0, keepdims=True)
            dscore = (weight * (dweight - delta)).astype(BF)
            dq.append(dot_tn(keys, dscore)[h * HEAD : (h + 1) * HEAD])
            dk = dk + dot_nn(dscore, head_queries)
            dv = dv + dot_nn(weight.astype(BF), head_grad)
        dq = jnp.concatenate(dq, axis=0).T * (HEAD ** -0.5)
        dsmall_ref[0:1, here] = column_sum(dq)
        dsmall_ref[1:2, here] = column_sum(dv)
        dproj_ref[:, here] = dq.astype(BF)
        dproj_ref[:, key_cols] = dk.astype(BF)
        dproj_ref[:, value_cols] = dv.astype(BF)

    loop(HEADS // 2, attend)
    weights.wait(3)

    def project(j):
        cols = tile_of(j)
        dx = dr_ref[:, cols] + dot_nt(dproj_ref[...], wqkv[cols, :])
        if block == 0:
            dx = dx + jnp.where(first_ref[...] > 0.5, 0.0, dnext_ref[:, cols])
        dx_ref[:, cols] = dx

    loop(width // TILE, project)


def in_vmem(count):
    return [pl.BlockSpec(memory_space=pltpu.VMEM)] * count


def in_hbm(count):
    return [pl.BlockSpec(memory_space=pl.ANY)] * count


def shaped(shape, dtype=F32):
    return jax.ShapeDtypeStruct(shape, dtype)


def block_forward(block, x, segr, segc, first, qkvb, small, upb, weights):
    rows, width = x.shape
    hidden_width = upb.shape[1]
    scratch = [pltpu.VMEM(w.shape, BF) for w in weights[::2]]
    return pl.pallas_call(
        functools.partial(forward_kernel, block),
        out_shape=(
            shaped((rows, 3 * width), BF), shaped((rows, width), BF), shaped((HEADS // 2, 2, rows)),
            shaped((rows, width)), shaped((rows, 128)), shaped((rows, width), BF),
            shaped((rows, hidden_width), BF), shaped((rows, hidden_width), BF),
            shaped((rows, width)), shaped((rows, 128)), shaped((rows, width), BF), shaped((rows, width), BF),
        ),
        in_specs=in_vmem(7) + in_hbm(8),
        out_specs=tuple(in_vmem(12)),
        scratch_shapes=scratch + [
            pltpu.VMEM((rows, rows), F32), pltpu.VMEM((rows, width), F32), pltpu.VMEM((rows, width), F32),
            pltpu.SemaphoreType.DMA((4,)),
        ],
        compiler_params=pltpu.CompilerParams(vmem_limit_bytes=VMEM_BYTES),
        name="forward" + str(block),
    )(x, segr, segc, first, qkvb, small, upb, *weights)


def block_backward(block, cot, dnext, segr, segc, first, small, kept, weights):
    rows, width = cot.shape
    hidden_width = weights[4].shape[1]
    scratch = [pltpu.VMEM(w.shape, BF) for w in weights[::2]]
    return pl.pallas_call(
        functools.partial(backward_kernel, block),
        out_shape=(
            shaped((rows, width)), shaped((rows, 3 * width), BF), shaped((rows, width), BF),
            shaped((rows, hidden_width), BF), shaped((rows, width), BF), shaped((16, width)), shaped((1, hidden_width)),
        ),
        in_specs=in_vmem(14) + in_hbm(8),
        out_specs=tuple(in_vmem(7)),
        scratch_shapes=scratch + [
            pltpu.VMEM((rows, rows), F32), pltpu.VMEM((rows, width), F32), pltpu.VMEM((rows, width), F32),
            pltpu.VMEM((rows, width), BF), pltpu.SemaphoreType.DMA((4,)),
        ],
        compiler_params=pltpu.CompilerParams(vmem_limit_bytes=VMEM_BYTES),
        name="backward" + str(block),
    )(cot, dnext, segr, segc, first, small, *kept, *weights)


ORDERS = {"A": (0, 1, 2, 3), "B": (1, 0, 2, 3), "C": (2, 3, 0, 1), "D": (2, 3, 1, 0)}
KINDS = "ABABABABABCD"
BITS = 4
PARTS = 1 << BITS


def sum_kernel(*refs):
    operands = (refs[0:8], refs[8:16])
    small_ref = refs[16]
    out_qkv, out_out, out_up, out_down, out_small = refs[17:22]
    held = refs[22:30]
    (total, outgoing, r1, r2, r3, r4, small_sum, small_in,
     send, recv, load, small_send, small_recv) = refs[30:]
    received = (r1, r2, r3, r4)
    chunks, share, width = total.shape[0], total.shape[-2], total.shape[-1]
    sec, me = lax.axis_index("section"), lax.axis_index("dp")
    bits = [(me >> k) & 1 for k in range(BITS)]

    def fetch(block, names):
        for n in names:
            for b in range(2):

                @pl.when(block == b)
                def _():
                    pltpu.make_async_copy(operands[b][n], held[n], load.at[n]).start()

    def fetched(names):
        for n in names:
            pltpu.make_async_copy(operands[0][n], held[n], load.at[n]).wait()

    barrier = pltpu.get_barrier_semaphore()
    for k in range(BITS):
        pl.semaphore_signal(barrier, inc=1, device_id={"dp": me ^ (1 << k)}, device_id_type=MESH)
    pl.semaphore_signal(barrier, inc=1, device_id={"section": 1 - sec}, device_id_type=MESH)
    qkv, out, up, down = (0, 1), (2, 3), (4, 5), (6, 7)
    for names in (down, up, qkv, out):
        fetch(1 - sec, names)
    pl.semaphore_wait(barrier, BITS + 1)

    def place(part):
        return tuple((part >> (BITS - 1 - k)) & 1 for k in range(BITS))

    def across(chunk):
        return pltpu.make_async_remote_copy(
            src_ref=outgoing.at[chunk], dst_ref=total.at[chunk],
            send_sem=send.at[chunk, 0], recv_sem=recv.at[chunk, 0],
            device_id={"section": 1 - sec}, device_id_type=MESH,
        )

    def product(target, add, left, left_col, right, right_col, chunk_of):
        for n in range(width // TILE):
            cols = pl.ds(n * TILE, TILE)
            rhs_cols = pl.ds(pl.multiple_of(right_col + n * TILE, TILE), TILE)
            result = dot_tn(held[left][:, pl.ds(pl.multiple_of(left_col, TILE), width)], held[right][:, rhs_cols])
            for piece in range(PARTS):
                chunk, part = chunk_of(piece)
                at = (chunk,) + tuple(part) + (slice(None), cols)
                value = result[piece * share : (piece + 1) * share]
                if add:
                    value = value + target[at].astype(F32)
                target[at] = value.astype(BF)

    def products_wide(add, names, first, count):
        target = total if add else outgoing

        def one(j):
            chunk = first + j
            if add:
                across(chunk).wait()
            product(target, add, names[0], 0, names[1], j * width, lambda piece: (chunk, place(piece)))
            if not add:
                across(chunk).start()

        loop(count, one)

    def products_tall(add, names, first, count):
        target = total if add else outgoing

        def one(j):
            def chunk_of(piece):
                return first + piece % count, place(j * (PARTS // count) + piece // count)

            product(target, add, names[0], j * width, names[1], 0, chunk_of)

        if add:
            for chunk in range(first, first + count):
                across(chunk).wait()
        loop(count, one)
        if not add:
            for chunk in range(first, first + count):
                across(chunk).start()

    def exchange(chunk, phase):
        order = ORDERS[KINDS[chunk]]
        at = [slice(None)] * BITS
        for done in range(phase):
            at[BITS - 1 - order[done]] = bits[order[done]]
        at[BITS - 1 - order[phase]] = 1 - bits[order[phase]]
        return pltpu.make_async_remote_copy(
            src_ref=total.at[(chunk,) + tuple(at)], dst_ref=received[phase].at[chunk],
            send_sem=send.at[chunk, phase + 1], recv_sem=recv.at[chunk, phase + 1],
            device_id={"dp": me ^ (1 << order[phase])}, device_id_type=MESH,
        )

    def take(chunk, phase):
        order = ORDERS[KINDS[chunk]]
        exchange(chunk, phase).wait()

        def one(i):
            at, inner, left = [None] * BITS, [], i
            for done in range(phase + 1):
                at[BITS - 1 - order[done]] = bits[order[done]]
            for d in reversed([d for d in range(BITS) if at[d] is None]):
                at[d] = left % 2
                inner.insert(0, at[d])
                left = left // 2
            at = (chunk,) + tuple(at)
            value = total[at].astype(F32) + received[phase][(chunk,) + tuple(inner)].astype(F32)
            total[at] = value.astype(BF)

        if phase < BITS - 1:
            loop(PARTS >> (phase + 1), one)
            exchange(chunk, phase + 1).start()
        else:
            value = total[(chunk,) + tuple(bits[BITS - 1 - d] for d in range(BITS))].astype(F32)
            value = value + received[phase][chunk].astype(F32)
            if chunk < 3:
                out_qkv[:, chunk * width : (chunk + 1) * width] = value
            elif chunk < 4:
                out_out[...] = value
            elif chunk < 8:
                out_up[:, (chunk - 4) * width : (chunk - 3) * width] = value
            else:
                out_down[(chunk - 8) * share : (chunk - 7) * share, :] = value

    def small_exchange(phase):
        target = {"section": 1 - sec} if phase == 0 else {"dp": me ^ (1 << (phase - 1))}
        source = small_ref.at[1 - sec] if phase == 0 else small_sum.at[phase]
        return pltpu.make_async_remote_copy(
            src_ref=source, dst_ref=small_in.at[phase], send_sem=small_send.at[phase], recv_sem=small_recv.at[phase],
            device_id=target, device_id_type=MESH,
        )

    def small_take(phase):
        small_exchange(phase).wait()
        before = small_ref[sec] if phase == 0 else small_sum[phase]
        if phase < BITS:
            small_sum[phase + 1] = before + small_in[phase]
            small_exchange(phase + 1).start()
        else:
            out_small[...] = before + small_in[phase]

    small_exchange(0).start()
    fetched(down)
    products_tall(False, down, 8, 4)
    fetch(sec, down)
    fetched(up)
    products_wide(False, up, 4, 4)
    fetch(sec, up)
    fetched(down)
    products_tall(True, down, 8, 4)
    for chunk in range(8, 12):
        exchange(chunk, 0).start()
    fetched(qkv)
    products_wide(False, qkv, 0, 3)
    fetch(sec, qkv)
    fetched(up)
    products_wide(True, up, 4, 4)
    for chunk in range(4, 8):
        exchange(chunk, 0).start()
    fetched(out)
    products_wide(False, out, 3, 1)
    fetch(sec, out)
    fetched(qkv)
    products_wide(True, qkv, 0, 3)
    for chunk in range(0, 3):
        exchange(chunk, 0).start()
    fetched(out)
    products_wide(True, out, 3, 1)
    exchange(3, 0).start()
    for phase in range(BITS):
        small_take(phase)
        for chunk in (8, 9, 10, 11, 4, 5, 6, 7, 0, 1, 2, 3):
            take(chunk, phase)
    small_take(BITS)


def sum_products(pieces, small):
    rows, width = pieces[0][0].shape
    hidden_width = pieces[0][6].shape[1]
    share = width // PARTS
    chunks = 2 * hidden_width // width + 4
    return pl.pallas_call(
        sum_kernel,
        out_shape=(
            shaped((share, 3 * width)), shaped((share, width)), shaped((share, hidden_width)),
            shaped((hidden_width // PARTS, width)), shaped((16, width)),
        ),
        in_specs=in_hbm(16) + in_vmem(1),
        out_specs=tuple(in_vmem(5)),
        scratch_shapes=[pltpu.VMEM(piece.shape, BF) for piece in pieces[0]] + [
            pltpu.VMEM((chunks, 2, 2, 2, 2, share, width), BF),
            pltpu.VMEM((chunks, 2, 2, 2, 2, share, width), BF),
            pltpu.VMEM((chunks, 2, 2, 2, share, width), BF),
            pltpu.VMEM((chunks, 2, 2, share, width), BF),
            pltpu.VMEM((chunks, 2, share, width), BF),
            pltpu.VMEM((chunks, share, width), BF),
            pltpu.VMEM((BITS + 1, 16, width), F32),
            pltpu.VMEM((BITS + 1, 16, width), F32),
            pltpu.SemaphoreType.DMA((chunks, BITS + 1)),
            pltpu.SemaphoreType.DMA((chunks, BITS + 1)),
            pltpu.SemaphoreType.DMA((8,)),
            pltpu.SemaphoreType.DMA((BITS + 1,)),
            pltpu.SemaphoreType.DMA((BITS + 1,)),
        ],
        compiler_params=pltpu.CompilerParams(
            collective_id=0, has_side_effects=True, vmem_limit_bytes=VMEM_BYTES
        ),
        name="sum_products",
    )(*pieces[0], *pieces[1], small)


def sum_plainly(pieces, small):
    def scattered(names):
        both = jnp.stack([dot_tn(pieces[b][names[0]], pieces[b][names[1]]) for b in range(2)])
        own = lax.psum_scatter(both, "section", scatter_dimension=0, tiled=False)
        return lax.psum_scatter(own, "dp", scatter_dimension=0, tiled=True)

    own_small = lax.psum(lax.psum_scatter(small, "section", scatter_dimension=0, tiled=False), "dp")
    return tuple(scattered(names) for names in ((0, 1), (2, 3), (4, 5), (6, 7))) + (own_small,)


def swap(value):
    return lax.ppermute(value, "section", [(0, 1), (1, 0)])


def local(hidden, segment_ids, cotangent, w_qkv, w_out, w_up, w_down, biases, gains, up_bias):
    sec, me = lax.axis_index("section"), lax.axis_index("dp")
    count = lax.axis_size("dp")
    length, width = segment_ids.shape[1], hidden.shape[1]
    rows = hidden.shape[0] // 2
    assert rows == length

    def rows_of(matrix, half):
        return lax.dynamic_slice_in_dim(matrix, half * rows, rows, 0)

    def by_block(mine, theirs):
        return jnp.where(sec == 0, mine, theirs), jnp.where(sec == 0, theirs, mine)

    mine = (w_qkv[0], w_out[0], w_up[0], w_down[0])
    weights = []
    for own in mine:
        weights += [own, swap(own)]
    packed = jnp.concatenate([biases[0], gains[0], up_bias[0].reshape(-1, width)], axis=0)
    smalls = by_block(packed, swap(packed))
    cots = by_block(rows_of(cotangent[0], sec), swap(rows_of(cotangent[0], 1 - sec)))
    x = rows_of(hidden, sec)
    segments = lax.dynamic_index_in_dim(segment_ids, sec, 0, False)
    segr, segc = segments.reshape(1, rows), segments.reshape(rows, 1)
    first = jnp.concatenate([jnp.ones((1,), F32), (segments[1:] != segments[:-1]).astype(F32)]).reshape(rows, 1)

    inputs, kept, states = [x], [], []
    for block in range(2):
        small = smalls[block]
        qkvb = jnp.concatenate([small[0:1], jnp.zeros((1, width), F32), small[1:2]], axis=1)
        result = block_forward(block, inputs[block], segr, segc, first, qkvb, small, small[8:].reshape(1, -1), weights)
        kept.append(result[:10])
        states.append(result[10])
        inputs.append(result[11])

    pieces, dsmalls, dnext = [None, None], [None, None], x
    for block in (1, 0):
        qkv, o, lse, n1, inv1, hlow, g, slope, n2, inv2 = kept[block]
        dnext, dproj, da, dz, df, dsmall, dup = block_backward(
            block, cots[block], dnext, segr, segc, first, smalls[block],
            (qkv, o, lse, n1, inv1, slope, n2, inv2), weights,
        )
        pieces[block] = (inputs[block], dproj, o, da, hlow, dz, g, df)
        dsmalls[block] = jnp.concatenate([dsmall[:8], dup.reshape(-1, width), jnp.zeros((4, width), F32)], axis=0)
    small = jnp.stack(dsmalls)
    fits = count == PARTS and width % (16 * PARTS) == 0
    sums = (sum_products if fits else sum_plainly)(pieces, small)
    gqkv, gout, gup, gdown, gsmall = sums
    share, up_share = width // count, up_bias.shape[1] // count
    columns = lax.dynamic_slice_in_dim(gsmall[:8], me * share, share, 1)
    gup_bias = lax.dynamic_slice_in_dim(gsmall[8:12].reshape(-1), me * up_share, up_share, 0)

    own_states = jnp.where(sec == 0, states[0], states[1])
    other_states = swap(jnp.where(sec == 0, states[1], states[0]))
    both_states = jnp.concatenate(by_block(own_states, other_states), axis=0)
    grad_input = jnp.concatenate(by_block(dnext, swap(dnext)), axis=0)
    totals = (gqkv, gout, gup, gdown, columns[:6], columns[6:], gup_bias)
    return (both_states[None], grad_input) + tuple(member[None] for member in totals)


def solution(mesh):
    placed = (
        P("dp", None),
        P("dp", None),
        P("section", "dp", None),
        P("section", None, None),
        P("section", None, None),
        P("section", None, None),
        P("section", None, None),
        P("section", None, None),
        P("section", None, None),
        P("section", None),
    )
    return jax.shard_map(
        local,
        mesh=mesh,
        in_specs=placed,
        out_specs=(
            P("section", "dp", None),
            P("dp", None),
            P("section", "dp", None),
            P("section", "dp", None),
            P("section", "dp", None),
            P("section", "dp", None),
            P("section", None, "dp"),
            P("section", None, "dp"),
            P("section", "dp"),
        ),
        check_vma=False,
    )
```

```python
import functools

import jax
import jax.numpy as jnp
from jax import lax
from jax.experimental import pallas as pl
from jax.experimental.pallas import tpu as pltpu
from jax.sharding import PartitionSpec as P

HEADS = 12
HEAD = 64
NORM_EPS = 1e-12
MASKED = -1e30
INV_ROOT_TWO = 0.7071067811865476
INV_ROOT_TAU = 0.3989422804014327
MESH = pl.DeviceIdType.MESH
BF = jnp.bfloat16
F32 = jnp.float32
TILE = 256
ROWS = 128
VMEM_BYTES = 60 * 1024 * 1024


def dot_nn(a, b):
    return lax.dot_general(a, b, (((1,), (0,)), ((), ())), preferred_element_type=F32)


def dot_nt(a, b):
    return lax.dot_general(a, b, (((1,), (1,)), ((), ())), preferred_element_type=F32)


def dot_tn(a, b):
    return lax.dot_general(a, b, (((0,), (0,)), ((), ())), preferred_element_type=F32)


def loop(count, body, unroll=1):
    def step(i, carry):
        body(i)
        return carry

    lax.fori_loop(0, count, step, 0, unroll=unroll)


def tile_of(i, size=TILE):
    return pl.ds(pl.multiple_of(i * size, size), size)


class Weights:
    def __init__(self, block, pairs, targets, sems):
        self.waits = []
        own = lax.axis_index("section") == block
        for n, ((mine, theirs), target) in enumerate(zip(pairs, targets)):
            sem = sems.at[n]

            @pl.when(own)
            def _():
                pltpu.make_async_copy(mine, target, sem).start()

            @pl.when(jnp.logical_not(own))
            def _():
                pltpu.make_async_copy(theirs, target, sem).start()

            self.waits.append(pltpu.make_async_copy(mine, target, sem))

    def wait(self, n):
        self.waits[n].wait()


def normed_rows(residue):
    centered = residue - jnp.mean(residue, axis=-1, keepdims=True)
    inv = lax.rsqrt(jnp.mean(centered * centered, axis=-1, keepdims=True) + NORM_EPS)
    return centered * inv, inv


def lane_masks(shape):
    lane = lax.broadcasted_iota(jnp.int32, shape, 1)
    return (lane < HEAD, lane >= HEAD)


def forward_kernel(
    block,
    x_ref, segr_ref, segc_ref, first_ref, qkvb_ref, small_ref, upb_ref,
    wqkv_m, wqkv_t, wout_m, wout_t, wup_m, wup_t, wdown_m, wdown_t,
    qkv_ref, o_ref, lse_ref, n1_ref, inv1_ref, hlow_ref, g_ref, slope_ref, n2_ref, inv2_ref, y_ref, x1_ref,
    wqkv, wout, wup, wdown, mask_ref, res_ref, h_ref, sems,
):
    rows, width = x_ref.shape
    hidden_width = wup.shape[1]
    weights = Weights(
        block,
        ((wqkv_m, wqkv_t), (wout_m, wout_t), (wup_m, wup_t), (wdown_m, wdown_t)),
        (wqkv, wout, wup, wdown),
        sems,
    )
    mask_ref[...] = jnp.where(segc_ref[...] == segr_ref[...], 0.0, MASKED)
    weights.wait(0)
    x = x_ref[...]

    def project(j):
        cols = tile_of(j)
        scale = jnp.where(j < width // TILE, HEAD ** -0.5, 1.0)
        qkv_ref[:, cols] = ((dot_nn(x_ref[...], wqkv[:, cols]) + qkvb_ref[:, cols]) * scale).astype(BF)

    loop(3 * width // TILE, project, 3)

    def attend(pair):
        queries = qkv_ref[:, tile_of(pair, 128)]
        keys = qkv_ref[:, pl.ds(pl.multiple_of(width + pair * 128, 128), 128)]
        values = qkv_ref[:, pl.ds(pl.multiple_of(2 * width + pair * 128, 128), 128)]
        masks = lane_masks((rows, 128))
        parts = []
        for h in range(2):
            scores = dot_nt(keys, jnp.where(masks[h], queries, jnp.zeros_like(queries))) + mask_ref[...]
            top = jnp.max(scores, axis=0, keepdims=True)
            weight = jnp.exp(scores - top)
            total = jnp.sum(weight, axis=0, keepdims=True)
            lse_ref[pair, pl.ds(h, 1), :] = top + jnp.log(total)
            result = dot_tn(values, weight.astype(BF))
            parts.append(result[h * HEAD : (h + 1) * HEAD] * (1.0 / total))
        o_ref[:, tile_of(pair, 128)] = jnp.concatenate(parts, axis=0).T.astype(BF)

    loop(HEADS // 2, attend, 2)
    weights.wait(1)

    def mix(j):
        cols = tile_of(j)
        res_ref[:, cols] = x_ref[:, cols].astype(F32) + (dot_nn(o_ref[...], wout[:, cols]) + small_ref[2:3, cols])

    loop(width // TILE, mix, 3)

    def norm_one(i):
        r = tile_of(i, ROWS)
        normed, inv = normed_rows(res_ref[r, :])
        n1_ref[r, :] = normed
        inv1_ref[r, :] = jnp.broadcast_to(inv, (ROWS, 128))
        h = normed * small_ref[6:7, :] + small_ref[3:4, :]
        h_ref[r, :] = h
        hlow_ref[r, :] = h.astype(BF)

    loop(rows // ROWS, norm_one, 2)
    weights.wait(2)

    def widen(j):
        cols = tile_of(j)
        z = dot_nn(hlow_ref[...], wup[:, cols]) + upb_ref[:, cols]
        half = 0.5 * (1.0 + lax.erf(z * INV_ROOT_TWO))
        g_ref[:, cols] = (z * half).astype(BF)
        slope_ref[:, cols] = (half + z * jnp.exp(-0.5 * z * z) * INV_ROOT_TAU).astype(BF)

    loop(hidden_width // TILE, widen, 3)
    weights.wait(3)

    def narrow(j):
        cols = tile_of(j)
        res_ref[:, cols] = h_ref[:, cols] + (dot_nn(g_ref[...], wdown[:, cols]) + small_ref[4:5, cols])

    loop(width // TILE, narrow, 3)

    def norm_two(i):
        r = tile_of(i, ROWS)
        normed, inv = normed_rows(res_ref[r, :])
        n2_ref[r, :] = normed
        inv2_ref[r, :] = jnp.broadcast_to(inv, (ROWS, 128))
        y = (normed * small_ref[7:8, :] + small_ref[5:6, :]).astype(BF)
        y_ref[r, :] = y
        x1_ref[r, :] = jnp.where(first_ref[r, :] > 0.5, y.astype(F32), x_ref[r, :].astype(F32)).astype(BF)

    loop(rows // ROWS, norm_two, 2)


def norm_back(gradient, normed, inv):
    return inv * (
        gradient
        - jnp.mean(gradient, axis=-1, keepdims=True)
        - normed * jnp.mean(gradient * normed, axis=-1, keepdims=True)
    )


def column_sum(v):
    return jnp.sum(v, axis=0, keepdims=True)


def backward_kernel(
    block,
    cot_ref, dnext_ref, segr_ref, segc_ref, first_ref, small_ref,
    qkv_ref, o_ref, lse_ref, n1_ref, inv1_ref, slope_ref, n2_ref, inv2_ref,
    wqkv_m, wqkv_t, wout_m, wout_t, wup_m, wup_t, wdown_m, wdown_t,
    dx_ref, dproj_ref, da_ref, dz_ref, df_ref, dsmall_ref, dup_ref,
    wqkv, wout, wup, wdown, mask_ref, dr_ref, dh_ref, do_ref, sems,
):
    rows, width = cot_ref.shape
    hidden_width = wup.shape[1]
    weights = Weights(
        block,
        ((wdown_m, wdown_t), (wup_m, wup_t), (wout_m, wout_t), (wqkv_m, wqkv_t)),
        (wdown, wup, wout, wqkv),
        sems,
    )
    mask_ref[...] = jnp.where(segc_ref[...] == segr_ref[...], 0.0, MASKED)
    dsmall_ref[...] = jnp.zeros_like(dsmall_ref)

    def norm_two(i):
        r = tile_of(i, ROWS)
        gradient = cot_ref[r, :].astype(F32)
        if block == 0:
            back = dnext_ref[r, :].astype(BF).astype(F32)
            gradient = gradient + jnp.where(first_ref[r, :] > 0.5, back, 0.0)
        normed = n2_ref[r, :]
        dr = norm_back(gradient * small_ref[7:8, :], normed, inv2_ref[r, 0:1])
        dr_ref[r, :] = dr
        df_ref[r, :] = dr.astype(BF)
        dsmall_ref[7:8, :] += column_sum(gradient * normed)
        dsmall_ref[5:6, :] += column_sum(gradient)
        dsmall_ref[4:5, :] += column_sum(dr)

    loop(rows // ROWS, norm_two, 2)
    weights.wait(0)

    def narrow(j):
        cols = tile_of(j)
        dz = dot_nt(df_ref[...], wdown[cols, :]) * slope_ref[:, cols].astype(F32)
        dup_ref[:, cols] = column_sum(dz)
        dz_ref[:, cols] = dz.astype(BF)

    loop(hidden_width // TILE, narrow)
    weights.wait(1)

    def widen(j):
        cols = tile_of(j)
        dh_ref[:, cols] = dr_ref[:, cols] + dot_nt(dz_ref[...], wup[cols, :])

    loop(width // TILE, widen, 3)

    def norm_one(i):
        r = tile_of(i, ROWS)
        gradient = dh_ref[r, :]
        normed = n1_ref[r, :]
        dr = norm_back(gradient * small_ref[6:7, :], normed, inv1_ref[r, 0:1])
        dr_ref[r, :] = dr
        da_ref[r, :] = dr.astype(BF)
        dsmall_ref[6:7, :] += column_sum(gradient * normed)
        dsmall_ref[3:4, :] += column_sum(gradient)
        dsmall_ref[2:3, :] += column_sum(dr)

    loop(rows // ROWS, norm_one, 2)
    weights.wait(2)

    def mix(j):
        cols = tile_of(j)
        do_ref[:, cols] = dot_nt(da_ref[...], wout[cols, :]).astype(BF)

    loop(width // TILE, mix, 3)

    def attend(pair):
        here = tile_of(pair, 128)
        key_cols = pl.ds(pl.multiple_of(width + pair * 128, 128), 128)
        value_cols = pl.ds(pl.multiple_of(2 * width + pair * 128, 128), 128)
        queries, keys, values = qkv_ref[:, here], qkv_ref[:, key_cols], qkv_ref[:, value_cols]
        grad = do_ref[:, here]
        masks = lane_masks((rows, 128))
        dq, dk, dv = [], 0.0, 0.0
        for h in range(2):
            head_queries = jnp.where(masks[h], queries, jnp.zeros_like(queries))
            head_grad = jnp.where(masks[h], grad, jnp.zeros_like(grad))
            scores = dot_nt(keys, head_queries) + mask_ref[...]
            weight = jnp.exp(scores - lse_ref[pair, pl.ds(h, 1), :])
            dweight = dot_nt(values, head_grad)
            delta = jnp.sum(weight * dweight, axis=0, keepdims=True)
            dscore = (weight * (dweight - delta)).astype(BF)
            dq.append(dot_tn(keys, dscore)[h * HEAD : (h + 1) * HEAD])
            dk = dk + dot_nn(dscore, head_queries)
            dv = dv + dot_nn(weight.astype(BF), head_grad)
        dq = jnp.concatenate(dq, axis=0).T * (HEAD ** -0.5)
        dsmall_ref[0:1, here] = column_sum(dq)
        dsmall_ref[1:2, here] = column_sum(dv)
        dproj_ref[:, here] = dq.astype(BF)
        dproj_ref[:, key_cols] = dk.astype(BF)
        dproj_ref[:, value_cols] = dv.astype(BF)

    loop(HEADS // 2, attend)
    weights.wait(3)

    def project(j):
        cols = tile_of(j)
        dx = dr_ref[:, cols] + dot_nt(dproj_ref[...], wqkv[cols, :])
        if block == 0:
            dx = dx + jnp.where(first_ref[...] > 0.5, 0.0, dnext_ref[:, cols])
        dx_ref[:, cols] = dx

    loop(width // TILE, project, 3)


def in_vmem(count):
    return [pl.BlockSpec(memory_space=pltpu.VMEM)] * count


def in_hbm(count):
    return [pl.BlockSpec(memory_space=pl.ANY)] * count


def shaped(shape, dtype=F32):
    return jax.ShapeDtypeStruct(shape, dtype)


def block_forward(block, x, segr, segc, first, qkvb, small, upb, weights):
    rows, width = x.shape
    hidden_width = upb.shape[1]
    scratch = [pltpu.VMEM(w.shape, BF) for w in weights[::2]]
    return pl.pallas_call(
        functools.partial(forward_kernel, block),
        out_shape=(
            shaped((rows, 3 * width), BF), shaped((rows, width), BF), shaped((HEADS // 2, 2, rows)),
            shaped((rows, width)), shaped((rows, 128)), shaped((rows, width), BF),
            shaped((rows, hidden_width), BF), shaped((rows, hidden_width), BF),
            shaped((rows, width)), shaped((rows, 128)), shaped((rows, width), BF), shaped((rows, width), BF),
        ),
        in_specs=in_vmem(7) + in_hbm(8),
        out_specs=tuple(in_vmem(12)),
        scratch_shapes=scratch + [
            pltpu.VMEM((rows, rows), F32), pltpu.VMEM((rows, width), F32), pltpu.VMEM((rows, width), F32),
            pltpu.SemaphoreType.DMA((4,)),
        ],
        compiler_params=pltpu.CompilerParams(vmem_limit_bytes=VMEM_BYTES),
        name="forward" + str(block),
    )(x, segr, segc, first, qkvb, small, upb, *weights)


def block_backward(block, cot, dnext, segr, segc, first, small, kept, weights):
    rows, width = cot.shape
    hidden_width = weights[4].shape[1]
    scratch = [pltpu.VMEM(w.shape, BF) for w in weights[::2]]
    return pl.pallas_call(
        functools.partial(backward_kernel, block),
        out_shape=(
            shaped((rows, width)), shaped((rows, 3 * width), BF), shaped((rows, width), BF),
            shaped((rows, hidden_width), BF), shaped((rows, width), BF), shaped((16, width)), shaped((1, hidden_width)),
        ),
        in_specs=in_vmem(14) + in_hbm(8),
        out_specs=tuple(in_vmem(7)),
        scratch_shapes=scratch + [
            pltpu.VMEM((rows, rows), F32), pltpu.VMEM((rows, width), F32), pltpu.VMEM((rows, width), F32),
            pltpu.VMEM((rows, width), BF), pltpu.SemaphoreType.DMA((4,)),
        ],
        compiler_params=pltpu.CompilerParams(vmem_limit_bytes=VMEM_BYTES),
        name="backward" + str(block),
    )(cot, dnext, segr, segc, first, small, *kept, *weights)


ORDERS = {
    "A": (0, 1, 2, 3), "B": (1, 0, 2, 3), "C": (2, 3, 0, 1), "D": (2, 3, 1, 0), "E": (0, 2, 3, 1), "F": (1, 2, 3, 0),
}
BITS = 4
PARTS = 1 << BITS
SLOTS = 4
SEQUENCE = (8, 9, 10, 11, 4, 5, 6, 7, 3, 0, 1, 2)
KINDS = ("AFEBABABEFAB", "EFAFEFEFEFAF")
SCHEDULE = (
    1428, 1424, 1892, 1888, 2005, 2001, 2108, 2104, 2081, 2184, 2181, 2194, 2572, 2582, 2681, 2775,
    2771, 2844, 2850, 2973, 3046, 3043, 3145, 3312, 3450, 3431, 3533, 3700, 3838, 3896, 4093, 4160,
    4181, 4202, 4302, 4319, 4315, 4548, 4566, 4574, 4587, 4657, 4720, 4840, 4857, 4833, 4916, 4913,
    4946, 4975, 4951, 5016, 5029, 5050, 5026, 5420, 5417, 5589, 5586, 5606, 5699, 5802, 5785, 5779,
    5772, 5803, 5786, 5819, 5811, 5787, 5773, 5764, 5774, 5765, 5775, 5766, 5767, 5823, 5805, 5782,
    5788, 5799, 5783, 5760, 5806, 5789, 5768, 5761, 5807, 5790, 5769, 5762, 5791, 5763, 5770, 5771,
)


def owner(b, chunk):
    return (b + SEQUENCE.index(chunk)) % 2


def backward_sum_kernel(*refs):
    acts = (refs[0:12], refs[12:24])
    weight_pairs = ((refs[24], refs[25]), (refs[26], refs[27]), (refs[28], refs[29]), (refs[30], refs[31]))
    segr_ref, segc_ref, first_ref, small0_ref, small1_ref = refs[32:37]
    out_qkv, out_out, out_up, out_down, out_small, dx_ref = refs[37:43]
    (total, slots, stage, r1, r2, r3, r4, wring, gring, sring, lhs, turned, norm_buf, inv_buf, cot_buf, qkv_buf, lse_buf,
     low_buf, dz_buf, acc, mask_ref, dsmall, small_sum, small_in,
     cross_send, cross_recv, done_send, done_recv, send, recv, small_send, small_recv, wsem, gsem, ssem, asem) = refs[43:]
    received = (r1, r2, r3, r4)
    rows, width = acc.shape
    share = total.shape[-2]
    wide = gring.shape[0]
    count = out_up.shape[1] // width
    sec, me = lax.axis_index("section"), lax.axis_index("dp")
    bits = [(me >> k) & 1 for k in range(BITS)]
    smalls = (small0_ref, small1_ref)

    barrier = pltpu.get_barrier_semaphore()
    for k in range(BITS):
        pl.semaphore_signal(barrier, inc=1, device_id={"dp": me ^ (1 << k)}, device_id_type=MESH)
    pl.semaphore_signal(barrier, inc=1, device_id={"section": 1 - sec}, device_id_type=MESH)

    weight_list = []
    for b in (1, 0):
        for j in range(count):
            weight_list += [(b, 3, j), (b, 2, j)]
        weight_list += [(b, 1, 0), (b, 0, 0), (b, 0, 1), (b, 0, 2)]

    def weight_copy(n, side):
        b, which, j = weight_list[n]
        ref = weight_pairs[which][side]
        source = ref.at[pl.ds(j * width, width), :] if which == 3 else ref.at[:, pl.ds(j * width, width)]
        return pltpu.make_async_copy(source, wring.at[n % wring.shape[0]], wsem.at[n % wring.shape[0]])

    def weight_start(n):
        if n < len(weight_list):
            own = sec == weight_list[n][0]

            @pl.when(own)
            def _():
                weight_copy(n, 0).start()

            @pl.when(jnp.logical_not(own))
            def _():
                weight_copy(n, 1).start()

    taken = [0]

    def weight_next():
        n = taken[0]
        taken[0] += 1
        weight_copy(n, 0).wait()
        return wring.at[n % wring.shape[0]]

    def weight_done():
        weight_start(taken[0] - 1 + wring.shape[0])

    COT, QKV, O, LSE, N1, INV1, HLOW, G, SLOPE, N2, INV2, X = range(12)
    targets = {
        COT: (cot_buf, 0), QKV: (qkv_buf, 1), O: (lhs, 2), LSE: (lse_buf, 3), N1: (norm_buf, 4), INV1: (inv_buf, 5),
        HLOW: (lhs, 2), N2: (norm_buf, 4), INV2: (inv_buf, 5), X: (lhs, 2),
    }

    def act(b, which):
        target, sem = targets[which]
        return pltpu.make_async_copy(acts[b][which], target, asem.at[sem])

    def ring(b, which, j):
        buf, sem = (gring, gsem) if which == G else (sring, ssem)
        source = acts[b][which].at[:, pl.ds(j * width, width)]
        return pltpu.make_async_copy(source, buf.at[j % wide], sem.at[j % wide])

    def place(part):
        return tuple((part >> (BITS - 1 - k)) & 1 for k in range(BITS))

    def across(chunk, slot):
        return pltpu.make_async_remote_copy(
            src_ref=slots.at[slot], dst_ref=total.at[chunk],
            send_sem=cross_send.at[chunk], recv_sem=cross_recv.at[chunk],
            device_id={"section": 1 - sec}, device_id_type=MESH,
        )

    def hand_over(b, chunk, slot):
        @pl.when(sec != owner(b, chunk))
        def _():
            across(chunk, slot).start()

    def exchange(b, chunk, phase):
        order = ORDERS[KINDS[b][SEQUENCE.index(chunk)]]
        at = [slice(None)] * BITS
        for done in range(phase):
            at[BITS - 1 - order[done]] = bits[order[done]]
        at[BITS - 1 - order[phase]] = 1 - bits[order[phase]]
        return pltpu.make_async_remote_copy(
            src_ref=total.at[(chunk,) + tuple(at)], dst_ref=received[phase].at[chunk],
            send_sem=send.at[chunk, phase], recv_sem=recv.at[chunk, phase],
            device_id={"dp": me ^ (1 << order[phase])}, device_id_type=MESH,
        )

    def finish(b, chunk, slot):
        @pl.when(sec == owner(b, chunk))
        def _():
            across(chunk, slot).wait_recv()

            def one(i):
                at = (i // 8, (i // 4) % 2, (i // 2) % 2, i % 2)
                total[(chunk,) + at] = total[(chunk,) + at] + slots[(slot,) + at]

            loop(PARTS, one, 4)
            exchange(b, chunk, 0).start()

        @pl.when(sec != owner(b, chunk))
        def _():
            across(chunk, slot).wait_send()

    def result_of(chunk):
        if chunk < 3:
            return out_qkv.at[:, pl.ds(chunk * width, width)]
        if chunk < 4:
            return out_out
        if chunk < 8:
            return out_up.at[:, pl.ds((chunk - 4) * width, width)]
        return out_down.at[pl.ds((chunk - 8) * share, share), :]

    def bring(chunk):
        return pltpu.make_async_remote_copy(
            src_ref=stage.at[SEQUENCE.index(chunk) // 2], dst_ref=result_of(chunk),
            send_sem=done_send.at[chunk], recv_sem=done_recv.at[chunk],
            device_id={"section": 1 - sec}, device_id_type=MESH,
        )

    def take(b, chunk, phase):
        order = ORDERS[KINDS[b][SEQUENCE.index(chunk)]]
        exchange(b, chunk, phase).wait()

        def one(i):
            at, inner, left = [None] * BITS, [], i
            for done in range(phase + 1):
                at[BITS - 1 - order[done]] = bits[order[done]]
            for d in reversed([d for d in range(BITS) if at[d] is None]):
                at[d] = left % 2
                inner.insert(0, at[d])
                left = left // 2
            at = (chunk,) + tuple(at)
            total[at] = total[at] + received[phase][(chunk,) + tuple(inner)]

        if phase < BITS - 1:
            loop(PARTS >> (phase + 1), one, min(4, PARTS >> (phase + 1)))
            exchange(b, chunk, phase + 1).start()
        else:
            value = total[(chunk,) + tuple(bits[BITS - 1 - d] for d in range(BITS))].astype(F32)
            value = value + received[phase][chunk].astype(F32)
            if owner(b, chunk) == b:
                result_of(chunk)[...] = value
            else:
                stage[SEQUENCE.index(chunk) // 2] = value
                bring(chunk).start()

    steps = [(n // 96, (n // 48) % 2, (n // 4) % 12, n % 4) for n in SCHEDULE]
    points = [0]

    def run_steps(chosen):
        for core in range(2):
            mine = [step for step in chosen if owner(step[1], step[2]) == core]
            if mine:

                @pl.when(sec == core)
                def _():
                    for _, b, chunk, phase in mine:
                        take(b, chunk, phase)

    def point():
        run_steps([step for step in steps if step[0] == points[0]])
        points[0] += 1

    def product(right, right_col, put):
        def one(n):
            cols = tile_of(n)
            rhs_cols = pl.ds(pl.multiple_of(right_col + n * TILE, TILE), TILE)
            result = dot_nn(turned[...], right[:, rhs_cols]).astype(BF)
            for piece in range(PARTS):
                slot, part = put(piece)
                slots[(slot,) + place(part) + (slice(None), cols)] = result[piece * share : (piece + 1) * share]

        loop(width // TILE, one, 3)

    def first_loads(b):
        act(b, COT).start()
        act(b, N2).start()
        act(b, INV2).start()
        for j in range(wide):
            ring(b, G, j).start()
            ring(b, SLOPE, j).start()

    first_loads(1)
    act(1, HLOW).start()
    for n in range(wring.shape[0]):
        weight_start(n)
    mask_ref[...] = jnp.where(segc_ref[...] == segr_ref[...], 0.0, MASKED)
    dsmall[...] = jnp.zeros_like(dsmall)

    for b in (1, 0):
        small = smalls[b]
        act(b, QKV).start()
        act(b, LSE).start()
        act(b, COT).wait()
        act(b, N2).wait()
        act(b, INV2).wait()

        def norm_two(i):
            r = tile_of(i, ROWS)
            gradient = cot_buf[r, :].astype(F32)
            if b == 0:
                back = dx_ref[r, :].astype(BF).astype(F32)
                gradient = gradient + jnp.where(first_ref[r, :] > 0.5, back, 0.0)
            normed = norm_buf[r, :]
            dr = norm_back(gradient * small[7:8, :], normed, inv_buf[r, 0:1])
            acc[r, :] = dr
            low_buf[r, :] = dr.astype(BF)
            dsmall[b, 7:8, :] += column_sum(gradient * normed)
            dsmall[b, 5:6, :] += column_sum(gradient)
            dsmall[b, 4:5, :] += column_sum(dr)

        loop(rows // ROWS, norm_two, 2)
        act(b, N1).start()
        act(b, INV1).start()
        if b == 1:
            pl.semaphore_wait(barrier, BITS + 1)
        point()
        for j in range(count):
            ring(b, G, j).wait()
            turned[...] = gring[j % wide].T
            if j + wide < count:
                ring(b, G, j + wide).start()
            product(low_buf, 0, lambda piece: (piece % count, j * (PARTS // count) + piece // count))
            point()
        for c in range(count):
            hand_over(b, 8 + c, c)
        act(b, HLOW).wait()
        turned[...] = lhs[...].T
        act(b, O).start()

        for j in range(count):
            down = weight_next()
            ring(b, SLOPE, j).wait()

            def narrow(t):
                cols = tile_of(t)
                dz = dot_nt(low_buf[...], down[cols, :]) * sring[j % wide, :, cols].astype(F32)
                dsmall[b, 8 + j : 9 + j, cols] = column_sum(dz)
                dz_buf[:, cols] = dz.astype(BF)

            loop(width // TILE, narrow, 3)
            weight_done()
            if j + wide < count:
                ring(b, SLOPE, j + wide).start()
            point()
            finish(b, 8 + j, j)
            product(dz_buf, 0, lambda piece: (j, piece))
            hand_over(b, 4 + j, j)
            point()
            up = weight_next()

            def widen(t):
                cols = tile_of(t)
                acc[:, cols] += dot_nt(dz_buf[...], up[cols, :])

            loop(width // TILE, widen, 3)
            weight_done()
            point()
            if j > 0:
                finish(b, 3 + j, j - 1)
        act(b, N1).wait()
        act(b, INV1).wait()

        def norm_one(i):
            r = tile_of(i, ROWS)
            gradient = acc[r, :]
            normed = norm_buf[r, :]
            dr = norm_back(gradient * small[6:7, :], normed, inv_buf[r, 0:1])
            acc[r, :] = dr
            low_buf[r, :] = dr.astype(BF)
            dsmall[b, 6:7, :] += column_sum(gradient * normed)
            dsmall[b, 3:4, :] += column_sum(gradient)
            dsmall[b, 2:3, :] += column_sum(dr)

        loop(rows // ROWS, norm_one, 2)
        finish(b, 7, 3)
        point()
        act(b, O).wait()
        turned[...] = lhs[...].T
        act(b, X).start()
        product(low_buf, 0, lambda piece: (0, piece))
        hand_over(b, 3, 0)
        point()
        mixer = weight_next()

        def mix(t):
            cols = tile_of(t)
            cot_buf[:, cols] = dot_nt(low_buf[...], mixer[cols, :]).astype(BF)

        loop(width // TILE, mix, 3)
        weight_done()
        act(b, QKV).wait()
        act(b, LSE).wait()
        point()

        def attend(pair):
            here = tile_of(pair, 128)
            key_cols = pl.ds(pl.multiple_of(width + pair * 128, 128), 128)
            value_cols = pl.ds(pl.multiple_of(2 * width + pair * 128, 128), 128)
            queries, keys, values = qkv_buf[:, here], qkv_buf[:, key_cols], qkv_buf[:, value_cols]
            grad = cot_buf[:, here]
            masks = lane_masks((rows, 128))
            dq, dk, dv = [], 0.0, 0.0
            for h in range(2):
                head_queries = jnp.where(masks[h], queries, jnp.zeros_like(queries))
                head_grad = jnp.where(masks[h], grad, jnp.zeros_like(grad))
                scores = dot_nt(keys, head_queries) + mask_ref[...]
                weight = jnp.exp(scores - lse_buf[pair, pl.ds(h, 1), :])
                dweight = dot_nt(values, head_grad)
                delta = jnp.sum(weight * dweight, axis=0, keepdims=True)
                dscore = (weight * (dweight - delta)).astype(BF)
                dq.append(dot_tn(keys, dscore)[h * HEAD : (h + 1) * HEAD])
                dk = dk + dot_nn(dscore, head_queries)
                dv = dv + dot_nn(weight.astype(BF), head_grad)
            dq = jnp.concatenate(dq, axis=0).T * (HEAD ** -0.5)
            dsmall[b, 0:1, here] = column_sum(dq)
            dsmall[b, 1:2, here] = column_sum(dv)
            qkv_buf[:, here] = dq.astype(BF)
            qkv_buf[:, key_cols] = dk.astype(BF)
            qkv_buf[:, value_cols] = dv.astype(BF)

        for third in range(3):
            loop(HEADS // 6, lambda i: attend(third * (HEADS // 6) + i), 2)
            if third == 0:
                finish(b, 3, 0)
            point()
        act(b, X).wait()
        turned[...] = lhs[...].T
        if b == 1:
            act(0, HLOW).start()
            first_loads(0)
        point()

        for j in range(3):
            product(qkv_buf, j * width, lambda piece: (1 + j, piece))
            hand_over(b, j, 1 + j)
            point()
            block_weight = weight_next()

            def project(t):
                cols = tile_of(t)
                dx = acc[:, cols] + dot_nt(qkv_buf[:, j * width : (j + 1) * width], block_weight[cols, :])
                if j < 2:
                    acc[:, cols] = dx
                elif b == 1:
                    dx_ref[:, cols] = dx
                else:
                    dx_ref[:, cols] = dx + jnp.where(first_ref[...] > 0.5, 0.0, dx_ref[:, cols])

            loop(width // TILE, project, 3)
            weight_done()
            point()
            if j > 0:
                finish(b, j - 1, j)
        finish(b, 2, 3)

    def small_exchange(phase):
        target = {"section": 1 - sec} if phase == 0 else {"dp": me ^ (1 << (phase - 1))}
        source = dsmall.at[1 - sec] if phase == 0 else small_sum.at[phase]
        return pltpu.make_async_remote_copy(
            src_ref=source, dst_ref=small_in.at[phase], send_sem=small_send.at[phase], recv_sem=small_recv.at[phase],
            device_id=target, device_id_type=MESH,
        )

    def small_take(phase):
        small_exchange(phase).wait()
        before = dsmall[sec] if phase == 0 else small_sum[phase]
        if phase < BITS:
            small_sum[phase + 1] = before + small_in[phase]
            small_exchange(phase + 1).start()
        else:
            out_small[...] = before + small_in[phase]

    small_exchange(0).start()
    left = [[step for step in steps if step[0] >= points[0] and owner(step[1], step[2]) == core] for core in range(2)]
    for phase in range(BITS + 1):
        run_steps(left[0][:3] + left[1][:3])
        left = [left[0][3:], left[1][3:]]
        small_take(phase)
    run_steps(left[0] + left[1])
    for chunk in SEQUENCE[1::2]:
        bring(chunk).wait()


def backward_sum(cots, kept, inputs, segr, segc, first, smalls, weights):
    rows, width = cots[0].shape
    hidden_width = weights[4].shape[1]
    share = width // PARTS
    chunks = 2 * hidden_width // width + 4
    acts = []
    for b in range(2):
        acts += [cots[b], *kept[b], inputs[b]]
    return pl.pallas_call(
        backward_sum_kernel,
        out_shape=(
            shaped((share, 3 * width)), shaped((share, width)), shaped((share, hidden_width)),
            shaped((hidden_width // PARTS, width)), shaped((16, width)), shaped((rows, width)),
        ),
        in_specs=in_hbm(24) + in_hbm(8) + in_vmem(5),
        out_specs=tuple(in_vmem(6)),
        scratch_shapes=[
            pltpu.VMEM((chunks, 2, 2, 2, 2, share, width), BF),
            pltpu.VMEM((SLOTS, 2, 2, 2, 2, share, width), BF),
            pltpu.VMEM((chunks // 2, share, width), F32),
            pltpu.VMEM((chunks, 2, 2, 2, share, width), BF),
            pltpu.VMEM((chunks, 2, 2, share, width), BF),
            pltpu.VMEM((chunks, 2, share, width), BF),
            pltpu.VMEM((chunks, share, width), BF),
            pltpu.VMEM((3, width, width), BF),
            pltpu.VMEM((2, rows, width), BF),
            pltpu.VMEM((2, rows, width), BF),
            pltpu.VMEM((rows, width), BF),
            pltpu.VMEM((width, rows), BF),
            pltpu.VMEM((rows, width), F32),
            pltpu.VMEM((rows, 128), F32),
            pltpu.VMEM((rows, width), BF),
            pltpu.VMEM((rows, 3 * width), BF),
            pltpu.VMEM((HEADS // 2, 2, rows), F32),
            pltpu.VMEM((rows, width), BF),
            pltpu.VMEM((rows, width), BF),
            pltpu.VMEM((rows, width), F32),
            pltpu.VMEM((rows, rows), F32),
            pltpu.VMEM((2, 16, width), F32),
            pltpu.VMEM((BITS + 1, 16, width), F32),
            pltpu.VMEM((BITS + 1, 16, width), F32),
            pltpu.SemaphoreType.DMA((chunks,)),
            pltpu.SemaphoreType.DMA((chunks,)),
            pltpu.SemaphoreType.DMA((chunks,)),
            pltpu.SemaphoreType.DMA((chunks,)),
            pltpu.SemaphoreType.DMA((chunks, BITS)),
            pltpu.SemaphoreType.DMA((chunks, BITS)),
            pltpu.SemaphoreType.DMA((BITS + 1,)),
            pltpu.SemaphoreType.DMA((BITS + 1,)),
            pltpu.SemaphoreType.DMA((3,)),
            pltpu.SemaphoreType.DMA((2,)),
            pltpu.SemaphoreType.DMA((2,)),
            pltpu.SemaphoreType.DMA((6,)),
        ],
        compiler_params=pltpu.CompilerParams(
            collective_id=0, has_side_effects=True, vmem_limit_bytes=VMEM_BYTES
        ),
        name="backward_sum",
    )(*acts, *weights, segr, segc, first, *smalls)


def sum_plainly(pieces, small):
    def scattered(names):
        both = jnp.stack([dot_tn(pieces[b][names[0]], pieces[b][names[1]]) for b in range(2)])
        own = lax.psum_scatter(both, "section", scatter_dimension=0, tiled=False)
        return lax.psum_scatter(own, "dp", scatter_dimension=0, tiled=True)

    own_small = lax.psum(lax.psum_scatter(small, "section", scatter_dimension=0, tiled=False), "dp")
    return tuple(scattered(names) for names in ((0, 1), (2, 3), (4, 5), (6, 7))) + (own_small,)


def backward_plainly(cots, kept, inputs, segr, segc, first, smalls, weights):
    width = inputs[0].shape[1]
    pieces, dsmalls, dnext = [None, None], [None, None], inputs[0]
    for block in (1, 0):
        qkv, o, lse, n1, inv1, hlow, g, slope, n2, inv2 = kept[block]
        dnext, dproj, da, dz, df, dsmall, dup = block_backward(
            block, cots[block], dnext, segr, segc, first, smalls[block],
            (qkv, o, lse, n1, inv1, slope, n2, inv2), weights,
        )
        pieces[block] = (inputs[block], dproj, o, da, hlow, dz, g, df)
        dsmalls[block] = jnp.concatenate([dsmall[:8], dup.reshape(-1, width), jnp.zeros((4, width), F32)], axis=0)
    return sum_plainly(pieces, jnp.stack(dsmalls)), dnext


def swap(value):
    return lax.ppermute(value, "section", [(0, 1), (1, 0)])


def local(hidden, segment_ids, cotangent, w_qkv, w_out, w_up, w_down, biases, gains, up_bias):
    sec, me = lax.axis_index("section"), lax.axis_index("dp")
    count = lax.axis_size("dp")
    length, width = segment_ids.shape[1], hidden.shape[1]
    rows = hidden.shape[0] // 2
    assert rows == length

    def rows_of(matrix, half):
        return lax.dynamic_slice_in_dim(matrix, half * rows, rows, 0)

    def by_block(mine, theirs):
        return jnp.where(sec == 0, mine, theirs), jnp.where(sec == 0, theirs, mine)

    mine = (w_qkv[0], w_out[0], w_up[0], w_down[0])
    weights = []
    for own in mine:
        weights += [own, swap(own)]
    packed = jnp.concatenate([biases[0], gains[0], up_bias[0].reshape(-1, width)], axis=0)
    smalls = by_block(packed, swap(packed))
    cots = by_block(rows_of(cotangent[0], sec), swap(rows_of(cotangent[0], 1 - sec)))
    x = rows_of(hidden, sec)
    segments = lax.dynamic_index_in_dim(segment_ids, sec, 0, False)
    segr, segc = segments.reshape(1, rows), segments.reshape(rows, 1)
    first = jnp.concatenate([jnp.ones((1,), F32), (segments[1:] != segments[:-1]).astype(F32)]).reshape(rows, 1)

    inputs, kept, states = [x], [], []
    for block in range(2):
        small = smalls[block]
        qkvb = jnp.concatenate([small[0:1], jnp.zeros((1, width), F32), small[1:2]], axis=1)
        result = block_forward(block, inputs[block], segr, segc, first, qkvb, small, small[8:].reshape(1, -1), weights)
        kept.append(result[:10])
        states.append(result[10])
        inputs.append(result[11])

    if count == PARTS and width % (16 * PARTS) == 0:
        *sums, dnext = backward_sum(cots, kept, inputs, segr, segc, first, smalls, weights)
    else:
        sums, dnext = backward_plainly(cots, kept, inputs, segr, segc, first, smalls, weights)
    gqkv, gout, gup, gdown, gsmall = sums
    share, up_share = width // count, up_bias.shape[1] // count
    columns = lax.dynamic_slice_in_dim(gsmall[:8], me * share, share, 1)
    gup_bias = lax.dynamic_slice_in_dim(gsmall[8:12].reshape(-1), me * up_share, up_share, 0)

    own_states = jnp.where(sec == 0, states[0], states[1])
    other_states = swap(jnp.where(sec == 0, states[1], states[0]))
    both_states = jnp.concatenate(by_block(own_states, other_states), axis=0)
    grad_input = jnp.concatenate(by_block(dnext, swap(dnext)), axis=0)
    totals = (gqkv, gout, gup, gdown, columns[:6], columns[6:], gup_bias)
    return (both_states[None], grad_input) + tuple(member[None] for member in totals)


def solution(mesh):
    placed = (
        P("dp", None),
        P("dp", None),
        P("section", "dp", None),
        P("section", None, None),
        P("section", None, None),
        P("section", None, None),
        P("section", None, None),
        P("section", None, None),
        P("section", None, None),
        P("section", None),
    )
    return jax.shard_map(
        local,
        mesh=mesh,
        in_specs=placed,
        out_specs=(
            P("section", "dp", None),
            P("dp", None),
            P("section", "dp", None),
            P("section", "dp", None),
            P("section", "dp", None),
            P("section", "dp", None),
            P("section", None, "dp"),
            P("section", None, "dp"),
            P("section", "dp"),
        ),
        check_vma=False,
    )
```

```python
import functools

import jax
import jax.numpy as jnp
from jax import lax
from jax.experimental import pallas as pl
from jax.experimental.pallas import tpu as pltpu
from jax.sharding import PartitionSpec as P

HEADS = 12
HEAD = 64
NORM_EPS = 1e-12
MASKED = -1e30
INV_ROOT_TWO = 0.7071067811865476
INV_ROOT_TAU = 0.3989422804014327
MESH = pl.DeviceIdType.MESH
BF = jnp.bfloat16
F32 = jnp.float32
TILE = 256
ROWS = 128
VMEM_BYTES = 60 * 1024 * 1024


def dot_nn(a, b):
    return lax.dot_general(a, b, (((1,), (0,)), ((), ())), preferred_element_type=F32)


def dot_nt(a, b):
    return lax.dot_general(a, b, (((1,), (1,)), ((), ())), preferred_element_type=F32)


def dot_tn(a, b):
    return lax.dot_general(a, b, (((0,), (0,)), ((), ())), preferred_element_type=F32)


def loop(count, body, unroll=1):
    def step(i, carry):
        body(i)
        return carry

    lax.fori_loop(0, count, step, 0, unroll=unroll)


def tile_of(i, size=TILE):
    return pl.ds(pl.multiple_of(i * size, size), size)


class Weights:
    def __init__(self, block, pairs, targets, sems):
        self.waits = []
        own = lax.axis_index("section") == block
        for n, ((mine, theirs), target) in enumerate(zip(pairs, targets)):
            sem = sems.at[n]

            @pl.when(own)
            def _():
                pltpu.make_async_copy(mine, target, sem).start()

            @pl.when(jnp.logical_not(own))
            def _():
                pltpu.make_async_copy(theirs, target, sem).start()

            self.waits.append(pltpu.make_async_copy(mine, target, sem))

    def wait(self, n):
        self.waits[n].wait()


def normed_rows(residue):
    centered = residue - jnp.mean(residue, axis=-1, keepdims=True)
    inv = lax.rsqrt(jnp.mean(centered * centered, axis=-1, keepdims=True) + NORM_EPS)
    return centered * inv, inv


def lane_masks(shape):
    lane = lax.broadcasted_iota(jnp.int32, shape, 1)
    return (lane < HEAD, lane >= HEAD)


def spread_marks(seg_ref, sec, mask_ref, first_ref):
    rows = mask_ref.shape[0]
    line = jnp.where(sec == 0, seg_ref[0:1, :], seg_ref[1:2, :]).astype(F32)
    column = jnp.broadcast_to(line, (128, rows)).T
    mask_ref[...] = jnp.where(column[:, 0:1] == line, 0.0, MASKED)
    lines = jnp.broadcast_to(line, (8, rows))
    before = pltpu.roll(lines, 1, 1)
    lane = lax.broadcasted_iota(jnp.int32, (8, rows), 1)
    marks = jnp.where((lines != before) | (lane == 0), 1.0, 0.0)
    first_ref[...] = jnp.broadcast_to(marks[0:1, :], (128, rows)).T


def weight_piece(refs, n, width):
    wqkv, wout, wup, wdown = refs
    if n < 3:
        return wqkv.at[0, :, pl.ds(n * width, width)]
    if n < 4:
        return wout.at[0]
    count = wdown.shape[1] // width
    if n < 4 + count:
        return wup.at[0, :, pl.ds((n - 4) * width, width)]
    return wdown.at[0, pl.ds((n - 4 - count) * width, width), :]


def forward_kernel(*refs):
    hidden, seg_ref, cotangent = refs[0:3]
    own_weights = refs[3:7]
    biases_ref, gains_ref, upb_ref = refs[7:10]
    (qkv_out, o_out, lse_out, n1_out, inv1_out, hlow_out, g_out, slope_out, n2_out, inv2_out,
     x1_out, states_out, theirs_out, cot_out, smalls) = refs[10:25]
    (wbuf, x_buf, qkv_buf, o_buf, lse_buf, n1_buf, inv1_buf, hlow_buf, g_buf, slope_buf, n2_buf, inv2_buf, y_buf,
     res, h_buf, mask_ref, first_ref,
     own_sem, piece_send, piece_recv, keep_sem, out_sem, x_sem, misc_send, misc_recv) = refs[25:]
    rows, width = x_buf.shape
    pieces = wbuf.shape[1]
    count = (pieces - 4) // 2
    sec = lax.axis_index("section")
    mine = pl.ds(pl.multiple_of(sec * rows, rows), rows)
    others = pl.ds(pl.multiple_of((1 - sec) * rows, rows), rows)
    partner = {"section": 1 - sec}

    def own_piece(n):
        return pltpu.make_async_copy(weight_piece(own_weights, n, width), wbuf.at[sec, n], own_sem.at[n])

    def sent_piece(n, block):
        return pltpu.make_async_remote_copy(
            src_ref=weight_piece(own_weights, n, width), dst_ref=wbuf.at[block, n],
            send_sem=piece_send.at[n], recv_sem=piece_recv.at[n], device_id=partner, device_id_type=MESH,
        )

    def kept_piece(n):
        return pltpu.make_async_copy(wbuf.at[1 - sec, n], theirs_out.at[n], keep_sem.at[n])

    def sent_small():
        return pltpu.make_async_remote_copy(
            src_ref=smalls.at[sec], dst_ref=smalls.at[sec],
            send_sem=misc_send.at[0], recv_sem=misc_recv.at[0], device_id=partner, device_id_type=MESH,
        )

    def sent_cot():
        return pltpu.make_async_remote_copy(
            src_ref=cotangent.at[0, others], dst_ref=cot_out,
            send_sem=misc_send.at[1], recv_sem=misc_recv.at[1], device_id=partner, device_id_type=MESH,
        )

    def sent_state(b):
        return pltpu.make_async_remote_copy(
            src_ref=y_buf.at[b], dst_ref=states_out.at[mine],
            send_sem=misc_send.at[2], recv_sem=misc_recv.at[2], device_id=partner, device_id_type=MESH,
        )

    def own_state(b):
        return pltpu.make_async_copy(y_buf.at[b], states_out.at[mine], x_sem.at[1])

    def piece(b, n):
        @pl.when(sec == b)
        def _():
            own_piece(n).wait()

        @pl.when(sec != b)
        def _():
            sent_piece(n, b).wait_recv()
            kept_piece(n).start()

        return wbuf.at[b, n]

    barrier = pltpu.get_barrier_semaphore()
    pl.semaphore_signal(barrier, inc=1, device_id=partner, device_id_type=MESH)
    load_x = pltpu.make_async_copy(hidden.at[mine], x_buf, x_sem.at[0])
    load_x.start()
    for n in range(pieces):
        own_piece(n).start()
    smalls[sec, 0:6, :] = biases_ref[0]
    smalls[sec, 6:8, :] = gains_ref[0]
    for j in range(count):
        smalls[sec, 8 + j : 9 + j, :] = upb_ref[:, j * width : (j + 1) * width]
    smalls[sec, 8 + count :, :] = jnp.zeros((smalls.shape[1] - 8 - count, width), F32)
    pl.semaphore_wait(barrier, 1)
    sent_small().start()
    for n in range(pieces):
        sent_piece(n, sec).start()
    sent_cot().start()
    spread_marks(seg_ref, sec, mask_ref, first_ref)
    load_x.wait()
    sent_small().wait()

    buffers = (
        (qkv_buf, qkv_out), (o_buf, o_out), (lse_buf, lse_out), (n1_buf, n1_out), (inv1_buf, inv1_out),
        (hlow_buf, hlow_out), (g_buf, g_out), (slope_buf, slope_out), (n2_buf, n2_out), (inv2_buf, inv2_out),
    )
    QKV, O, LSE, N1, INV1, HLOW, G, SLOPE, N2, INV2 = range(10)

    def stored(b, which):
        return pltpu.make_async_copy(buffers[which][0], buffers[which][1].at[b], out_sem.at[which])

    def store(b, *names):
        for which in names:
            stored(b, which).start()

    def free(b, *names):
        if b == 1:
            for which in names:
                stored(0, which).wait()

    for b in range(2):
        small = smalls.at[b]
        free(b, QKV)
        for n in range(3):
            block = piece(b, n)

            def project(t):
                cols = tile_of(t)
                there = pl.ds(pl.multiple_of(n * width + t * TILE, TILE), TILE)
                value = dot_nn(x_buf[...], block[:, cols])
                if n == 0:
                    value = (value + small[0:1, cols]) * (HEAD ** -0.5)
                elif n == 2:
                    value = value + small[1:2, cols]
                qkv_buf[:, there] = value.astype(BF)

            loop(width // TILE, project, 3)
        store(b, QKV)
        free(b, O, LSE)

        def attend(pair):
            queries = qkv_buf[:, tile_of(pair, 128)]
            keys = qkv_buf[:, pl.ds(pl.multiple_of(width + pair * 128, 128), 128)]
            values = qkv_buf[:, pl.ds(pl.multiple_of(2 * width + pair * 128, 128), 128)]
            masks = lane_masks((rows, 128))
            parts = []
            for h in range(2):
                scores = dot_nt(keys, jnp.where(masks[h], queries, jnp.zeros_like(queries))) + mask_ref[...]
                top = jnp.max(scores, axis=0, keepdims=True)
                weight = jnp.exp(scores - top)
                total = jnp.sum(weight, axis=0, keepdims=True)
                lse_buf[pair, pl.ds(h, 1), :] = top + jnp.log(total)
                result = dot_tn(values, weight.astype(BF))
                parts.append(result[h * HEAD : (h + 1) * HEAD] * (1.0 / total))
            o_buf[:, tile_of(pair, 128)] = jnp.concatenate(parts, axis=0).T.astype(BF)

        loop(HEADS // 2, attend, 2)
        store(b, O, LSE)
        mixer = piece(b, 3)

        def mix(t):
            cols = tile_of(t)
            res[:, cols] = x_buf[:, cols].astype(F32) + (dot_nn(o_buf[...], mixer[:, cols]) + small[2:3, cols])

        loop(width // TILE, mix, 3)
        free(b, N1, INV1, HLOW)

        def norm_one(i):
            r = tile_of(i, ROWS)
            normed, inv = normed_rows(res[r, :])
            n1_buf[r, :] = normed
            inv1_buf[r, :] = jnp.broadcast_to(inv, (ROWS, 128))
            h = normed * small[6:7, :] + small[3:4, :]
            h_buf[r, :] = h + small[4:5, :]
            hlow_buf[r, :] = h.astype(BF)

        loop(rows // ROWS, norm_one, 2)
        store(b, N1, INV1, HLOW)
        free(b, G, SLOPE)
        for j in range(count):
            up = piece(b, 4 + j)

            def widen(t):
                cols = tile_of(t)
                there = pl.ds(pl.multiple_of(j * width + t * TILE, TILE), TILE)
                z = dot_nn(hlow_buf[...], up[:, cols]) + small[8 + j : 9 + j, cols]
                half = 0.5 * (1.0 + lax.erf(z * INV_ROOT_TWO))
                g_buf[:, there] = (z * half).astype(BF)
                slope_buf[:, there] = (half + z * jnp.exp(-0.5 * z * z) * INV_ROOT_TAU).astype(BF)

            loop(width // TILE, widen, 3)
        store(b, G, SLOPE)
        for j in range(count):
            down = piece(b, 4 + count + j)

            def narrow(t):
                cols = tile_of(t)
                h_buf[:, cols] += dot_nn(g_buf[:, j * width : (j + 1) * width], down[:, cols])

            loop(width // TILE, narrow, 3)
        free(b, N2, INV2)

        def norm_two(i):
            r = tile_of(i, ROWS)
            normed, inv = normed_rows(h_buf[r, :])
            n2_buf[r, :] = normed
            inv2_buf[r, :] = jnp.broadcast_to(inv, (ROWS, 128))
            y = (normed * small[7:8, :] + small[5:6, :]).astype(BF)
            y_buf[b, r, :] = y
            if b == 0:
                x = x_buf[r, :].astype(F32)
                x_buf[r, :] = jnp.where(first_ref[r, 0:1] > 0.5, y.astype(F32), x).astype(BF)

        loop(rows // ROWS, norm_two, 2)
        store(b, N2, INV2)
        if b == 0:
            pltpu.make_async_copy(x_buf, x1_out, x_sem.at[0]).start()

        @pl.when(sec == b)
        def _():
            own_state(b).start()

        @pl.when(sec != b)
        def _():
            sent_state(b).start()

    for which in range(10):
        stored(1, which).wait()
    pltpu.make_async_copy(x_buf, x1_out, x_sem.at[0]).wait()
    own_state(0).wait()
    sent_state(0).wait()
    sent_cot().wait()
    for n in range(pieces):
        sent_piece(n, sec).wait_send()
        kept_piece(n).wait()


def norm_back(gradient, normed, inv):
    return inv * (
        gradient
        - jnp.mean(gradient, axis=-1, keepdims=True)
        - normed * jnp.mean(gradient * normed, axis=-1, keepdims=True)
    )


def column_sum(v):
    return jnp.sum(v, axis=0, keepdims=True)


def backward_kernel(
    block,
    cot_ref, dnext_ref, segr_ref, segc_ref, first_ref, small_ref,
    qkv_ref, o_ref, lse_ref, n1_ref, inv1_ref, slope_ref, n2_ref, inv2_ref,
    wqkv_m, wqkv_t, wout_m, wout_t, wup_m, wup_t, wdown_m, wdown_t,
    dx_ref, dproj_ref, da_ref, dz_ref, df_ref, dsmall_ref, dup_ref,
    wqkv, wout, wup, wdown, mask_ref, dr_ref, dh_ref, do_ref, sems,
):
    rows, width = cot_ref.shape
    hidden_width = wup.shape[1]
    weights = Weights(
        block,
        ((wdown_m, wdown_t), (wup_m, wup_t), (wout_m, wout_t), (wqkv_m, wqkv_t)),
        (wdown, wup, wout, wqkv),
        sems,
    )
    mask_ref[...] = jnp.where(segc_ref[...] == segr_ref[...], 0.0, MASKED)
    dsmall_ref[...] = jnp.zeros_like(dsmall_ref)

    def norm_two(i):
        r = tile_of(i, ROWS)
        gradient = cot_ref[r, :].astype(F32)
        if block == 0:
            back = dnext_ref[r, :].astype(BF).astype(F32)
            gradient = gradient + jnp.where(first_ref[r, :] > 0.5, back, 0.0)
        normed = n2_ref[r, :]
        dr = norm_back(gradient * small_ref[7:8, :], normed, inv2_ref[r, 0:1])
        dr_ref[r, :] = dr
        df_ref[r, :] = dr.astype(BF)
        dsmall_ref[7:8, :] += column_sum(gradient * normed)
        dsmall_ref[5:6, :] += column_sum(gradient)
        dsmall_ref[4:5, :] += column_sum(dr)

    loop(rows // ROWS, norm_two, 2)
    weights.wait(0)

    def narrow(j):
        cols = tile_of(j)
        dz = dot_nt(df_ref[...], wdown[cols, :]) * slope_ref[:, cols].astype(F32)
        dup_ref[:, cols] = column_sum(dz)
        dz_ref[:, cols] = dz.astype(BF)

    loop(hidden_width // TILE, narrow)
    weights.wait(1)

    def widen(j):
        cols = tile_of(j)
        dh_ref[:, cols] = dr_ref[:, cols] + dot_nt(dz_ref[...], wup[cols, :])

    loop(width // TILE, widen, 3)

    def norm_one(i):
        r = tile_of(i, ROWS)
        gradient = dh_ref[r, :]
        normed = n1_ref[r, :]
        dr = norm_back(gradient * small_ref[6:7, :], normed, inv1_ref[r, 0:1])
        dr_ref[r, :] = dr
        da_ref[r, :] = dr.astype(BF)
        dsmall_ref[6:7, :] += column_sum(gradient * normed)
        dsmall_ref[3:4, :] += column_sum(gradient)
        dsmall_ref[2:3, :] += column_sum(dr)

    loop(rows // ROWS, norm_one, 2)
    weights.wait(2)

    def mix(j):
        cols = tile_of(j)
        do_ref[:, cols] = dot_nt(da_ref[...], wout[cols, :]).astype(BF)

    loop(width // TILE, mix, 3)

    def attend(pair):
        here = tile_of(pair, 128)
        key_cols = pl.ds(pl.multiple_of(width + pair * 128, 128), 128)
        value_cols = pl.ds(pl.multiple_of(2 * width + pair * 128, 128), 128)
        queries, keys, values = qkv_ref[:, here], qkv_ref[:, key_cols], qkv_ref[:, value_cols]
        grad = do_ref[:, here]
        masks = lane_masks((rows, 128))
        dq, dk, dv = [], 0.0, 0.0
        for h in range(2):
            head_queries = jnp.where(masks[h], queries, jnp.zeros_like(queries))
            head_grad = jnp.where(masks[h], grad, jnp.zeros_like(grad))
            scores = dot_nt(keys, head_queries) + mask_ref[...]
            weight = jnp.exp(scores - lse_ref[pair, pl.ds(h, 1), :])
            dweight = dot_nt(values, head_grad)
            delta = jnp.sum(weight * dweight, axis=0, keepdims=True)
            dscore = (weight * (dweight - delta)).astype(BF)
            dq.append(dot_tn(keys, dscore)[h * HEAD : (h + 1) * HEAD])
            dk = dk + dot_nn(dscore, head_queries)
            dv = dv + dot_nn(weight.astype(BF), head_grad)
        dq = jnp.concatenate(dq, axis=0).T * (HEAD ** -0.5)
        dsmall_ref[0:1, here] = column_sum(dq)
        dsmall_ref[1:2, here] = column_sum(dv)
        dproj_ref[:, here] = dq.astype(BF)
        dproj_ref[:, key_cols] = dk.astype(BF)
        dproj_ref[:, value_cols] = dv.astype(BF)

    loop(HEADS // 2, attend)
    weights.wait(3)

    def project(j):
        cols = tile_of(j)
        dx = dr_ref[:, cols] + dot_nt(dproj_ref[...], wqkv[cols, :])
        if block == 0:
            dx = dx + jnp.where(first_ref[...] > 0.5, 0.0, dnext_ref[:, cols])
        dx_ref[:, cols] = dx

    loop(width // TILE, project, 3)


def in_vmem(count):
    return [pl.BlockSpec(memory_space=pltpu.VMEM)] * count


def in_hbm(count):
    return [pl.BlockSpec(memory_space=pl.ANY)] * count


def shaped(shape, dtype=F32):
    return jax.ShapeDtypeStruct(shape, dtype)


def both_forward(hidden, seg, cotangent, weights, biases, gains, up_bias):
    rows, width = hidden.shape[0] // 2, hidden.shape[1]
    hidden_width = up_bias.shape[1]
    pieces = 2 * hidden_width // width + 4
    kept = (
        ((rows, 3 * width), BF), ((rows, width), BF), ((HEADS // 2, 2, rows), F32), ((rows, width), F32),
        ((rows, 128), F32), ((rows, width), BF), ((rows, hidden_width), BF), ((rows, hidden_width), BF),
        ((rows, width), F32), ((rows, 128), F32),
    )
    return pl.pallas_call(
        forward_kernel,
        out_shape=tuple(shaped((2,) + shape, dtype) for shape, dtype in kept) + (
            shaped((rows, width), BF), shaped((2 * rows, width), BF), shaped((pieces, width, width), BF),
            shaped((rows, width), BF), shaped((2, 16, width)),
        ),
        in_specs=in_hbm(1) + in_vmem(1) + in_hbm(1) + in_hbm(4) + in_vmem(3),
        out_specs=tuple(in_hbm(14) + in_vmem(1)),
        scratch_shapes=[
            pltpu.VMEM((2, pieces, width, width), BF),
            pltpu.VMEM((rows, width), BF),
        ] + [pltpu.VMEM(shape, dtype) for shape, dtype in kept] + [
            pltpu.VMEM((2, rows, width), BF),
            pltpu.VMEM((rows, width), F32),
            pltpu.VMEM((rows, width), F32),
            pltpu.VMEM((rows, rows), F32),
            pltpu.VMEM((rows, 128), F32),
            pltpu.SemaphoreType.DMA((pieces,)),
            pltpu.SemaphoreType.DMA((pieces,)),
            pltpu.SemaphoreType.DMA((pieces,)),
            pltpu.SemaphoreType.DMA((pieces,)),
            pltpu.SemaphoreType.DMA((10,)),
            pltpu.SemaphoreType.DMA((2,)),
            pltpu.SemaphoreType.DMA((3,)),
            pltpu.SemaphoreType.DMA((3,)),
        ],
        compiler_params=pltpu.CompilerParams(
            collective_id=1, has_side_effects=True, vmem_limit_bytes=VMEM_BYTES
        ),
        name="forward",
    )(hidden, seg, cotangent, *weights, biases, gains, up_bias)


def block_backward(block, cot, dnext, segr, segc, first, small, kept, weights):
    rows, width = cot.shape
    hidden_width = weights[4].shape[1]
    scratch = [pltpu.VMEM(w.shape, BF) for w in weights[::2]]
    return pl.pallas_call(
        functools.partial(backward_kernel, block),
        out_shape=(
            shaped((rows, width)), shaped((rows, 3 * width), BF), shaped((rows, width), BF),
            shaped((rows, hidden_width), BF), shaped((rows, width), BF), shaped((16, width)), shaped((1, hidden_width)),
        ),
        in_specs=in_vmem(14) + in_hbm(8),
        out_specs=tuple(in_vmem(7)),
        scratch_shapes=scratch + [
            pltpu.VMEM((rows, rows), F32), pltpu.VMEM((rows, width), F32), pltpu.VMEM((rows, width), F32),
            pltpu.VMEM((rows, width), BF), pltpu.SemaphoreType.DMA((4,)),
        ],
        compiler_params=pltpu.CompilerParams(vmem_limit_bytes=VMEM_BYTES),
        name="backward" + str(block),
    )(cot, dnext, segr, segc, first, small, *kept, *weights)


ORDERS = {
    "A": (0, 1, 2, 3), "B": (1, 0, 2, 3), "C": (2, 3, 0, 1), "D": (2, 3, 1, 0), "E": (0, 2, 3, 1), "F": (1, 2, 3, 0),
}
BITS = 4
PARTS = 1 << BITS
SLOTS = 4
SEQUENCE = (8, 9, 10, 11, 4, 5, 6, 7, 3, 0, 1, 2)
KINDS = ("AFEBABABEFAB", "EFAFEFEFEFAF")
SCHEDULE = (
    1428, 1424, 1892, 1888, 2005, 2001, 2108, 2104, 2081, 2184, 2181, 2194, 2572, 2582, 2681, 2775,
    2771, 2844, 2850, 2973, 3046, 3043, 3145, 3312, 3450, 3431, 3533, 3700, 3838, 3896, 4093, 4160,
    4181, 4202, 4302, 4319, 4315, 4548, 4566, 4574, 4587, 4657, 4720, 4840, 4857, 4833, 4916, 4913,
    4946, 4975, 4951, 5016, 5029, 5050, 5026, 5420, 5417, 5589, 5586, 5606, 5699, 5802, 5785, 5779,
    5772, 5803, 5786, 5819, 5811, 5787, 5773, 5764, 5774, 5765, 5775, 5766, 5767, 5823, 5805, 5782,
    5788, 5799, 5783, 5760, 5806, 5789, 5768, 5761, 5807, 5790, 5769, 5762, 5791, 5763, 5770, 5771,
)


def owner(b, chunk):
    return (b + SEQUENCE.index(chunk)) % 2


def backward_sum_kernel(*refs):
    kept = refs[0:10]
    hidden, x1, cotangent, cot_theirs = refs[10:14]
    own_weights, theirs = refs[14:18], refs[18]
    seg_ref, smalls = refs[19:21]
    out_qkv, out_out, out_up, out_down, out_biases, out_gains, out_upb, grad_input = refs[21:29]
    (total, slots, stage, r1, r2, r3, r4, wring, gring, sring, lhs, turned, norm_buf, inv_buf, cot_buf, qkv_buf, lse_buf,
     low_buf, dz_buf, acc, dx_ref, mask_ref, first_ref, dsmall, small_sum, small_in,
     cross_send, cross_recv, done_send, done_recv, send, recv, small_send, small_recv, wsem, gsem, ssem, asem,
     grad_sem) = refs[29:]
    received = (r1, r2, r3, r4)
    rows, width = acc.shape
    share = total.shape[-2]
    wide = gring.shape[0]
    count = out_up.shape[1] // width
    sec, me = lax.axis_index("section"), lax.axis_index("dp")
    bits = [(me >> k) & 1 for k in range(BITS)]
    mine = pl.ds(pl.multiple_of(sec * rows, rows), rows)

    barrier = pltpu.get_barrier_semaphore()
    for k in range(BITS):
        pl.semaphore_signal(barrier, inc=1, device_id={"dp": me ^ (1 << k)}, device_id_type=MESH)
    pl.semaphore_signal(barrier, inc=1, device_id={"section": 1 - sec}, device_id_type=MESH)

    weight_list = []
    for b in (1, 0):
        for j in range(count):
            weight_list += [(b, 4 + count + j), (b, 4 + j)]
        weight_list += [(b, 3), (b, 0), (b, 1), (b, 2)]

    def weight_copy(n, own):
        which = weight_list[n][1]
        source = weight_piece(own_weights, which, width) if own else theirs.at[which]
        return pltpu.make_async_copy(source, wring.at[n % wring.shape[0]], wsem.at[n % wring.shape[0]])

    def weight_start(n):
        if n < len(weight_list):
            own = sec == weight_list[n][0]

            @pl.when(own)
            def _():
                weight_copy(n, True).start()

            @pl.when(jnp.logical_not(own))
            def _():
                weight_copy(n, False).start()

    taken = [0]

    def weight_next():
        n = taken[0]
        taken[0] += 1
        weight_copy(n, False).wait()
        return wring.at[n % wring.shape[0]]

    def weight_done():
        weight_start(taken[0] - 1 + wring.shape[0])

    QKV, O, LSE, N1, INV1, HLOW, G, SLOPE, N2, INV2, COT, X = range(12)
    targets = {
        COT: (cot_buf, 0), QKV: (qkv_buf, 1), O: (lhs, 2), LSE: (lse_buf, 3), N1: (norm_buf, 4), INV1: (inv_buf, 5),
        HLOW: (lhs, 2), N2: (norm_buf, 4), INV2: (inv_buf, 5), X: (lhs, 2),
    }

    def act(b, which, own=False):
        target, sem = targets[which]
        if which == COT:
            source = cotangent.at[0, mine] if own else cot_theirs
        elif which == X:
            source = x1 if b == 1 else hidden.at[mine]
        else:
            source = kept[which].at[b]
        return pltpu.make_async_copy(source, target, asem.at[sem])

    def ring(b, which, j):
        buf, sem = (gring, gsem) if which == G else (sring, ssem)
        source = kept[which].at[b, :, pl.ds(j * width, width)]
        return pltpu.make_async_copy(source, buf.at[j % wide], sem.at[j % wide])

    def place(part):
        return tuple((part >> (BITS - 1 - k)) & 1 for k in range(BITS))

    def across(chunk, slot):
        return pltpu.make_async_remote_copy(
            src_ref=slots.at[slot], dst_ref=total.at[chunk],
            send_sem=cross_send.at[chunk], recv_sem=cross_recv.at[chunk],
            device_id={"section": 1 - sec}, device_id_type=MESH,
        )

    def hand_over(b, chunk, slot):
        @pl.when(sec != owner(b, chunk))
        def _():
            across(chunk, slot).start()

    def exchange(b, chunk, phase):
        order = ORDERS[KINDS[b][SEQUENCE.index(chunk)]]
        at = [slice(None)] * BITS
        for done in range(phase):
            at[BITS - 1 - order[done]] = bits[order[done]]
        at[BITS - 1 - order[phase]] = 1 - bits[order[phase]]
        return pltpu.make_async_remote_copy(
            src_ref=total.at[(chunk,) + tuple(at)], dst_ref=received[phase].at[chunk],
            send_sem=send.at[chunk, phase], recv_sem=recv.at[chunk, phase],
            device_id={"dp": me ^ (1 << order[phase])}, device_id_type=MESH,
        )

    def finish(b, chunk, slot):
        @pl.when(sec == owner(b, chunk))
        def _():
            across(chunk, slot).wait_recv()

            def one(i):
                at = (i // 8, (i // 4) % 2, (i // 2) % 2, i % 2)
                total[(chunk,) + at] = total[(chunk,) + at] + slots[(slot,) + at]

            loop(PARTS, one, 4)
            exchange(b, chunk, 0).start()

        @pl.when(sec != owner(b, chunk))
        def _():
            across(chunk, slot).wait_send()

    def result_of(chunk):
        if chunk < 3:
            return out_qkv.at[:, pl.ds(chunk * width, width)]
        if chunk < 4:
            return out_out
        if chunk < 8:
            return out_up.at[:, pl.ds((chunk - 4) * width, width)]
        return out_down.at[pl.ds((chunk - 8) * share, share), :]

    def bring(chunk):
        return pltpu.make_async_remote_copy(
            src_ref=stage.at[SEQUENCE.index(chunk) // 2], dst_ref=result_of(chunk),
            send_sem=done_send.at[chunk], recv_sem=done_recv.at[chunk],
            device_id={"section": 1 - sec}, device_id_type=MESH,
        )

    def take(b, chunk, phase):
        order = ORDERS[KINDS[b][SEQUENCE.index(chunk)]]
        exchange(b, chunk, phase).wait()

        def one(i):
            at, inner, left = [None] * BITS, [], i
            for done in range(phase + 1):
                at[BITS - 1 - order[done]] = bits[order[done]]
            for d in reversed([d for d in range(BITS) if at[d] is None]):
                at[d] = left % 2
                inner.insert(0, at[d])
                left = left // 2
            at = (chunk,) + tuple(at)
            total[at] = total[at] + received[phase][(chunk,) + tuple(inner)]

        if phase < BITS - 1:
            loop(PARTS >> (phase + 1), one, min(4, PARTS >> (phase + 1)))
            exchange(b, chunk, phase + 1).start()
        else:
            value = total[(chunk,) + tuple(bits[BITS - 1 - d] for d in range(BITS))].astype(F32)
            value = value + received[phase][chunk].astype(F32)
            if owner(b, chunk) == b:
                result_of(chunk)[...] = value
            else:
                stage[SEQUENCE.index(chunk) // 2] = value
                bring(chunk).start()

    steps = [(n // 96, (n // 48) % 2, (n // 4) % 12, n % 4) for n in SCHEDULE]
    points = [0]

    def run_steps(chosen):
        for core in range(2):
            mine = [step for step in chosen if owner(step[1], step[2]) == core]
            if mine:

                @pl.when(sec == core)
                def _():
                    for _, b, chunk, phase in mine:
                        take(b, chunk, phase)

    def point():
        run_steps([step for step in steps if step[0] == points[0]])
        points[0] += 1

    def product(right, right_col, put):
        def one(n):
            cols = tile_of(n)
            rhs_cols = pl.ds(pl.multiple_of(right_col + n * TILE, TILE), TILE)
            result = dot_nn(turned[...], right[:, rhs_cols]).astype(BF)
            for piece in range(PARTS):
                slot, part = put(piece)
                slots[(slot,) + place(part) + (slice(None), cols)] = result[piece * share : (piece + 1) * share]

        loop(width // TILE, one, 3)

    def first_loads(b):
        @pl.when(sec == b)
        def _():
            act(b, COT, True).start()

        @pl.when(sec != b)
        def _():
            act(b, COT).start()

        act(b, N2).start()
        act(b, INV2).start()
        for j in range(wide):
            ring(b, G, j).start()
            ring(b, SLOPE, j).start()

    first_loads(1)
    act(1, HLOW).start()
    for n in range(wring.shape[0]):
        weight_start(n)
    spread_marks(seg_ref, sec, mask_ref, first_ref)
    dsmall[...] = jnp.zeros_like(dsmall)

    for b in (1, 0):
        small = smalls.at[b]
        act(b, QKV).start()
        act(b, LSE).start()
        act(b, COT).wait()
        act(b, N2).wait()
        act(b, INV2).wait()

        def norm_two(i):
            r = tile_of(i, ROWS)
            gradient = cot_buf[r, :].astype(F32)
            if b == 0:
                back = dx_ref[r, :].astype(BF).astype(F32)
                gradient = gradient + jnp.where(first_ref[r, 0:1] > 0.5, back, 0.0)
            normed = norm_buf[r, :]
            dr = norm_back(gradient * small[7:8, :], normed, inv_buf[r, 0:1])
            acc[r, :] = dr
            low_buf[r, :] = dr.astype(BF)
            dsmall[b, 7:8, :] += column_sum(gradient * normed)
            dsmall[b, 5:6, :] += column_sum(gradient)
            dsmall[b, 4:5, :] += column_sum(dr)

        loop(rows // ROWS, norm_two, 2)
        act(b, N1).start()
        act(b, INV1).start()
        if b == 1:
            pl.semaphore_wait(barrier, BITS + 1)
        point()
        for j in range(count):
            ring(b, G, j).wait()
            turned[...] = gring[j % wide].T
            if j + wide < count:
                ring(b, G, j + wide).start()
            product(low_buf, 0, lambda piece: (piece % count, j * (PARTS // count) + piece // count))
            point()
        for c in range(count):
            hand_over(b, 8 + c, c)
        act(b, HLOW).wait()
        turned[...] = lhs[...].T
        act(b, O).start()

        for j in range(count):
            down = weight_next()
            ring(b, SLOPE, j).wait()

            def narrow(t):
                cols = tile_of(t)
                dz = dot_nt(low_buf[...], down[cols, :]) * sring[j % wide, :, cols].astype(F32)
                dsmall[b, 8 + j : 9 + j, cols] = column_sum(dz)
                dz_buf[:, cols] = dz.astype(BF)

            loop(width // TILE, narrow, 3)
            weight_done()
            if j + wide < count:
                ring(b, SLOPE, j + wide).start()
            point()
            finish(b, 8 + j, j)
            product(dz_buf, 0, lambda piece: (j, piece))
            hand_over(b, 4 + j, j)
            point()
            up = weight_next()

            def widen(t):
                cols = tile_of(t)
                acc[:, cols] += dot_nt(dz_buf[...], up[cols, :])

            loop(width // TILE, widen, 3)
            weight_done()
            point()
            if j > 0:
                finish(b, 3 + j, j - 1)
        act(b, N1).wait()
        act(b, INV1).wait()

        def norm_one(i):
            r = tile_of(i, ROWS)
            gradient = acc[r, :]
            normed = norm_buf[r, :]
            dr = norm_back(gradient * small[6:7, :], normed, inv_buf[r, 0:1])
            acc[r, :] = dr
            low_buf[r, :] = dr.astype(BF)
            dsmall[b, 6:7, :] += column_sum(gradient * normed)
            dsmall[b, 3:4, :] += column_sum(gradient)
            dsmall[b, 2:3, :] += column_sum(dr)

        loop(rows // ROWS, norm_one, 2)
        finish(b, 7, 3)
        point()
        act(b, O).wait()
        turned[...] = lhs[...].T
        act(b, X).start()
        product(low_buf, 0, lambda piece: (0, piece))
        hand_over(b, 3, 0)
        point()
        mixer = weight_next()

        def mix(t):
            cols = tile_of(t)
            cot_buf[:, cols] = dot_nt(low_buf[...], mixer[cols, :]).astype(BF)

        loop(width // TILE, mix, 3)
        weight_done()
        act(b, QKV).wait()
        act(b, LSE).wait()
        point()

        def attend(pair):
            here = tile_of(pair, 128)
            key_cols = pl.ds(pl.multiple_of(width + pair * 128, 128), 128)
            value_cols = pl.ds(pl.multiple_of(2 * width + pair * 128, 128), 128)
            queries, keys, values = qkv_buf[:, here], qkv_buf[:, key_cols], qkv_buf[:, value_cols]
            grad = cot_buf[:, here]
            masks = lane_masks((rows, 128))
            dq, dk, dv = [], 0.0, 0.0
            for h in range(2):
                head_queries = jnp.where(masks[h], queries, jnp.zeros_like(queries))
                head_grad = jnp.where(masks[h], grad, jnp.zeros_like(grad))
                scores = dot_nt(keys, head_queries) + mask_ref[...]
                weight = jnp.exp(scores - lse_buf[pair, pl.ds(h, 1), :])
                dweight = dot_nt(values, head_grad)
                delta = jnp.sum(weight * dweight, axis=0, keepdims=True)
                dscore = (weight * (dweight - delta)).astype(BF)
                dq.append(dot_tn(keys, dscore)[h * HEAD : (h + 1) * HEAD])
                dk = dk + dot_nn(dscore, head_queries)
                dv = dv + dot_nn(weight.astype(BF), head_grad)
            dq = jnp.concatenate(dq, axis=0).T * (HEAD ** -0.5)
            dsmall[b, 0:1, here] = column_sum(dq)
            dsmall[b, 1:2, here] = column_sum(dv)
            qkv_buf[:, here] = dq.astype(BF)
            qkv_buf[:, key_cols] = dk.astype(BF)
            qkv_buf[:, value_cols] = dv.astype(BF)

        for third in range(3):
            loop(HEADS // 6, lambda i: attend(third * (HEADS // 6) + i), 2)
            if third == 0:
                finish(b, 3, 0)
            point()
        act(b, X).wait()
        turned[...] = lhs[...].T
        if b == 1:
            act(0, HLOW).start()
            first_loads(0)
        point()

        for j in range(3):
            product(qkv_buf, j * width, lambda piece: (1 + j, piece))
            hand_over(b, j, 1 + j)
            point()
            block_weight = weight_next()

            def project(t):
                cols = tile_of(t)
                dx = acc[:, cols] + dot_nt(qkv_buf[:, j * width : (j + 1) * width], block_weight[cols, :])
                if j < 2:
                    acc[:, cols] = dx
                elif b == 1:
                    dx_ref[:, cols] = dx
                else:
                    dx_ref[:, cols] = dx + jnp.where(first_ref[:, 0:1] > 0.5, 0.0, dx_ref[:, cols])

            loop(width // TILE, project, 3)
            weight_done()
            point()
            if j > 0:
                finish(b, j - 1, j)
        finish(b, 2, 3)

    def own_grad():
        return pltpu.make_async_copy(dx_ref, grad_input.at[mine], grad_sem.at[0])

    def sent_grad():
        return pltpu.make_async_remote_copy(
            src_ref=dx_ref, dst_ref=grad_input.at[mine], send_sem=grad_sem.at[1], recv_sem=grad_sem.at[2],
            device_id={"section": 1 - sec}, device_id_type=MESH,
        )

    own_grad().start()
    sent_grad().start()

    def small_exchange(phase):
        target = {"section": 1 - sec} if phase == 0 else {"dp": me ^ (1 << (phase - 1))}
        source = dsmall.at[1 - sec] if phase == 0 else small_sum.at[phase]
        return pltpu.make_async_remote_copy(
            src_ref=source, dst_ref=small_in.at[phase], send_sem=small_send.at[phase], recv_sem=small_recv.at[phase],
            device_id=target, device_id_type=MESH,
        )

    def small_take(phase):
        small_exchange(phase).wait()
        before = dsmall[sec] if phase == 0 else small_sum[phase]
        if phase < BITS:
            small_sum[phase + 1] = before + small_in[phase]
            small_exchange(phase + 1).start()
        else:
            sums = before + small_in[phase]
            for part in range(PARTS):
                cut = slice(part * share, (part + 1) * share)
                line, start = part * count // PARTS, (part % (PARTS // count)) * count * share

                @pl.when(me == part)
                def _():
                    out_biases[...] = sums[0:6, cut]
                    out_gains[...] = sums[6:8, cut]
                    out_upb[...] = sums[8 + line : 9 + line, start : start + count * share]

    small_exchange(0).start()
    left = [[step for step in steps if step[0] >= points[0] and owner(step[1], step[2]) == core] for core in range(2)]
    for phase in range(BITS + 1):
        run_steps(left[0][:3] + left[1][:3])
        left = [left[0][3:], left[1][3:]]
        small_take(phase)
    run_steps(left[0] + left[1])
    for chunk in SEQUENCE[1::2]:
        bring(chunk).wait()
    own_grad().wait()
    sent_grad().wait()


def backward_sum(kept, hidden, x1, cotangent, cot_theirs, weights, theirs, seg, smalls):
    rows, width = x1.shape
    hidden_width = kept[6].shape[2]
    share = width // PARTS
    chunks = 2 * hidden_width // width + 4
    return pl.pallas_call(
        backward_sum_kernel,
        out_shape=(
            shaped((share, 3 * width)), shaped((share, width)), shaped((share, hidden_width)),
            shaped((hidden_width // PARTS, width)), shaped((6, share)), shaped((2, share)),
            shaped((1, hidden_width // PARTS)), shaped((2 * rows, width)),
        ),
        in_specs=in_hbm(19) + in_vmem(2),
        out_specs=tuple(in_vmem(7) + in_hbm(1)),
        scratch_shapes=[
            pltpu.VMEM((chunks, 2, 2, 2, 2, share, width), BF),
            pltpu.VMEM((SLOTS, 2, 2, 2, 2, share, width), BF),
            pltpu.VMEM((chunks // 2, share, width), F32),
            pltpu.VMEM((chunks, 2, 2, 2, share, width), BF),
            pltpu.VMEM((chunks, 2, 2, share, width), BF),
            pltpu.VMEM((chunks, 2, share, width), BF),
            pltpu.VMEM((chunks, share, width), BF),
            pltpu.VMEM((3, width, width), BF),
            pltpu.VMEM((2, rows, width), BF),
            pltpu.VMEM((2, rows, width), BF),
            pltpu.VMEM((rows, width), BF),
            pltpu.VMEM((width, rows), BF),
            pltpu.VMEM((rows, width), F32),
            pltpu.VMEM((rows, 128), F32),
            pltpu.VMEM((rows, width), BF),
            pltpu.VMEM((rows, 3 * width), BF),
            pltpu.VMEM((HEADS // 2, 2, rows), F32),
            pltpu.VMEM((rows, width), BF),
            pltpu.VMEM((rows, width), BF),
            pltpu.VMEM((rows, width), F32),
            pltpu.VMEM((rows, width), F32),
            pltpu.VMEM((rows, rows), F32),
            pltpu.VMEM((rows, 128), F32),
            pltpu.VMEM((2, 16, width), F32),
            pltpu.VMEM((BITS + 1, 16, width), F32),
            pltpu.VMEM((BITS + 1, 16, width), F32),
            pltpu.SemaphoreType.DMA((chunks,)),
            pltpu.SemaphoreType.DMA((chunks,)),
            pltpu.SemaphoreType.DMA((chunks,)),
            pltpu.SemaphoreType.DMA((chunks,)),
            pltpu.SemaphoreType.DMA((chunks, BITS)),
            pltpu.SemaphoreType.DMA((chunks, BITS)),
            pltpu.SemaphoreType.DMA((BITS + 1,)),
            pltpu.SemaphoreType.DMA((BITS + 1,)),
            pltpu.SemaphoreType.DMA((3,)),
            pltpu.SemaphoreType.DMA((2,)),
            pltpu.SemaphoreType.DMA((2,)),
            pltpu.SemaphoreType.DMA((6,)),
            pltpu.SemaphoreType.DMA((3,)),
        ],
        compiler_params=pltpu.CompilerParams(
            collective_id=0, has_side_effects=True, vmem_limit_bytes=VMEM_BYTES
        ),
        name="backward_sum",
    )(*kept, hidden, x1, cotangent, cot_theirs, *weights, theirs, seg, smalls)


def sum_plainly(pieces, small):
    def scattered(names):
        both = jnp.stack([dot_tn(pieces[b][names[0]], pieces[b][names[1]]) for b in range(2)])
        own = lax.psum_scatter(both, "section", scatter_dimension=0, tiled=False)
        return lax.psum_scatter(own, "dp", scatter_dimension=0, tiled=True)

    own_small = lax.psum(lax.psum_scatter(small, "section", scatter_dimension=0, tiled=False), "dp")
    return tuple(scattered(names) for names in ((0, 1), (2, 3), (4, 5), (6, 7))) + (own_small,)


def hand_out_kernel(count, *refs):
    given, results, held, sems = refs[:count], refs[count : 2 * count], refs[2 * count : 3 * count], refs[3 * count]
    loads = [pltpu.make_async_copy(given[i], held[i], sems.at[0, i]) for i in range(count)]
    stores = [pltpu.make_async_copy(held[i], results[i], sems.at[1, i]) for i in range(count)]
    for load in loads:
        load.start()
    for load, store in zip(loads, stores):
        load.wait()
        store.start()
    for store in stores:
        store.wait()


def hand_out(results):
    count = len(results)
    return pl.pallas_call(
        functools.partial(hand_out_kernel, count),
        out_shape=tuple(shaped(result.shape, result.dtype) for result in results),
        in_specs=in_hbm(count),
        out_specs=tuple(in_hbm(count)),
        scratch_shapes=[pltpu.VMEM(result.shape, result.dtype) for result in results] + [
            pltpu.SemaphoreType.DMA((2, count))
        ],
        compiler_params=pltpu.CompilerParams(vmem_limit_bytes=VMEM_BYTES),
        name="hand_out",
    )(*results)


def swap(value):
    return lax.ppermute(value, "section", [(0, 1), (1, 0)])


def backward_plainly(kept, hidden, x1, cotangent, cot_theirs, weights, theirs, seg, smalls):
    sec, me = lax.axis_index("section"), lax.axis_index("dp")
    share = hidden.shape[1] // lax.axis_size("dp")
    rows, width = x1.shape
    inputs = (lax.dynamic_slice_in_dim(hidden, sec * rows, rows, 0), x1)
    cot_own = lax.dynamic_slice_in_dim(cotangent[0], sec * rows, rows, 0)
    segments = lax.dynamic_index_in_dim(seg, sec, 0, False)
    segr, segc = segments.reshape(1, rows), segments.reshape(rows, 1)
    first = jnp.concatenate([jnp.ones((1,), F32), (segments[1:] != segments[:-1]).astype(F32)]).reshape(rows, 1)
    pairs = []
    for own in weights:
        pairs += [own[0], swap(own[0])]
    pieces, dsmalls, dnext = [None, None], [None, None], x1
    for block in (1, 0):
        qkv, o, lse, n1, inv1, hlow, g, slope, n2, inv2 = (member[block] for member in kept)
        cot = jnp.where(sec == block, cot_own, cot_theirs)
        dnext, dproj, da, dz, df, dsmall, dup = block_backward(
            block, cot, dnext, segr, segc, first, smalls[block], (qkv, o, lse, n1, inv1, slope, n2, inv2), pairs,
        )
        pieces[block] = (inputs[block], dproj, o, da, hlow, dz, g, df)
        dsmalls[block] = jnp.concatenate([dsmall[:8], dup.reshape(-1, width), jnp.zeros((4, width), F32)], axis=0)
    *sums, small = sum_plainly(pieces, jnp.stack(dsmalls))
    columns = lax.dynamic_slice_in_dim(small[:8], me * share, share, 1)
    up_share = kept[6].shape[2] // lax.axis_size("dp")
    upb = lax.dynamic_slice_in_dim(small[8:12].reshape(1, -1), me * up_share, up_share, 1)
    other = swap(dnext)
    grad_input = jnp.concatenate([jnp.where(sec == 0, dnext, other), jnp.where(sec == 0, other, dnext)], axis=0)
    return (*sums, columns[:6], columns[6:], upb, grad_input)


def local(hidden, segment_ids, cotangent, w_qkv, w_out, w_up, w_down, biases, gains, up_bias):
    width = hidden.shape[1]
    assert hidden.shape[0] == 2 * segment_ids.shape[1]
    weights = (w_qkv, w_out, w_up, w_down)
    *kept, x1, states, theirs, cot_theirs, smalls = both_forward(
        hidden, segment_ids, cotangent, weights, biases, gains, up_bias
    )
    fits = lax.axis_size("dp") == PARTS and width % (16 * PARTS) == 0
    backward = backward_sum if fits else backward_plainly
    *totals, upb, grad_input = backward(
        kept, hidden, x1, cotangent, cot_theirs, weights, theirs, segment_ids, smalls
    )
    results = (states, grad_input, *totals, upb)
    if fits:
        results = hand_out(results)
    states, grad_input, *totals, upb = results
    return (states[None], grad_input) + tuple(member[None] for member in totals) + (upb,)


def solution(mesh):
    placed = (
        P("dp", None),
        P("dp", None),
        P("section", "dp", None),
        P("section", None, None),
        P("section", None, None),
        P("section", None, None),
        P("section", None, None),
        P("section", None, None),
        P("section", None, None),
        P("section", None),
    )
    return jax.shard_map(
        local,
        mesh=mesh,
        in_specs=placed,
        out_specs=(
            P("section", "dp", None),
            P("dp", None),
            P("section", "dp", None),
            P("section", "dp", None),
            P("section", "dp", None),
            P("section", "dp", None),
            P("section", None, "dp"),
            P("section", None, "dp"),
            P("section", "dp"),
        ),
        check_vma=False,
    )
```

```python
import functools

import jax
import jax.numpy as jnp
from jax import lax
from jax.experimental import pallas as pl
from jax.experimental.pallas import tpu as pltpu
from jax.sharding import PartitionSpec as P

HEADS = 12
HEAD = 64
NORM_EPS = 1e-12
MASKED = -1e30
INV_ROOT_TWO = 0.7071067811865476
INV_ROOT_TAU = 0.3989422804014327
MESH = pl.DeviceIdType.MESH
BF = jnp.bfloat16
F32 = jnp.float32
TILE = 256
ROWS = 128
VMEM_BYTES = 60 * 1024 * 1024


def dot_nn(a, b):
    return lax.dot_general(a, b, (((1,), (0,)), ((), ())), preferred_element_type=F32)


def dot_nt(a, b):
    return lax.dot_general(a, b, (((1,), (1,)), ((), ())), preferred_element_type=F32)


def dot_tn(a, b):
    return lax.dot_general(a, b, (((0,), (0,)), ((), ())), preferred_element_type=F32)


def loop(count, body, unroll=1):
    def step(i, carry):
        body(i)
        return carry

    lax.fori_loop(0, count, step, 0, unroll=unroll)


def tile_of(i, size=TILE):
    return pl.ds(pl.multiple_of(i * size, size), size)


class Weights:
    def __init__(self, block, pairs, targets, sems):
        self.waits = []
        own = lax.axis_index("section") == block
        for n, ((mine, theirs), target) in enumerate(zip(pairs, targets)):
            sem = sems.at[n]

            @pl.when(own)
            def _():
                pltpu.make_async_copy(mine, target, sem).start()

            @pl.when(jnp.logical_not(own))
            def _():
                pltpu.make_async_copy(theirs, target, sem).start()

            self.waits.append(pltpu.make_async_copy(mine, target, sem))

    def wait(self, n):
        self.waits[n].wait()


def normed_rows(residue):
    centered = residue - jnp.mean(residue, axis=-1, keepdims=True)
    inv = lax.rsqrt(jnp.mean(centered * centered, axis=-1, keepdims=True) + NORM_EPS)
    return centered * inv, inv


def lane_masks(shape):
    lane = lax.broadcasted_iota(jnp.int32, shape, 1)
    return (lane < HEAD, lane >= HEAD)


def spread_marks(seg_ref, sec, mask_ref, first_ref):
    rows = mask_ref.shape[0]
    line = jnp.where(sec == 0, seg_ref[0:1, :], seg_ref[1:2, :]).astype(F32)
    column = jnp.broadcast_to(line, (128, rows)).T
    mask_ref[...] = jnp.where(column[:, 0:1] == line, 0.0, MASKED)
    lines = jnp.broadcast_to(line, (8, rows))
    before = pltpu.roll(lines, 1, 1)
    lane = lax.broadcasted_iota(jnp.int32, (8, rows), 1)
    marks = jnp.where((lines != before) | (lane == 0), 1.0, 0.0)
    first_ref[...] = jnp.broadcast_to(marks[0:1, :], (128, rows)).T


def weight_piece(refs, n, width):
    wqkv, wout, wup, wdown = refs
    if n < 3:
        return wqkv.at[0, :, pl.ds(n * width, width)]
    if n < 4:
        return wout.at[0]
    count = wdown.shape[1] // width
    if n < 4 + count:
        return wup.at[0, :, pl.ds((n - 4) * width, width)]
    return wdown.at[0, pl.ds((n - 4 - count) * width, width), :]


def forward_kernel(*refs):
    hidden, seg_ref, cotangent = refs[0:3]
    own_weights = refs[3:7]
    biases_ref, gains_ref, upb_ref = refs[7:10]
    (qkv_out, o_out, lse_out, n1_out, inv1_out, hlow_out, g_out, slope_out, n2_out, inv2_out,
     x1_out, states_out, theirs_out, cot_out, smalls) = refs[10:25]
    (wbuf, x_buf, qkv_buf, o_buf, lse_buf, n1_buf, inv1_buf, hlow_buf, g_buf, slope_buf, n2_buf, inv2_buf, y_buf,
     res, h_buf, mask_ref, first_ref,
     own_sem, piece_send, piece_recv, keep_sem, out_sem, x_sem, misc_send, misc_recv) = refs[25:]
    rows, width = x_buf.shape
    pieces = wbuf.shape[1]
    count = (pieces - 4) // 2
    sec = lax.axis_index("section")
    mine = pl.ds(pl.multiple_of(sec * rows, rows), rows)
    others = pl.ds(pl.multiple_of((1 - sec) * rows, rows), rows)
    partner = {"section": 1 - sec}

    def own_piece(n):
        return pltpu.make_async_copy(weight_piece(own_weights, n, width), wbuf.at[sec, n], own_sem.at[n])

    def sent_piece(n, block):
        return pltpu.make_async_remote_copy(
            src_ref=weight_piece(own_weights, n, width), dst_ref=wbuf.at[block, n],
            send_sem=piece_send.at[n], recv_sem=piece_recv.at[n], device_id=partner, device_id_type=MESH,
        )

    def kept_piece(n):
        return pltpu.make_async_copy(wbuf.at[1 - sec, n], theirs_out.at[n], keep_sem.at[n])

    def sent_small():
        return pltpu.make_async_remote_copy(
            src_ref=smalls.at[sec], dst_ref=smalls.at[sec],
            send_sem=misc_send.at[0], recv_sem=misc_recv.at[0], device_id=partner, device_id_type=MESH,
        )

    def sent_cot():
        return pltpu.make_async_remote_copy(
            src_ref=cotangent.at[0, others], dst_ref=cot_out,
            send_sem=misc_send.at[1], recv_sem=misc_recv.at[1], device_id=partner, device_id_type=MESH,
        )

    def sent_state(b):
        return pltpu.make_async_remote_copy(
            src_ref=y_buf.at[b], dst_ref=states_out.at[mine],
            send_sem=misc_send.at[2], recv_sem=misc_recv.at[2], device_id=partner, device_id_type=MESH,
        )

    def own_state(b):
        return pltpu.make_async_copy(y_buf.at[b], states_out.at[mine], x_sem.at[1])

    def piece(b, n):
        @pl.when(sec == b)
        def _():
            own_piece(n).wait()

        @pl.when(sec != b)
        def _():
            sent_piece(n, b).wait_recv()
            kept_piece(n).start()

        return wbuf.at[b, n]

    barrier = pltpu.get_barrier_semaphore()
    pl.semaphore_signal(barrier, inc=1, device_id=partner, device_id_type=MESH)
    load_x = pltpu.make_async_copy(hidden.at[mine], x_buf, x_sem.at[0])
    load_x.start()
    for n in range(pieces):
        own_piece(n).start()
    for k in range(biases_ref.shape[0]):
        smalls[sec, k : k + 1, :] = biases_ref[k]
    smalls[sec, 6:8, :] = gains_ref[0]
    for j in range(count):
        smalls[sec, 8 + j : 9 + j, :] = upb_ref[:, j * width : (j + 1) * width]
    smalls[sec, 8 + count :, :] = jnp.zeros((smalls.shape[1] - 8 - count, width), F32)
    pl.semaphore_wait(barrier, 1)
    sent_small().start()
    for n in range(pieces):
        sent_piece(n, sec).start()
    sent_cot().start()
    spread_marks(seg_ref, sec, mask_ref, first_ref)
    load_x.wait()
    sent_small().wait()

    buffers = (
        (qkv_buf, qkv_out), (o_buf, o_out), (lse_buf, lse_out), (n1_buf, n1_out), (inv1_buf, inv1_out),
        (hlow_buf, hlow_out), (g_buf, g_out), (slope_buf, slope_out), (n2_buf, n2_out), (inv2_buf, inv2_out),
    )
    QKV, O, LSE, N1, INV1, HLOW, G, SLOPE, N2, INV2 = range(10)

    def stored(b, which):
        return pltpu.make_async_copy(buffers[which][0], buffers[which][1].at[b], out_sem.at[which])

    def store(b, *names):
        for which in names:
            stored(b, which).start()

    def free(b, *names):
        if b == 1:
            for which in names:
                stored(0, which).wait()

    for b in range(2):
        small = smalls.at[b]
        free(b, QKV)
        for n in range(3):
            block = piece(b, n)

            def project(t):
                cols = tile_of(t)
                there = pl.ds(pl.multiple_of(n * width + t * TILE, TILE), TILE)
                value = dot_nn(x_buf[...], block[:, cols])
                if n == 0:
                    value = (value + small[0:1, cols]) * (HEAD ** -0.5)
                elif n == 2:
                    value = value + small[1:2, cols]
                qkv_buf[:, there] = value.astype(BF)

            loop(width // TILE, project, 3)
        store(b, QKV)
        free(b, O, LSE)

        def attend(pair):
            queries = qkv_buf[:, tile_of(pair, 128)]
            keys = qkv_buf[:, pl.ds(pl.multiple_of(width + pair * 128, 128), 128)]
            values = qkv_buf[:, pl.ds(pl.multiple_of(2 * width + pair * 128, 128), 128)]
            masks = lane_masks((rows, 128))
            parts = []
            for h in range(2):
                scores = dot_nt(keys, jnp.where(masks[h], queries, jnp.zeros_like(queries))) + mask_ref[...]
                top = jnp.max(scores, axis=0, keepdims=True)
                weight = jnp.exp(scores - top)
                total = jnp.sum(weight, axis=0, keepdims=True)
                lse_buf[pair, pl.ds(h, 1), :] = top + jnp.log(total)
                result = dot_tn(values, weight.astype(BF))
                parts.append(result[h * HEAD : (h + 1) * HEAD] * (1.0 / total))
            o_buf[:, tile_of(pair, 128)] = jnp.concatenate(parts, axis=0).T.astype(BF)

        loop(HEADS // 2, attend, 2)
        store(b, O, LSE)
        mixer = piece(b, 3)

        def mix(t):
            cols = tile_of(t)
            res[:, cols] = x_buf[:, cols].astype(F32) + (dot_nn(o_buf[...], mixer[:, cols]) + small[2:3, cols])

        loop(width // TILE, mix, 3)
        free(b, N1, INV1, HLOW)

        def norm_one(i):
            r = tile_of(i, ROWS)
            normed, inv = normed_rows(res[r, :])
            n1_buf[r, :] = normed
            inv1_buf[r, :] = jnp.broadcast_to(inv, (ROWS, 128))
            h = normed * small[6:7, :] + small[3:4, :]
            h_buf[r, :] = h + small[4:5, :]
            hlow_buf[r, :] = h.astype(BF)

        loop(rows // ROWS, norm_one, 2)
        store(b, N1, INV1, HLOW)
        free(b, G, SLOPE)
        for j in range(count):
            up = piece(b, 4 + j)

            def widen(t):
                cols = tile_of(t)
                there = pl.ds(pl.multiple_of(j * width + t * TILE, TILE), TILE)
                z = dot_nn(hlow_buf[...], up[:, cols]) + small[8 + j : 9 + j, cols]
                half = 0.5 * (1.0 + lax.erf(z * INV_ROOT_TWO))
                g_buf[:, there] = (z * half).astype(BF)
                slope_buf[:, there] = (half + z * jnp.exp(-0.5 * z * z) * INV_ROOT_TAU).astype(BF)

            loop(width // TILE, widen, 3)
        store(b, G, SLOPE)
        for j in range(count):
            down = piece(b, 4 + count + j)

            def narrow(t):
                cols = tile_of(t)
                h_buf[:, cols] += dot_nn(g_buf[:, j * width : (j + 1) * width], down[:, cols])

            loop(width // TILE, narrow, 3)
        free(b, N2, INV2)

        def norm_two(i):
            r = tile_of(i, ROWS)
            normed, inv = normed_rows(h_buf[r, :])
            n2_buf[r, :] = normed
            inv2_buf[r, :] = jnp.broadcast_to(inv, (ROWS, 128))
            y = (normed * small[7:8, :] + small[5:6, :]).astype(BF)
            y_buf[b, r, :] = y
            if b == 0:
                x = x_buf[r, :].astype(F32)
                x_buf[r, :] = jnp.where(first_ref[r, 0:1] > 0.5, y.astype(F32), x).astype(BF)

        loop(rows // ROWS, norm_two, 2)
        store(b, N2, INV2)
        if b == 0:
            pltpu.make_async_copy(x_buf, x1_out, x_sem.at[0]).start()

        @pl.when(sec == b)
        def _():
            own_state(b).start()

        @pl.when(sec != b)
        def _():
            sent_state(b).start()

    for which in range(10):
        stored(1, which).wait()
    pltpu.make_async_copy(x_buf, x1_out, x_sem.at[0]).wait()
    own_state(0).wait()
    sent_state(0).wait()
    sent_cot().wait()
    for n in range(pieces):
        sent_piece(n, sec).wait_send()
        kept_piece(n).wait()


def norm_back(gradient, normed, inv):
    return inv * (
        gradient
        - jnp.mean(gradient, axis=-1, keepdims=True)
        - normed * jnp.mean(gradient * normed, axis=-1, keepdims=True)
    )


def column_sum(v):
    return jnp.sum(v, axis=0, keepdims=True)


def backward_kernel(
    block,
    cot_ref, dnext_ref, segr_ref, segc_ref, first_ref, small_ref,
    qkv_ref, o_ref, lse_ref, n1_ref, inv1_ref, slope_ref, n2_ref, inv2_ref,
    wqkv_m, wqkv_t, wout_m, wout_t, wup_m, wup_t, wdown_m, wdown_t,
    dx_ref, dproj_ref, da_ref, dz_ref, df_ref, dsmall_ref, dup_ref,
    wqkv, wout, wup, wdown, mask_ref, dr_ref, dh_ref, do_ref, sems,
):
    rows, width = cot_ref.shape
    hidden_width = wup.shape[1]
    weights = Weights(
        block,
        ((wdown_m, wdown_t), (wup_m, wup_t), (wout_m, wout_t), (wqkv_m, wqkv_t)),
        (wdown, wup, wout, wqkv),
        sems,
    )
    mask_ref[...] = jnp.where(segc_ref[...] == segr_ref[...], 0.0, MASKED)
    dsmall_ref[...] = jnp.zeros_like(dsmall_ref)

    def norm_two(i):
        r = tile_of(i, ROWS)
        gradient = cot_ref[r, :].astype(F32)
        if block == 0:
            back = dnext_ref[r, :].astype(BF).astype(F32)
            gradient = gradient + jnp.where(first_ref[r, :] > 0.5, back, 0.0)
        normed = n2_ref[r, :]
        dr = norm_back(gradient * small_ref[7:8, :], normed, inv2_ref[r, 0:1])
        dr_ref[r, :] = dr
        df_ref[r, :] = dr.astype(BF)
        dsmall_ref[7:8, :] += column_sum(gradient * normed)
        dsmall_ref[5:6, :] += column_sum(gradient)
        dsmall_ref[4:5, :] += column_sum(dr)

    loop(rows // ROWS, norm_two, 2)
    weights.wait(0)

    def narrow(j):
        cols = tile_of(j)
        dz = dot_nt(df_ref[...], wdown[cols, :]) * slope_ref[:, cols].astype(F32)
        dup_ref[:, cols] = column_sum(dz)
        dz_ref[:, cols] = dz.astype(BF)

    loop(hidden_width // TILE, narrow)
    weights.wait(1)

    def widen(j):
        cols = tile_of(j)
        dh_ref[:, cols] = dr_ref[:, cols] + dot_nt(dz_ref[...], wup[cols, :])

    loop(width // TILE, widen, 3)

    def norm_one(i):
        r = tile_of(i, ROWS)
        gradient = dh_ref[r, :]
        normed = n1_ref[r, :]
        dr = norm_back(gradient * small_ref[6:7, :], normed, inv1_ref[r, 0:1])
        dr_ref[r, :] = dr
        da_ref[r, :] = dr.astype(BF)
        dsmall_ref[6:7, :] += column_sum(gradient * normed)
        dsmall_ref[3:4, :] += column_sum(gradient)
        dsmall_ref[2:3, :] += column_sum(dr)

    loop(rows // ROWS, norm_one, 2)
    weights.wait(2)

    def mix(j):
        cols = tile_of(j)
        do_ref[:, cols] = dot_nt(da_ref[...], wout[cols, :]).astype(BF)

    loop(width // TILE, mix, 3)

    def attend(pair):
        here = tile_of(pair, 128)
        key_cols = pl.ds(pl.multiple_of(width + pair * 128, 128), 128)
        value_cols = pl.ds(pl.multiple_of(2 * width + pair * 128, 128), 128)
        queries, keys, values = qkv_ref[:, here], qkv_ref[:, key_cols], qkv_ref[:, value_cols]
        grad = do_ref[:, here]
        masks = lane_masks((rows, 128))
        dq, dk, dv = [], 0.0, 0.0
        for h in range(2):
            head_queries = jnp.where(masks[h], queries, jnp.zeros_like(queries))
            head_grad = jnp.where(masks[h], grad, jnp.zeros_like(grad))
            scores = dot_nt(keys, head_queries) + mask_ref[...]
            weight = jnp.exp(scores - lse_ref[pair, pl.ds(h, 1), :])
            dweight = dot_nt(values, head_grad)
            delta = jnp.sum(weight * dweight, axis=0, keepdims=True)
            dscore = (weight * (dweight - delta)).astype(BF)
            dq.append(dot_tn(keys, dscore)[h * HEAD : (h + 1) * HEAD])
            dk = dk + dot_nn(dscore, head_queries)
            dv = dv + dot_nn(weight.astype(BF), head_grad)
        dq = jnp.concatenate(dq, axis=0).T * (HEAD ** -0.5)
        dsmall_ref[0:1, here] = column_sum(dq)
        dsmall_ref[1:2, here] = column_sum(dv)
        dproj_ref[:, here] = dq.astype(BF)
        dproj_ref[:, key_cols] = dk.astype(BF)
        dproj_ref[:, value_cols] = dv.astype(BF)

    loop(HEADS // 2, attend)
    weights.wait(3)

    def project(j):
        cols = tile_of(j)
        dx = dr_ref[:, cols] + dot_nt(dproj_ref[...], wqkv[cols, :])
        if block == 0:
            dx = dx + jnp.where(first_ref[...] > 0.5, 0.0, dnext_ref[:, cols])
        dx_ref[:, cols] = dx

    loop(width // TILE, project, 3)


def in_vmem(count):
    return [pl.BlockSpec(memory_space=pltpu.VMEM)] * count


def in_hbm(count):
    return [pl.BlockSpec(memory_space=pl.ANY)] * count


def shaped(shape, dtype=F32):
    return jax.ShapeDtypeStruct(shape, dtype)


def both_forward(hidden, seg, cotangent, weights, biases, gains, up_bias):
    rows, width = hidden.shape[0] // 2, hidden.shape[1]
    hidden_width = up_bias.shape[1]
    pieces = 2 * hidden_width // width + 4
    kept = (
        ((rows, 3 * width), BF), ((rows, width), BF), ((HEADS // 2, 2, rows), F32), ((rows, width), F32),
        ((rows, 128), F32), ((rows, width), BF), ((rows, hidden_width), BF), ((rows, hidden_width), BF),
        ((rows, width), F32), ((rows, 128), F32),
    )
    return pl.pallas_call(
        forward_kernel,
        out_shape=tuple(shaped((2,) + shape, dtype) for shape, dtype in kept) + (
            shaped((rows, width), BF), shaped((2 * rows, width), BF), shaped((pieces, width, width), BF),
            shaped((rows, width), BF), shaped((2, 16, width)),
        ),
        in_specs=in_hbm(1) + in_vmem(1) + in_hbm(1) + in_hbm(4) + in_vmem(3),
        out_specs=tuple(in_hbm(14) + in_vmem(1)),
        scratch_shapes=[
            pltpu.VMEM((2, pieces, width, width), BF),
            pltpu.VMEM((rows, width), BF),
        ] + [pltpu.VMEM(shape, dtype) for shape, dtype in kept] + [
            pltpu.VMEM((2, rows, width), BF),
            pltpu.VMEM((rows, width), F32),
            pltpu.VMEM((rows, width), F32),
            pltpu.VMEM((rows, rows), F32),
            pltpu.VMEM((rows, 128), F32),
            pltpu.SemaphoreType.DMA((pieces,)),
            pltpu.SemaphoreType.DMA((pieces,)),
            pltpu.SemaphoreType.DMA((pieces,)),
            pltpu.SemaphoreType.DMA((pieces,)),
            pltpu.SemaphoreType.DMA((10,)),
            pltpu.SemaphoreType.DMA((2,)),
            pltpu.SemaphoreType.DMA((3,)),
            pltpu.SemaphoreType.DMA((3,)),
        ],
        compiler_params=pltpu.CompilerParams(
            collective_id=1, has_side_effects=True, vmem_limit_bytes=VMEM_BYTES
        ),
        name="forward",
    )(hidden, seg, cotangent, *weights, jnp.swapaxes(biases, 0, 1), gains, up_bias)


def block_backward(block, cot, dnext, segr, segc, first, small, kept, weights):
    rows, width = cot.shape
    hidden_width = weights[4].shape[1]
    scratch = [pltpu.VMEM(w.shape, BF) for w in weights[::2]]
    return pl.pallas_call(
        functools.partial(backward_kernel, block),
        out_shape=(
            shaped((rows, width)), shaped((rows, 3 * width), BF), shaped((rows, width), BF),
            shaped((rows, hidden_width), BF), shaped((rows, width), BF), shaped((16, width)), shaped((1, hidden_width)),
        ),
        in_specs=in_vmem(14) + in_hbm(8),
        out_specs=tuple(in_vmem(7)),
        scratch_shapes=scratch + [
            pltpu.VMEM((rows, rows), F32), pltpu.VMEM((rows, width), F32), pltpu.VMEM((rows, width), F32),
            pltpu.VMEM((rows, width), BF), pltpu.SemaphoreType.DMA((4,)),
        ],
        compiler_params=pltpu.CompilerParams(vmem_limit_bytes=VMEM_BYTES),
        name="backward" + str(block),
    )(cot, dnext, segr, segc, first, small, *kept, *weights)


ORDERS = {
    "A": (0, 1, 2, 3), "B": (1, 0, 2, 3), "C": (2, 3, 0, 1), "D": (2, 3, 1, 0), "E": (0, 2, 3, 1), "F": (1, 2, 3, 0),
}
BITS = 4
PARTS = 1 << BITS
SLOTS = 4
SEQUENCE = (4, 5, 6, 7, 8, 9, 10, 11, 3, 0, 1, 2)
KINDS = ("AFEFAFEBABAB", "FFEBEFEFAFEB")
SCHEDULE = (
    1792, 1892, 1896, 1985, 2092, 2288, 2388, 2377, 2469, 2466, 2765, 2876, 3064, 3253, 3249, 3242,
    3334, 3408, 3612, 3630, 3715, 3723, 3815, 4121, 4114, 4184, 4221, 4189, 4276, 4310, 4410, 4624,
    4628, 4691, 4753, 4766, 4783, 4824, 4853, 4894, 4953, 4913, 4983, 5020, 5013, 5042, 5055, 5083,
    5216, 5375, 5430, 5508, 5593, 5778, 5800, 5793, 5818, 5786, 5772, 5779, 5811, 5819, 5787, 5801,
    5773, 5794, 5764, 5802, 5795, 5765, 5803, 5774, 5766, 5775, 5767, 5782, 5789, 5804, 5815, 5783,
    5797, 5790, 5805, 5760, 5791, 5798, 5806, 5761, 5799, 5768, 5807, 5762, 5769, 5763, 5770, 5771,
)


def owner(b, chunk):
    return (b + SEQUENCE.index(chunk)) % 2


def backward_sum_kernel(*refs):
    kept = refs[0:10]
    hidden, x1, cotangent, cot_theirs = refs[10:14]
    own_weights, theirs = refs[14:18], refs[18]
    seg_ref, smalls = refs[19:21]
    out_qkv, out_out, out_up, out_down, out_biases, out_gains, out_upb, grad_input = refs[21:29]
    (total, slots, stage, r1, r2, r3, r4, wring, gring, sring, lhs, turned, norm_buf, inv_buf, cot_buf, qkv_buf, lse_buf,
     low_buf, dz_buf, acc, dx_ref, mask_ref, first_ref, dsmall, small_sum, small_in,
     cross_send, cross_recv, done_send, done_recv, send, recv, small_send, small_recv, wsem, gsem, ssem, asem,
     grad_sem) = refs[29:]
    received = (r1, r2, r3, r4)
    rows, width = acc.shape
    share = total.shape[-2]
    wide = gring.shape[0]
    count = out_up.shape[1] // width
    sec, me = lax.axis_index("section"), lax.axis_index("dp")
    bits = [(me >> k) & 1 for k in range(BITS)]
    mine = pl.ds(pl.multiple_of(sec * rows, rows), rows)

    barrier = pltpu.get_barrier_semaphore()
    for k in range(BITS):
        pl.semaphore_signal(barrier, inc=1, device_id={"dp": me ^ (1 << k)}, device_id_type=MESH)
    pl.semaphore_signal(barrier, inc=1, device_id={"section": 1 - sec}, device_id_type=MESH)

    weight_list = []
    for b in (1, 0):
        for j in range(count):
            weight_list += [(b, 4 + count + j), (b, 4 + j)]
        weight_list += [(b, 3), (b, 0), (b, 1), (b, 2)]

    def weight_copy(n, own):
        which = weight_list[n][1]
        source = weight_piece(own_weights, which, width) if own else theirs.at[which]
        return pltpu.make_async_copy(source, wring.at[n % wring.shape[0]], wsem.at[n % wring.shape[0]])

    def weight_start(n):
        if n < len(weight_list):
            own = sec == weight_list[n][0]

            @pl.when(own)
            def _():
                weight_copy(n, True).start()

            @pl.when(jnp.logical_not(own))
            def _():
                weight_copy(n, False).start()

    taken = [0]

    def weight_next():
        n = taken[0]
        taken[0] += 1
        weight_copy(n, False).wait()
        return wring.at[n % wring.shape[0]]

    def weight_done():
        weight_start(taken[0] - 1 + wring.shape[0])

    QKV, O, LSE, N1, INV1, HLOW, G, SLOPE, N2, INV2, COT, X = range(12)
    targets = {
        COT: (cot_buf, 0), QKV: (qkv_buf, 1), O: (lhs, 2), LSE: (lse_buf, 3), N1: (norm_buf, 4), INV1: (inv_buf, 5),
        HLOW: (lhs, 2), N2: (norm_buf, 4), INV2: (inv_buf, 5), X: (lhs, 2),
    }

    def act(b, which, own=False):
        target, sem = targets[which]
        if which == COT:
            source = cotangent.at[0, mine] if own else cot_theirs
        elif which == X:
            source = x1 if b == 1 else hidden.at[mine]
        else:
            source = kept[which].at[b]
        return pltpu.make_async_copy(source, target, asem.at[sem])

    def ring(b, which, j):
        buf, sem = (gring, gsem) if which == G else (sring, ssem)
        source = kept[which].at[b, :, pl.ds(j * width, width)]
        return pltpu.make_async_copy(source, buf.at[j % wide], sem.at[j % wide])

    def place(part):
        return tuple((part >> (BITS - 1 - k)) & 1 for k in range(BITS))

    def across(chunk, slot):
        return pltpu.make_async_remote_copy(
            src_ref=slots.at[slot], dst_ref=total.at[chunk],
            send_sem=cross_send.at[chunk], recv_sem=cross_recv.at[chunk],
            device_id={"section": 1 - sec}, device_id_type=MESH,
        )

    def hand_over(b, chunk, slot):
        @pl.when(sec != owner(b, chunk))
        def _():
            across(chunk, slot).start()

    def exchange(b, chunk, phase):
        order = ORDERS[KINDS[b][SEQUENCE.index(chunk)]]
        at = [slice(None)] * BITS
        for done in range(phase):
            at[BITS - 1 - order[done]] = bits[order[done]]
        at[BITS - 1 - order[phase]] = 1 - bits[order[phase]]
        return pltpu.make_async_remote_copy(
            src_ref=total.at[(chunk,) + tuple(at)], dst_ref=received[phase].at[chunk],
            send_sem=send.at[chunk, phase], recv_sem=recv.at[chunk, phase],
            device_id={"dp": me ^ (1 << order[phase])}, device_id_type=MESH,
        )

    def finish(b, chunk, slot):
        @pl.when(sec == owner(b, chunk))
        def _():
            across(chunk, slot).wait_recv()

            def one(i):
                at = (i // 8, (i // 4) % 2, (i // 2) % 2, i % 2)
                total[(chunk,) + at] = total[(chunk,) + at] + slots[(slot,) + at]

            loop(PARTS, one, 4)
            exchange(b, chunk, 0).start()

        @pl.when(sec != owner(b, chunk))
        def _():
            across(chunk, slot).wait_send()

    def result_of(chunk):
        if chunk < 3:
            return out_qkv.at[:, pl.ds(chunk * width, width)]
        if chunk < 4:
            return out_out
        if chunk < 8:
            return out_up.at[:, pl.ds((chunk - 4) * width, width)]
        return out_down.at[pl.ds((chunk - 8) * share, share), :]

    def bring(chunk):
        return pltpu.make_async_remote_copy(
            src_ref=stage.at[SEQUENCE.index(chunk) // 2], dst_ref=result_of(chunk),
            send_sem=done_send.at[chunk], recv_sem=done_recv.at[chunk],
            device_id={"section": 1 - sec}, device_id_type=MESH,
        )

    def take(b, chunk, phase):
        order = ORDERS[KINDS[b][SEQUENCE.index(chunk)]]
        exchange(b, chunk, phase).wait()

        def one(i):
            at, inner, left = [None] * BITS, [], i
            for done in range(phase + 1):
                at[BITS - 1 - order[done]] = bits[order[done]]
            for d in reversed([d for d in range(BITS) if at[d] is None]):
                at[d] = left % 2
                inner.insert(0, at[d])
                left = left // 2
            at = (chunk,) + tuple(at)
            total[at] = total[at] + received[phase][(chunk,) + tuple(inner)]

        if phase < BITS - 1:
            loop(PARTS >> (phase + 1), one, min(4, PARTS >> (phase + 1)))
            exchange(b, chunk, phase + 1).start()
        else:
            value = total[(chunk,) + tuple(bits[BITS - 1 - d] for d in range(BITS))].astype(F32)
            value = value + received[phase][chunk].astype(F32)
            if owner(b, chunk) == b:
                result_of(chunk)[...] = value
            else:
                stage[SEQUENCE.index(chunk) // 2] = value
                bring(chunk).start()

    steps = [(n // 96, (n // 48) % 2, (n // 4) % 12, n % 4) for n in SCHEDULE]
    points = [0]

    def run_steps(chosen):
        for core in range(2):
            mine = [step for step in chosen if owner(step[1], step[2]) == core]
            if mine:

                @pl.when(sec == core)
                def _():
                    for _, b, chunk, phase in mine:
                        take(b, chunk, phase)

    def point():
        run_steps([step for step in steps if step[0] == points[0]])
        points[0] += 1

    def product(right, right_col, put):
        def one(n):
            cols = tile_of(n)
            rhs_cols = pl.ds(pl.multiple_of(right_col + n * TILE, TILE), TILE)
            result = dot_nn(turned[...], right[:, rhs_cols]).astype(BF)
            for piece in range(PARTS):
                slot, part = put(piece)
                slots[(slot,) + place(part) + (slice(None), cols)] = result[piece * share : (piece + 1) * share]

        loop(width // TILE, one, 3)

    def first_loads(b):
        @pl.when(sec == b)
        def _():
            act(b, COT, True).start()

        @pl.when(sec != b)
        def _():
            act(b, COT).start()

        act(b, N2).start()
        act(b, INV2).start()
        for j in range(wide):
            ring(b, G, j).start()
            ring(b, SLOPE, j).start()

    first_loads(1)
    act(1, HLOW).start()
    for n in range(wring.shape[0]):
        weight_start(n)
    spread_marks(seg_ref, sec, mask_ref, first_ref)
    dsmall[...] = jnp.zeros_like(dsmall)

    for b in (1, 0):
        small = smalls.at[b]
        act(b, QKV).start()
        act(b, LSE).start()
        act(b, COT).wait()
        act(b, N2).wait()
        act(b, INV2).wait()

        def norm_two(i):
            r = tile_of(i, ROWS)
            gradient = cot_buf[r, :].astype(F32)
            if b == 0:
                back = dx_ref[r, :].astype(BF).astype(F32)
                gradient = gradient + jnp.where(first_ref[r, 0:1] > 0.5, back, 0.0)
            normed = norm_buf[r, :]
            dr = norm_back(gradient * small[7:8, :], normed, inv_buf[r, 0:1])
            acc[r, :] = dr
            low_buf[r, :] = dr.astype(BF)
            dsmall[b, 7:8, :] += column_sum(gradient * normed)
            dsmall[b, 5:6, :] += column_sum(gradient)
            dsmall[b, 4:5, :] += column_sum(dr)

        loop(rows // ROWS, norm_two, 2)
        act(b, N1).start()
        act(b, INV1).start()
        if b == 1:
            pl.semaphore_wait(barrier, BITS + 1)
        point()
        act(b, HLOW).wait()
        turned[...] = lhs[...].T
        act(b, O).start()

        for j in range(count):
            down = weight_next()
            ring(b, SLOPE, j).wait()

            def narrow(t):
                cols = tile_of(t)
                dz = dot_nt(low_buf[...], down[cols, :]) * sring[j % wide, :, cols].astype(F32)
                dsmall[b, 8 + j : 9 + j, cols] = column_sum(dz)
                dz_buf[:, cols] = dz.astype(BF)

            loop(width // TILE, narrow, 3)
            weight_done()
            if j + wide < count:
                ring(b, SLOPE, j + wide).start()
            point()
            product(dz_buf, 0, lambda piece: (j, piece))
            hand_over(b, 4 + j, j)
            point()
            up = weight_next()

            def widen(t):
                cols = tile_of(t)
                acc[:, cols] += dot_nt(dz_buf[...], up[cols, :])

            loop(width // TILE, widen, 3)
            weight_done()
            point()
            if j > 0:
                finish(b, 3 + j, j - 1)
        act(b, N1).wait()
        act(b, INV1).wait()

        def norm_one(i):
            r = tile_of(i, ROWS)
            gradient = acc[r, :]
            normed = norm_buf[r, :]
            dr = norm_back(gradient * small[6:7, :], normed, inv_buf[r, 0:1])
            acc[r, :] = dr
            dz_buf[r, :] = dr.astype(BF)
            dsmall[b, 6:7, :] += column_sum(gradient * normed)
            dsmall[b, 3:4, :] += column_sum(gradient)
            dsmall[b, 2:3, :] += column_sum(dr)

        loop(rows // ROWS, norm_one, 2)
        finish(b, 7, 3)
        point()
        for j in range(count):
            ring(b, G, j).wait()
            turned[...] = gring[j % wide].T
            if j + wide < count:
                ring(b, G, j + wide).start()
            product(low_buf, 0, lambda piece: (piece % count, j * (PARTS // count) + piece // count))
            point()
        for c in range(count):
            hand_over(b, 8 + c, c)
        mixer = weight_next()

        def mix(t):
            cols = tile_of(t)
            cot_buf[:, cols] = dot_nt(dz_buf[...], mixer[cols, :]).astype(BF)

        loop(width // TILE, mix, 3)
        weight_done()
        act(b, QKV).wait()
        act(b, LSE).wait()
        point()

        def attend(pair):
            here = tile_of(pair, 128)
            key_cols = pl.ds(pl.multiple_of(width + pair * 128, 128), 128)
            value_cols = pl.ds(pl.multiple_of(2 * width + pair * 128, 128), 128)
            queries, keys, values = qkv_buf[:, here], qkv_buf[:, key_cols], qkv_buf[:, value_cols]
            grad = cot_buf[:, here]
            masks = lane_masks((rows, 128))
            dq, dk, dv = [], 0.0, 0.0
            for h in range(2):
                head_queries = jnp.where(masks[h], queries, jnp.zeros_like(queries))
                head_grad = jnp.where(masks[h], grad, jnp.zeros_like(grad))
                scores = dot_nt(keys, head_queries) + mask_ref[...]
                weight = jnp.exp(scores - lse_buf[pair, pl.ds(h, 1), :])
                dweight = dot_nt(values, head_grad)
                delta = jnp.sum(weight * dweight, axis=0, keepdims=True)
                dscore = (weight * (dweight - delta)).astype(BF)
                dq.append(dot_tn(keys, dscore)[h * HEAD : (h + 1) * HEAD])
                dk = dk + dot_nn(dscore, head_queries)
                dv = dv + dot_nn(weight.astype(BF), head_grad)
            dq = jnp.concatenate(dq, axis=0).T * (HEAD ** -0.5)
            dsmall[b, 0:1, here] = column_sum(dq)
            dsmall[b, 1:2, here] = column_sum(dv)
            qkv_buf[:, here] = dq.astype(BF)
            qkv_buf[:, key_cols] = dk.astype(BF)
            qkv_buf[:, value_cols] = dv.astype(BF)

        for third in range(3):
            loop(HEADS // 6, lambda i: attend(third * (HEADS // 6) + i), 2)
            if third == 0:
                finish(b, 8, 0)
                finish(b, 9, 1)
                point()
                act(b, O).wait()
                turned[...] = lhs[...].T
                act(b, X).start()
                product(dz_buf, 0, lambda piece: (0, piece))
                hand_over(b, 3, 0)
                point()
            elif third == 1:
                finish(b, 10, 2)
                finish(b, 11, 3)
                point()
            else:
                finish(b, 3, 0)
                point()
        act(b, X).wait()
        turned[...] = lhs[...].T
        if b == 1:
            act(0, HLOW).start()
            first_loads(0)
        point()

        for j in range(3):
            product(qkv_buf, j * width, lambda piece: (1 + j, piece))
            hand_over(b, j, 1 + j)
            point()
            block_weight = weight_next()

            def project(t):
                cols = tile_of(t)
                dx = acc[:, cols] + dot_nt(qkv_buf[:, j * width : (j + 1) * width], block_weight[cols, :])
                if j < 2:
                    acc[:, cols] = dx
                elif b == 1:
                    dx_ref[:, cols] = dx
                else:
                    dx_ref[:, cols] = dx + jnp.where(first_ref[:, 0:1] > 0.5, 0.0, dx_ref[:, cols])

            loop(width // TILE, project, 3)
            weight_done()
            point()
            if j > 0:
                finish(b, j - 1, j)
        finish(b, 2, 3)

    def own_grad():
        return pltpu.make_async_copy(dx_ref, grad_input.at[mine], grad_sem.at[0])

    def sent_grad():
        return pltpu.make_async_remote_copy(
            src_ref=dx_ref, dst_ref=grad_input.at[mine], send_sem=grad_sem.at[1], recv_sem=grad_sem.at[2],
            device_id={"section": 1 - sec}, device_id_type=MESH,
        )

    own_grad().start()
    sent_grad().start()

    def small_exchange(phase):
        target = {"section": 1 - sec} if phase == 0 else {"dp": me ^ (1 << (phase - 1))}
        source = dsmall.at[1 - sec] if phase == 0 else small_sum.at[phase]
        return pltpu.make_async_remote_copy(
            src_ref=source, dst_ref=small_in.at[phase], send_sem=small_send.at[phase], recv_sem=small_recv.at[phase],
            device_id=target, device_id_type=MESH,
        )

    def small_take(phase):
        small_exchange(phase).wait()
        before = dsmall[sec] if phase == 0 else small_sum[phase]
        if phase < BITS:
            small_sum[phase + 1] = before + small_in[phase]
            small_exchange(phase + 1).start()
        else:
            sums = before + small_in[phase]
            for part in range(PARTS):
                cut = slice(part * share, (part + 1) * share)
                line, start = part * count // PARTS, (part % (PARTS // count)) * count * share

                @pl.when(me == part)
                def _():
                    for k in range(out_biases.shape[0]):
                        out_biases[k] = sums[k : k + 1, cut]
                    out_gains[...] = sums[6:8, cut]
                    out_upb[...] = sums[8 + line : 9 + line, start : start + count * share]

    small_exchange(0).start()
    left = [[step for step in steps if step[0] >= points[0] and owner(step[1], step[2]) == core] for core in range(2)]
    for phase in range(BITS + 1):
        run_steps(left[0][:3] + left[1][:3])
        left = [left[0][3:], left[1][3:]]
        small_take(phase)
    run_steps(left[0] + left[1])
    for chunk in SEQUENCE[1::2]:
        bring(chunk).wait()
    own_grad().wait()
    sent_grad().wait()


def backward_sum(kept, hidden, x1, cotangent, cot_theirs, weights, theirs, seg, smalls):
    rows, width = x1.shape
    hidden_width = kept[6].shape[2]
    share = width // PARTS
    chunks = 2 * hidden_width // width + 4
    return pl.pallas_call(
        backward_sum_kernel,
        out_shape=(
            shaped((share, 3 * width)), shaped((share, width)), shaped((share, hidden_width)),
            shaped((hidden_width // PARTS, width)), shaped((6, 1, share)), shaped((2, share)),
            shaped((1, hidden_width // PARTS)), shaped((2 * rows, width)),
        ),
        in_specs=in_hbm(19) + in_vmem(2),
        out_specs=tuple(in_vmem(7) + in_hbm(1)),
        scratch_shapes=[
            pltpu.VMEM((chunks, 2, 2, 2, 2, share, width), BF),
            pltpu.VMEM((SLOTS, 2, 2, 2, 2, share, width), BF),
            pltpu.VMEM((chunks // 2, share, width), F32),
            pltpu.VMEM((chunks, 2, 2, 2, share, width), BF),
            pltpu.VMEM((chunks, 2, 2, share, width), BF),
            pltpu.VMEM((chunks, 2, share, width), BF),
            pltpu.VMEM((chunks, share, width), BF),
            pltpu.VMEM((3, width, width), BF),
            pltpu.VMEM((2, rows, width), BF),
            pltpu.VMEM((2, rows, width), BF),
            pltpu.VMEM((rows, width), BF),
            pltpu.VMEM((width, rows), BF),
            pltpu.VMEM((rows, width), F32),
            pltpu.VMEM((rows, 128), F32),
            pltpu.VMEM((rows, width), BF),
            pltpu.VMEM((rows, 3 * width), BF),
            pltpu.VMEM((HEADS // 2, 2, rows), F32),
            pltpu.VMEM((rows, width), BF),
            pltpu.VMEM((rows, width), BF),
            pltpu.VMEM((rows, width), F32),
            pltpu.VMEM((rows, width), F32),
            pltpu.VMEM((rows, rows), F32),
            pltpu.VMEM((rows, 128), F32),
            pltpu.VMEM((2, 16, width), F32),
            pltpu.VMEM((BITS + 1, 16, width), F32),
            pltpu.VMEM((BITS + 1, 16, width), F32),
            pltpu.SemaphoreType.DMA((chunks,)),
            pltpu.SemaphoreType.DMA((chunks,)),
            pltpu.SemaphoreType.DMA((chunks,)),
            pltpu.SemaphoreType.DMA((chunks,)),
            pltpu.SemaphoreType.DMA((chunks, BITS)),
            pltpu.SemaphoreType.DMA((chunks, BITS)),
            pltpu.SemaphoreType.DMA((BITS + 1,)),
            pltpu.SemaphoreType.DMA((BITS + 1,)),
            pltpu.SemaphoreType.DMA((3,)),
            pltpu.SemaphoreType.DMA((2,)),
            pltpu.SemaphoreType.DMA((2,)),
            pltpu.SemaphoreType.DMA((6,)),
            pltpu.SemaphoreType.DMA((3,)),
        ],
        compiler_params=pltpu.CompilerParams(
            collective_id=0, has_side_effects=True, vmem_limit_bytes=VMEM_BYTES
        ),
        name="backward_sum",
    )(*kept, hidden, x1, cotangent, cot_theirs, *weights, theirs, seg, smalls)


def sum_plainly(pieces, small):
    def scattered(names):
        both = jnp.stack([dot_tn(pieces[b][names[0]], pieces[b][names[1]]) for b in range(2)])
        own = lax.psum_scatter(both, "section", scatter_dimension=0, tiled=False)
        return lax.psum_scatter(own, "dp", scatter_dimension=0, tiled=True)

    own_small = lax.psum(lax.psum_scatter(small, "section", scatter_dimension=0, tiled=False), "dp")
    return tuple(scattered(names) for names in ((0, 1), (2, 3), (4, 5), (6, 7))) + (own_small,)


def hand_out_kernel(cuts, *refs):
    count = len(cuts)
    given, results, held, sems = refs[:count], refs[count : 2 * count], refs[2 * count : 3 * count], refs[3 * count]
    loads, stores = [], []
    for i, cut in enumerate(cuts):
        size = given[i].shape[0] // cut
        for part in range(cut):
            at = pl.ds(part * size, size)
            loads.append(pltpu.make_async_copy(given[i].at[at], held[i].at[at], sems.at[0, len(loads)]))
            stores.append(pltpu.make_async_copy(held[i].at[at], results[i].at[at], sems.at[1, len(stores)]))
    for load in loads:
        load.start()
    for load, store in zip(loads, stores):
        load.wait()
        store.start()
    for store in stores:
        store.wait()


def hand_out(results):
    count = len(results)
    cuts = [1] * count
    return pl.pallas_call(
        functools.partial(hand_out_kernel, cuts),
        out_shape=tuple(shaped(result.shape, result.dtype) for result in results),
        in_specs=in_hbm(count),
        out_specs=tuple(in_hbm(count)),
        scratch_shapes=[pltpu.VMEM(result.shape, result.dtype) for result in results] + [
            pltpu.SemaphoreType.DMA((2, sum(cuts)))
        ],
        compiler_params=pltpu.CompilerParams(vmem_limit_bytes=VMEM_BYTES),
        name="hand_out",
    )(*results)


def swap(value):
    return lax.ppermute(value, "section", [(0, 1), (1, 0)])


def backward_plainly(kept, hidden, x1, cotangent, cot_theirs, weights, theirs, seg, smalls):
    sec, me = lax.axis_index("section"), lax.axis_index("dp")
    share = hidden.shape[1] // lax.axis_size("dp")
    rows, width = x1.shape
    inputs = (lax.dynamic_slice_in_dim(hidden, sec * rows, rows, 0), x1)
    cot_own = lax.dynamic_slice_in_dim(cotangent[0], sec * rows, rows, 0)
    segments = lax.dynamic_index_in_dim(seg, sec, 0, False)
    segr, segc = segments.reshape(1, rows), segments.reshape(rows, 1)
    first = jnp.concatenate([jnp.ones((1,), F32), (segments[1:] != segments[:-1]).astype(F32)]).reshape(rows, 1)
    pairs = []
    for own in weights:
        pairs += [own[0], swap(own[0])]
    pieces, dsmalls, dnext = [None, None], [None, None], x1
    for block in (1, 0):
        qkv, o, lse, n1, inv1, hlow, g, slope, n2, inv2 = (member[block] for member in kept)
        cot = jnp.where(sec == block, cot_own, cot_theirs)
        dnext, dproj, da, dz, df, dsmall, dup = block_backward(
            block, cot, dnext, segr, segc, first, smalls[block], (qkv, o, lse, n1, inv1, slope, n2, inv2), pairs,
        )
        pieces[block] = (inputs[block], dproj, o, da, hlow, dz, g, df)
        dsmalls[block] = jnp.concatenate([dsmall[:8], dup.reshape(-1, width), jnp.zeros((4, width), F32)], axis=0)
    *sums, small = sum_plainly(pieces, jnp.stack(dsmalls))
    columns = lax.dynamic_slice_in_dim(small[:8], me * share, share, 1)
    up_share = kept[6].shape[2] // lax.axis_size("dp")
    upb = lax.dynamic_slice_in_dim(small[8:12].reshape(1, -1), me * up_share, up_share, 1)
    other = swap(dnext)
    grad_input = jnp.concatenate([jnp.where(sec == 0, dnext, other), jnp.where(sec == 0, other, dnext)], axis=0)
    return (*sums, columns[:6][:, None], columns[6:], upb, grad_input)


def local(hidden, segment_ids, cotangent, w_qkv, w_out, w_up, w_down, biases, gains, up_bias):
    width = hidden.shape[1]
    assert hidden.shape[0] == 2 * segment_ids.shape[1]
    weights = (w_qkv, w_out, w_up, w_down)
    *kept, x1, states, theirs, cot_theirs, smalls = both_forward(
        hidden, segment_ids, cotangent, weights, biases, gains, up_bias
    )
    fits = lax.axis_size("dp") == PARTS and width % (16 * PARTS) == 0
    backward = backward_sum if fits else backward_plainly
    *totals, upb, grad_input = backward(
        kept, hidden, x1, cotangent, cot_theirs, weights, theirs, segment_ids, smalls
    )
    results = (states, grad_input, *totals, upb)
    if fits:
        results = hand_out(results)
    states, grad_input, *products, bias_sums, gain_sums, upb = results
    products = tuple(member[None] for member in products)
    return (states[None], grad_input) + products + (jnp.swapaxes(bias_sums, 0, 1), gain_sums[None], upb)


def solution(mesh):
    placed = (
        P("dp", None),
        P("dp", None),
        P("section", "dp", None),
        P("section", None, None),
        P("section", None, None),
        P("section", None, None),
        P("section", None, None),
        P("section", None, None),
        P("section", None, None),
        P("section", None),
    )
    return jax.shard_map(
        local,
        mesh=mesh,
        in_specs=placed,
        out_specs=(
            P("section", "dp", None),
            P("dp", None),
            P("section", "dp", None),
            P("section", "dp", None),
            P("section", "dp", None),
            P("section", "dp", None),
            P("section", None, "dp"),
            P("section", None, "dp"),
            P("section", "dp"),
        ),
        check_vma=False,
    )
```

```python
import functools

import jax
import jax.numpy as jnp
from jax import lax
from jax.experimental import pallas as pl
from jax.experimental.pallas import tpu as pltpu
from jax.sharding import PartitionSpec as P

HEADS = 12
HEAD = 64
NORM_EPS = 1e-12
MASKED = -1e30
INV_ROOT_TWO = 0.7071067811865476
INV_ROOT_TAU = 0.3989422804014327
MESH = pl.DeviceIdType.MESH
BF = jnp.bfloat16
F32 = jnp.float32
TILE = 768
ROWS = 128
VMEM_BYTES = 60 * 1024 * 1024


def dot_nn(a, b):
    return lax.dot_general(a, b, (((1,), (0,)), ((), ())), preferred_element_type=F32)


def dot_nt(a, b):
    return lax.dot_general(a, b, (((1,), (1,)), ((), ())), preferred_element_type=F32)


def dot_tn(a, b):
    return lax.dot_general(a, b, (((0,), (0,)), ((), ())), preferred_element_type=F32)


def loop(count, body, unroll=1):
    def step(i, carry):
        body(i)
        return carry

    lax.fori_loop(0, count, step, 0, unroll=unroll)


def tile_of(i, size=TILE):
    return pl.ds(pl.multiple_of(i * size, size), size)


class Weights:
    def __init__(self, block, pairs, targets, sems):
        self.waits = []
        own = lax.axis_index("section") == block
        for n, ((mine, theirs), target) in enumerate(zip(pairs, targets)):
            sem = sems.at[n]

            @pl.when(own)
            def _():
                pltpu.make_async_copy(mine, target, sem).start()

            @pl.when(jnp.logical_not(own))
            def _():
                pltpu.make_async_copy(theirs, target, sem).start()

            self.waits.append(pltpu.make_async_copy(mine, target, sem))

    def wait(self, n):
        self.waits[n].wait()


def normed_rows(residue):
    centered = residue - jnp.mean(residue, axis=-1, keepdims=True)
    inv = lax.rsqrt(jnp.mean(centered * centered, axis=-1, keepdims=True) + NORM_EPS)
    return centered * inv, inv


def lane_masks(shape):
    lane = lax.broadcasted_iota(jnp.int32, shape, 1)
    return (lane < HEAD, lane >= HEAD)


def spread_marks(seg_ref, sec, mask_ref, first_ref):
    rows = mask_ref.shape[0]
    line = jnp.where(sec == 0, seg_ref[0:1, :], seg_ref[1:2, :]).astype(F32)
    column = jnp.broadcast_to(line, (128, rows)).T
    mask_ref[...] = jnp.where(column[:, 0:1] == line, 0.0, MASKED)
    lines = jnp.broadcast_to(line, (8, rows))
    before = pltpu.roll(lines, 1, 1)
    lane = lax.broadcasted_iota(jnp.int32, (8, rows), 1)
    marks = jnp.where((lines != before) | (lane == 0), 1.0, 0.0)
    first_ref[...] = jnp.broadcast_to(marks[0:1, :], (128, rows)).T


def weight_piece(refs, n, width):
    wqkv, wout, wup, wdown = refs
    if n < 3:
        return wqkv.at[0, :, pl.ds(n * width, width)]
    if n < 4:
        return wout.at[0]
    count = wdown.shape[1] // width
    if n < 4 + count:
        return wup.at[0, :, pl.ds((n - 4) * width, width)]
    return wdown.at[0, pl.ds((n - 4 - count) * width, width), :]


def forward_kernel(*refs):
    hidden, seg_ref, cotangent = refs[0:3]
    own_weights = refs[3:7]
    biases_ref, gains_ref, upb_ref = refs[7:10]
    (qkv_out, o_out, lse_out, n1_out, inv1_out, hlow_out, g_out, slope_out, n2_out, inv2_out,
     x1_out, states_out, theirs_out, cot_out, smalls) = refs[10:25]
    (wbuf, x_buf, qkv_buf, o_buf, lse_buf, n1_buf, inv1_buf, hlow_buf, g_buf, slope_buf, n2_buf, inv2_buf, y_buf,
     res, h_buf, mask_ref, first_ref,
     own_sem, piece_send, piece_recv, keep_sem, out_sem, x_sem, misc_send, misc_recv) = refs[25:]
    rows, width = x_buf.shape
    pieces = wbuf.shape[1]
    count = (pieces - 4) // 2
    sec = lax.axis_index("section")
    mine = pl.ds(pl.multiple_of(sec * rows, rows), rows)
    others = pl.ds(pl.multiple_of((1 - sec) * rows, rows), rows)
    partner = {"section": 1 - sec}

    def own_piece(n):
        return pltpu.make_async_copy(weight_piece(own_weights, n, width), wbuf.at[sec, n], own_sem.at[n])

    def sent_piece(n, block):
        return pltpu.make_async_remote_copy(
            src_ref=weight_piece(own_weights, n, width), dst_ref=wbuf.at[block, n],
            send_sem=piece_send.at[n], recv_sem=piece_recv.at[n], device_id=partner, device_id_type=MESH,
        )

    def kept_piece(n):
        return pltpu.make_async_copy(wbuf.at[1 - sec, n], theirs_out.at[n], keep_sem.at[n])

    def sent_small():
        return pltpu.make_async_remote_copy(
            src_ref=smalls.at[sec], dst_ref=smalls.at[sec],
            send_sem=misc_send.at[0], recv_sem=misc_recv.at[0], device_id=partner, device_id_type=MESH,
        )

    def sent_cot():
        return pltpu.make_async_remote_copy(
            src_ref=cotangent.at[0, others], dst_ref=cot_out,
            send_sem=misc_send.at[1], recv_sem=misc_recv.at[1], device_id=partner, device_id_type=MESH,
        )

    def sent_state(b):
        return pltpu.make_async_remote_copy(
            src_ref=y_buf.at[b], dst_ref=states_out.at[mine],
            send_sem=misc_send.at[2], recv_sem=misc_recv.at[2], device_id=partner, device_id_type=MESH,
        )

    def own_state(b):
        return pltpu.make_async_copy(y_buf.at[b], states_out.at[mine], x_sem.at[1])

    def piece(b, n):
        @pl.when(sec == b)
        def _():
            own_piece(n).wait()

        @pl.when(sec != b)
        def _():
            sent_piece(n, b).wait_recv()
            kept_piece(n).start()

        return wbuf.at[b, n]

    barrier = pltpu.get_barrier_semaphore()
    pl.semaphore_signal(barrier, inc=1, device_id=partner, device_id_type=MESH)
    load_x = pltpu.make_async_copy(hidden.at[mine], x_buf, x_sem.at[0])
    load_x.start()
    for n in range(pieces):
        own_piece(n).start()
    for k in range(biases_ref.shape[0]):
        smalls[sec, k : k + 1, :] = biases_ref[k]
    smalls[sec, 6:8, :] = gains_ref[0]
    for j in range(count):
        smalls[sec, 8 + j : 9 + j, :] = upb_ref[:, j * width : (j + 1) * width]
    smalls[sec, 8 + count :, :] = jnp.zeros((smalls.shape[1] - 8 - count, width), F32)
    pl.semaphore_wait(barrier, 1)
    sent_small().start()
    for n in range(pieces):
        sent_piece(n, sec).start()
    sent_cot().start()
    spread_marks(seg_ref, sec, mask_ref, first_ref)
    load_x.wait()
    sent_small().wait()

    buffers = (
        (qkv_buf, qkv_out), (o_buf, o_out), (lse_buf, lse_out), (n1_buf, n1_out), (inv1_buf, inv1_out),
        (hlow_buf, hlow_out), (g_buf, g_out), (slope_buf, slope_out), (n2_buf, n2_out), (inv2_buf, inv2_out),
    )
    QKV, O, LSE, N1, INV1, HLOW, G, SLOPE, N2, INV2 = range(10)

    def stored(b, which):
        return pltpu.make_async_copy(buffers[which][0], buffers[which][1].at[b], out_sem.at[which])

    def store(b, *names):
        for which in names:
            stored(b, which).start()

    def free(b, *names):
        if b == 1:
            for which in names:
                stored(0, which).wait()

    for b in range(2):
        small = smalls.at[b]
        free(b, QKV)
        for n in range(3):
            block = piece(b, n)

            def project(t):
                cols = tile_of(t)
                there = pl.ds(pl.multiple_of(n * width + t * TILE, TILE), TILE)
                value = dot_nn(x_buf[...], block[:, cols])
                if n == 0:
                    value = (value + small[0:1, cols]) * (HEAD ** -0.5)
                elif n == 2:
                    value = value + small[1:2, cols]
                qkv_buf[:, there] = value.astype(BF)

            loop(width // TILE, project, width // TILE)
        store(b, QKV)
        free(b, O, LSE)

        def attend(pair):
            queries = qkv_buf[:, tile_of(pair, 128)]
            keys = qkv_buf[:, pl.ds(pl.multiple_of(width + pair * 128, 128), 128)]
            values = qkv_buf[:, pl.ds(pl.multiple_of(2 * width + pair * 128, 128), 128)]
            masks = lane_masks((rows, 128))
            parts = []
            for h in range(2):
                scores = dot_nt(keys, jnp.where(masks[h], queries, jnp.zeros_like(queries))) + mask_ref[...]
                top = jnp.max(scores, axis=0, keepdims=True)
                weight = jnp.exp(scores - top)
                total = jnp.sum(weight, axis=0, keepdims=True)
                lse_buf[pair, pl.ds(h, 1), :] = top + jnp.log(total)
                result = dot_tn(values, weight.astype(BF))
                parts.append(result[h * HEAD : (h + 1) * HEAD] * (1.0 / total))
            o_buf[:, tile_of(pair, 128)] = jnp.concatenate(parts, axis=0).T.astype(BF)

        loop(HEADS // 2, attend, 2)
        store(b, O, LSE)
        mixer = piece(b, 3)

        def mix(t):
            cols = tile_of(t)
            res[:, cols] = x_buf[:, cols].astype(F32) + (dot_nn(o_buf[...], mixer[:, cols]) + small[2:3, cols])

        loop(width // TILE, mix, width // TILE)
        free(b, N1, INV1, HLOW)

        def norm_one(i):
            r = tile_of(i, ROWS)
            normed, inv = normed_rows(res[r, :])
            n1_buf[r, :] = normed
            inv1_buf[r, :] = jnp.broadcast_to(inv, (ROWS, 128))
            h = normed * small[6:7, :] + small[3:4, :]
            h_buf[r, :] = h + small[4:5, :]
            hlow_buf[r, :] = h.astype(BF)

        loop(rows // ROWS, norm_one, 2)
        store(b, N1, INV1, HLOW)
        free(b, G, SLOPE)
        for j in range(count):
            up = piece(b, 4 + j)

            def widen(t):
                cols = tile_of(t)
                there = pl.ds(pl.multiple_of(j * width + t * TILE, TILE), TILE)
                z = dot_nn(hlow_buf[...], up[:, cols]) + small[8 + j : 9 + j, cols]
                half = 0.5 * (1.0 + lax.erf(z * INV_ROOT_TWO))
                g_buf[:, there] = (z * half).astype(BF)
                slope_buf[:, there] = (half + z * jnp.exp(-0.5 * z * z) * INV_ROOT_TAU).astype(BF)

            loop(width // TILE, widen, width // TILE)
        store(b, G, SLOPE)
        downs = [piece(b, 4 + count + j) for j in range(count)] if b == 1 else []
        for j in range(count if b == 0 else 0):
            down = piece(b, 4 + count + j)

            def narrow(t):
                cols = tile_of(t)
                h_buf[:, cols] += dot_nn(g_buf[:, j * width : (j + 1) * width], down[:, cols])

            loop(width // TILE, narrow, width // TILE)

        def narrow_whole(t):
            cols = tile_of(t)
            value = h_buf[:, cols]
            for j, down in enumerate(downs):
                value = value + dot_nn(g_buf[:, j * width : (j + 1) * width], down[:, cols])
            h_buf[:, cols] = value

        if b == 1:
            loop(width // TILE, narrow_whole, width // TILE)
        free(b, N2, INV2)

        def norm_two(i):
            r = tile_of(i, ROWS)
            normed, inv = normed_rows(h_buf[r, :])
            n2_buf[r, :] = normed
            inv2_buf[r, :] = jnp.broadcast_to(inv, (ROWS, 128))
            y = (normed * small[7:8, :] + small[5:6, :]).astype(BF)
            y_buf[b, r, :] = y
            if b == 0:
                x = x_buf[r, :].astype(F32)
                x_buf[r, :] = jnp.where(first_ref[r, 0:1] > 0.5, y.astype(F32), x).astype(BF)

        loop(rows // ROWS, norm_two, 2)
        store(b, N2, INV2)
        if b == 0:
            pltpu.make_async_copy(x_buf, x1_out, x_sem.at[0]).start()

        @pl.when(sec == b)
        def _():
            own_state(b).start()

        @pl.when(sec != b)
        def _():
            sent_state(b).start()

    for which in range(10):
        stored(1, which).wait()
    pltpu.make_async_copy(x_buf, x1_out, x_sem.at[0]).wait()
    own_state(0).wait()
    sent_state(0).wait()
    sent_cot().wait()
    for n in range(pieces):
        sent_piece(n, sec).wait_send()
        kept_piece(n).wait()


def norm_back(gradient, normed, inv):
    return inv * (
        gradient
        - jnp.mean(gradient, axis=-1, keepdims=True)
        - normed * jnp.mean(gradient * normed, axis=-1, keepdims=True)
    )


def column_sum(v):
    return jnp.sum(v, axis=0, keepdims=True)


def backward_kernel(
    block,
    cot_ref, dnext_ref, segr_ref, segc_ref, first_ref, small_ref,
    qkv_ref, o_ref, lse_ref, n1_ref, inv1_ref, slope_ref, n2_ref, inv2_ref,
    wqkv_m, wqkv_t, wout_m, wout_t, wup_m, wup_t, wdown_m, wdown_t,
    dx_ref, dproj_ref, da_ref, dz_ref, df_ref, dsmall_ref, dup_ref,
    wqkv, wout, wup, wdown, mask_ref, dr_ref, dh_ref, do_ref, sems,
):
    rows, width = cot_ref.shape
    hidden_width = wup.shape[1]
    weights = Weights(
        block,
        ((wdown_m, wdown_t), (wup_m, wup_t), (wout_m, wout_t), (wqkv_m, wqkv_t)),
        (wdown, wup, wout, wqkv),
        sems,
    )
    mask_ref[...] = jnp.where(segc_ref[...] == segr_ref[...], 0.0, MASKED)
    dsmall_ref[...] = jnp.zeros_like(dsmall_ref)

    def norm_two(i):
        r = tile_of(i, ROWS)
        gradient = cot_ref[r, :].astype(F32)
        if block == 0:
            back = dnext_ref[r, :].astype(BF).astype(F32)
            gradient = gradient + jnp.where(first_ref[r, :] > 0.5, back, 0.0)
        normed = n2_ref[r, :]
        dr = norm_back(gradient * small_ref[7:8, :], normed, inv2_ref[r, 0:1])
        dr_ref[r, :] = dr
        df_ref[r, :] = dr.astype(BF)
        dsmall_ref[7:8, :] += column_sum(gradient * normed)
        dsmall_ref[5:6, :] += column_sum(gradient)
        dsmall_ref[4:5, :] += column_sum(dr)

    loop(rows // ROWS, norm_two, 2)
    weights.wait(0)

    def narrow(j):
        cols = tile_of(j)
        dz = dot_nt(df_ref[...], wdown[cols, :]) * slope_ref[:, cols].astype(F32)
        dup_ref[:, cols] = column_sum(dz)
        dz_ref[:, cols] = dz.astype(BF)

    loop(hidden_width // TILE, narrow)
    weights.wait(1)

    def widen(j):
        cols = tile_of(j)
        dh_ref[:, cols] = dr_ref[:, cols] + dot_nt(dz_ref[...], wup[cols, :])

    loop(width // TILE, widen, width // TILE)

    def norm_one(i):
        r = tile_of(i, ROWS)
        gradient = dh_ref[r, :]
        normed = n1_ref[r, :]
        dr = norm_back(gradient * small_ref[6:7, :], normed, inv1_ref[r, 0:1])
        dr_ref[r, :] = dr
        da_ref[r, :] = dr.astype(BF)
        dsmall_ref[6:7, :] += column_sum(gradient * normed)
        dsmall_ref[3:4, :] += column_sum(gradient)
        dsmall_ref[2:3, :] += column_sum(dr)

    loop(rows // ROWS, norm_one, 2)
    weights.wait(2)

    def mix(j):
        cols = tile_of(j)
        do_ref[:, cols] = dot_nt(da_ref[...], wout[cols, :]).astype(BF)

    loop(width // TILE, mix, width // TILE)

    def attend(pair):
        here = tile_of(pair, 128)
        key_cols = pl.ds(pl.multiple_of(width + pair * 128, 128), 128)
        value_cols = pl.ds(pl.multiple_of(2 * width + pair * 128, 128), 128)
        queries, keys, values = qkv_ref[:, here], qkv_ref[:, key_cols], qkv_ref[:, value_cols]
        grad = do_ref[:, here]
        masks = lane_masks((rows, 128))
        dq, dk, dv = [], 0.0, 0.0
        for h in range(2):
            head_queries = jnp.where(masks[h], queries, jnp.zeros_like(queries))
            head_grad = jnp.where(masks[h], grad, jnp.zeros_like(grad))
            scores = dot_nt(keys, head_queries) + mask_ref[...]
            weight = jnp.exp(scores - lse_ref[pair, pl.ds(h, 1), :])
            dweight = dot_nt(values, head_grad)
            delta = jnp.sum(weight * dweight, axis=0, keepdims=True)
            dscore = (weight * (dweight - delta)).astype(BF)
            dq.append(dot_tn(keys, dscore)[h * HEAD : (h + 1) * HEAD])
            dk = dk + dot_nn(dscore, head_queries)
            dv = dv + dot_nn(weight.astype(BF), head_grad)
        dq = jnp.concatenate(dq, axis=0).T * (HEAD ** -0.5)
        dsmall_ref[0:1, here] = column_sum(dq)
        dsmall_ref[1:2, here] = column_sum(dv)
        dproj_ref[:, here] = dq.astype(BF)
        dproj_ref[:, key_cols] = dk.astype(BF)
        dproj_ref[:, value_cols] = dv.astype(BF)

    loop(HEADS // 2, attend)
    weights.wait(3)

    def project(j):
        cols = tile_of(j)
        dx = dr_ref[:, cols] + dot_nt(dproj_ref[...], wqkv[cols, :])
        if block == 0:
            dx = dx + jnp.where(first_ref[...] > 0.5, 0.0, dnext_ref[:, cols])
        dx_ref[:, cols] = dx

    loop(width // TILE, project, width // TILE)


def in_vmem(count):
    return [pl.BlockSpec(memory_space=pltpu.VMEM)] * count


def in_hbm(count):
    return [pl.BlockSpec(memory_space=pl.ANY)] * count


def shaped(shape, dtype=F32):
    return jax.ShapeDtypeStruct(shape, dtype)


def both_forward(hidden, seg, cotangent, weights, biases, gains, up_bias):
    rows, width = hidden.shape[0] // 2, hidden.shape[1]
    hidden_width = up_bias.shape[1]
    pieces = 2 * hidden_width // width + 4
    kept = (
        ((rows, 3 * width), BF), ((rows, width), BF), ((HEADS // 2, 2, rows), F32), ((rows, width), F32),
        ((rows, 128), F32), ((rows, width), BF), ((rows, hidden_width), BF), ((rows, hidden_width), BF),
        ((rows, width), F32), ((rows, 128), F32),
    )
    return pl.pallas_call(
        forward_kernel,
        out_shape=tuple(shaped((2,) + shape, dtype) for shape, dtype in kept) + (
            shaped((rows, width), BF), shaped((2 * rows, width), BF), shaped((pieces, width, width), BF),
            shaped((rows, width), BF), shaped((2, 16, width)),
        ),
        in_specs=in_hbm(1) + in_vmem(1) + in_hbm(1) + in_hbm(4) + in_vmem(3),
        out_specs=tuple(in_hbm(14) + in_vmem(1)),
        scratch_shapes=[
            pltpu.VMEM((2, pieces, width, width), BF),
            pltpu.VMEM((rows, width), BF),
        ] + [pltpu.VMEM(shape, dtype) for shape, dtype in kept] + [
            pltpu.VMEM((2, rows, width), BF),
            pltpu.VMEM((rows, width), F32),
            pltpu.VMEM((rows, width), F32),
            pltpu.VMEM((rows, rows), F32),
            pltpu.VMEM((rows, 128), F32),
            pltpu.SemaphoreType.DMA((pieces,)),
            pltpu.SemaphoreType.DMA((pieces,)),
            pltpu.SemaphoreType.DMA((pieces,)),
            pltpu.SemaphoreType.DMA((pieces,)),
            pltpu.SemaphoreType.DMA((10,)),
            pltpu.SemaphoreType.DMA((2,)),
            pltpu.SemaphoreType.DMA((3,)),
            pltpu.SemaphoreType.DMA((3,)),
        ],
        compiler_params=pltpu.CompilerParams(
            collective_id=1, has_side_effects=True, vmem_limit_bytes=VMEM_BYTES
        ),
        name="forward",
    )(hidden, seg, cotangent, *weights, jnp.swapaxes(biases, 0, 1), gains, up_bias)


def block_backward(block, cot, dnext, segr, segc, first, small, kept, weights):
    rows, width = cot.shape
    hidden_width = weights[4].shape[1]
    scratch = [pltpu.VMEM(w.shape, BF) for w in weights[::2]]
    return pl.pallas_call(
        functools.partial(backward_kernel, block),
        out_shape=(
            shaped((rows, width)), shaped((rows, 3 * width), BF), shaped((rows, width), BF),
            shaped((rows, hidden_width), BF), shaped((rows, width), BF), shaped((16, width)), shaped((1, hidden_width)),
        ),
        in_specs=in_vmem(14) + in_hbm(8),
        out_specs=tuple(in_vmem(7)),
        scratch_shapes=scratch + [
            pltpu.VMEM((rows, rows), F32), pltpu.VMEM((rows, width), F32), pltpu.VMEM((rows, width), F32),
            pltpu.VMEM((rows, width), BF), pltpu.SemaphoreType.DMA((4,)),
        ],
        compiler_params=pltpu.CompilerParams(vmem_limit_bytes=VMEM_BYTES),
        name="backward" + str(block),
    )(cot, dnext, segr, segc, first, small, *kept, *weights)


ORDERS = {
    "A": (0, 1, 2, 3), "B": (1, 0, 2, 3), "C": (2, 3, 0, 1), "D": (2, 3, 1, 0), "E": (0, 2, 3, 1), "F": (1, 2, 3, 0),
}
BITS = 4
PARTS = 1 << BITS
SLOTS = 4
SEQUENCE = (4, 5, 6, 7, 8, 9, 10, 11, 3, 0, 1, 2)
KINDS = ("AFEFAFEBABAB", "FFEBEFEFAFEB")
SCHEDULE = (
    1792, 1892, 1896, 1985, 2092, 2288, 2388, 2377, 2469, 2466, 2765, 2876, 3064, 3253, 3249, 3242,
    3334, 3408, 3612, 3630, 3715, 3723, 3815, 4121, 4114, 4184, 4221, 4189, 4276, 4310, 4410, 4624,
    4628, 4691, 4753, 4766, 4783, 4824, 4853, 4894, 4953, 4913, 4983, 5020, 5013, 5042, 5055, 5083,
    5216, 5375, 5430, 5508, 5593, 5778, 5800, 5793, 5818, 5786, 5772, 5779, 5811, 5819, 5787, 5801,
    5773, 5794, 5764, 5802, 5795, 5765, 5803, 5774, 5766, 5775, 5767, 5782, 5789, 5804, 5815, 5783,
    5797, 5790, 5805, 5760, 5791, 5798, 5806, 5761, 5799, 5768, 5807, 5762, 5769, 5763, 5770, 5771,
)


def owner(b, chunk):
    return (b + SEQUENCE.index(chunk)) % 2


def backward_sum_kernel(*refs):
    kept = refs[0:10]
    hidden, x1, cotangent, cot_theirs = refs[10:14]
    own_weights, theirs = refs[14:18], refs[18]
    seg_ref, smalls = refs[19:21]
    out_qkv, out_out, out_up, out_down, out_biases, out_gains, out_upb, grad_input = refs[21:29]
    (total, slots, stage, r1, r2, r3, r4, wring, gring, sring, lhs, turned, norm_buf, inv_buf, cot_buf, qkv_buf, lse_buf,
     low_buf, dz_buf, acc, dx_ref, mask_ref, first_ref, dsmall, small_sum, small_in,
     cross_send, cross_recv, done_send, done_recv, send, recv, small_send, small_recv, wsem, gsem, ssem, asem,
     grad_sem) = refs[29:]
    received = (r1, r2, r3, r4)
    rows, width = acc.shape
    share = total.shape[-2]
    wide = gring.shape[0]
    count = out_up.shape[1] // width
    sec, me = lax.axis_index("section"), lax.axis_index("dp")
    bits = [(me >> k) & 1 for k in range(BITS)]
    mine = pl.ds(pl.multiple_of(sec * rows, rows), rows)

    barrier = pltpu.get_barrier_semaphore()
    for k in range(BITS):
        pl.semaphore_signal(barrier, inc=1, device_id={"dp": me ^ (1 << k)}, device_id_type=MESH)
    pl.semaphore_signal(barrier, inc=1, device_id={"section": 1 - sec}, device_id_type=MESH)

    weight_list = []
    for b in (1, 0):
        for j in range(count):
            weight_list += [(b, 4 + count + j), (b, 4 + j)]
        weight_list += [(b, 3), (b, 0), (b, 1), (b, 2)]

    def weight_copy(n, own):
        which = weight_list[n][1]
        source = weight_piece(own_weights, which, width) if own else theirs.at[which]
        return pltpu.make_async_copy(source, wring.at[n % wring.shape[0]], wsem.at[n % wring.shape[0]])

    def weight_start(n):
        if n < len(weight_list):
            own = sec == weight_list[n][0]

            @pl.when(own)
            def _():
                weight_copy(n, True).start()

            @pl.when(jnp.logical_not(own))
            def _():
                weight_copy(n, False).start()

    taken = [0]

    def weight_next():
        n = taken[0]
        taken[0] += 1
        weight_copy(n, False).wait()
        return wring.at[n % wring.shape[0]]

    def weight_done():
        weight_start(taken[0] - 1 + wring.shape[0])

    QKV, O, LSE, N1, INV1, HLOW, G, SLOPE, N2, INV2, COT, X = range(12)
    targets = {
        COT: (cot_buf, 0), QKV: (qkv_buf, 1), O: (lhs, 2), LSE: (lse_buf, 3), N1: (norm_buf, 4), INV1: (inv_buf, 5),
        HLOW: (lhs, 2), N2: (norm_buf, 4), INV2: (inv_buf, 5), X: (lhs, 2),
    }

    def act(b, which, own=False):
        target, sem = targets[which]
        if which == COT:
            source = cotangent.at[0, mine] if own else cot_theirs
        elif which == X:
            source = x1 if b == 1 else hidden.at[mine]
        else:
            source = kept[which].at[b]
        return pltpu.make_async_copy(source, target, asem.at[sem])

    def ring(b, which, j):
        buf, sem = (gring, gsem) if which == G else (sring, ssem)
        source = kept[which].at[b, :, pl.ds(j * width, width)]
        return pltpu.make_async_copy(source, buf.at[j % wide], sem.at[j % wide])

    def place(part):
        return tuple((part >> (BITS - 1 - k)) & 1 for k in range(BITS))

    def across(chunk, slot):
        return pltpu.make_async_remote_copy(
            src_ref=slots.at[slot], dst_ref=total.at[chunk],
            send_sem=cross_send.at[chunk], recv_sem=cross_recv.at[chunk],
            device_id={"section": 1 - sec}, device_id_type=MESH,
        )

    def hand_over(b, chunk, slot):
        @pl.when(sec != owner(b, chunk))
        def _():
            across(chunk, slot).start()

    def exchange(b, chunk, phase):
        order = ORDERS[KINDS[b][SEQUENCE.index(chunk)]]
        at = [slice(None)] * BITS
        for done in range(phase):
            at[BITS - 1 - order[done]] = bits[order[done]]
        at[BITS - 1 - order[phase]] = 1 - bits[order[phase]]
        return pltpu.make_async_remote_copy(
            src_ref=total.at[(chunk,) + tuple(at)], dst_ref=received[phase].at[chunk],
            send_sem=send.at[chunk, phase], recv_sem=recv.at[chunk, phase],
            device_id={"dp": me ^ (1 << order[phase])}, device_id_type=MESH,
        )

    def finish(b, chunk, slot):
        @pl.when(sec == owner(b, chunk))
        def _():
            across(chunk, slot).wait_recv()

            def one(i):
                at = (i // 8, (i // 4) % 2, (i // 2) % 2, i % 2)
                total[(chunk,) + at] = total[(chunk,) + at] + slots[(slot,) + at]

            loop(PARTS, one, 4)
            exchange(b, chunk, 0).start()

        @pl.when(sec != owner(b, chunk))
        def _():
            across(chunk, slot).wait_send()

    def result_of(chunk):
        if chunk < 3:
            return out_qkv.at[:, pl.ds(chunk * width, width)]
        if chunk < 4:
            return out_out
        if chunk < 8:
            return out_up.at[:, pl.ds((chunk - 4) * width, width)]
        return out_down.at[pl.ds((chunk - 8) * share, share), :]

    def bring(chunk):
        return pltpu.make_async_remote_copy(
            src_ref=stage.at[SEQUENCE.index(chunk) // 2], dst_ref=result_of(chunk),
            send_sem=done_send.at[chunk], recv_sem=done_recv.at[chunk],
            device_id={"section": 1 - sec}, device_id_type=MESH,
        )

    def take(b, chunk, phase):
        order = ORDERS[KINDS[b][SEQUENCE.index(chunk)]]
        exchange(b, chunk, phase).wait()

        def one(i):
            at, inner, left = [None] * BITS, [], i
            for done in range(phase + 1):
                at[BITS - 1 - order[done]] = bits[order[done]]
            for d in reversed([d for d in range(BITS) if at[d] is None]):
                at[d] = left % 2
                inner.insert(0, at[d])
                left = left // 2
            at = (chunk,) + tuple(at)
            total[at] = total[at] + received[phase][(chunk,) + tuple(inner)]

        if phase < BITS - 1:
            loop(PARTS >> (phase + 1), one, min(4, PARTS >> (phase + 1)))
            exchange(b, chunk, phase + 1).start()
        else:
            value = total[(chunk,) + tuple(bits[BITS - 1 - d] for d in range(BITS))].astype(F32)
            value = value + received[phase][chunk].astype(F32)
            if owner(b, chunk) == b:
                result_of(chunk)[...] = value
            else:
                stage[SEQUENCE.index(chunk) // 2] = value
                bring(chunk).start()

    steps = [(n // 96, (n // 48) % 2, (n // 4) % 12, n % 4) for n in SCHEDULE]
    points = [0]

    def run_steps(chosen):
        for core in range(2):
            mine = [step for step in chosen if owner(step[1], step[2]) == core]
            if mine:

                @pl.when(sec == core)
                def _():
                    for _, b, chunk, phase in mine:
                        take(b, chunk, phase)

    def point():
        run_steps([step for step in steps if step[0] == points[0]])
        points[0] += 1

    def product(right, right_col, put):
        def one(n):
            cols = tile_of(n)
            rhs_cols = pl.ds(pl.multiple_of(right_col + n * TILE, TILE), TILE)
            result = dot_nn(turned[...], right[:, rhs_cols]).astype(BF)
            for piece in range(PARTS):
                slot, part = put(piece)
                slots[(slot,) + place(part) + (slice(None), cols)] = result[piece * share : (piece + 1) * share]

        loop(width // TILE, one, width // TILE)

    def first_loads(b):
        @pl.when(sec == b)
        def _():
            act(b, COT, True).start()

        @pl.when(sec != b)
        def _():
            act(b, COT).start()

        act(b, N2).start()
        act(b, INV2).start()
        for j in range(wide):
            ring(b, G, j).start()
            ring(b, SLOPE, j).start()

    first_loads(1)
    act(1, HLOW).start()
    for n in range(wring.shape[0]):
        weight_start(n)
    spread_marks(seg_ref, sec, mask_ref, first_ref)
    dsmall[...] = jnp.zeros_like(dsmall)

    for b in (1, 0):
        small = smalls.at[b]
        act(b, QKV).start()
        act(b, LSE).start()
        act(b, COT).wait()
        act(b, N2).wait()
        act(b, INV2).wait()

        def norm_two(i):
            r = tile_of(i, ROWS)
            gradient = cot_buf[r, :].astype(F32)
            if b == 0:
                back = dx_ref[r, :].astype(BF).astype(F32)
                gradient = gradient + jnp.where(first_ref[r, 0:1] > 0.5, back, 0.0)
            normed = norm_buf[r, :]
            dr = norm_back(gradient * small[7:8, :], normed, inv_buf[r, 0:1])
            acc[r, :] = dr
            low_buf[r, :] = dr.astype(BF)
            dsmall[b, 7:8, :] += column_sum(gradient * normed)
            dsmall[b, 5:6, :] += column_sum(gradient)
            dsmall[b, 4:5, :] += column_sum(dr)

        loop(rows // ROWS, norm_two, 2)
        act(b, N1).start()
        act(b, INV1).start()
        if b == 1:
            pl.semaphore_wait(barrier, BITS + 1)
        point()
        act(b, HLOW).wait()
        turned[...] = lhs[...].T
        act(b, O).start()

        for j in range(count):
            down = weight_next()
            ring(b, SLOPE, j).wait()

            def narrow(t):
                cols = tile_of(t)
                dz = dot_nt(low_buf[...], down[cols, :]) * sring[j % wide, :, cols].astype(F32)
                dsmall[b, 8 + j : 9 + j, cols] = column_sum(dz)
                dz_buf[:, cols] = dz.astype(BF)

            loop(width // TILE, narrow, width // TILE)
            weight_done()
            if j + wide < count:
                ring(b, SLOPE, j + wide).start()
            point()
            product(dz_buf, 0, lambda piece: (j, piece))
            hand_over(b, 4 + j, j)
            point()
            up = weight_next()

            def widen(t):
                cols = tile_of(t)
                acc[:, cols] += dot_nt(dz_buf[...], up[cols, :])

            loop(width // TILE, widen, width // TILE)
            weight_done()
            point()
            if j > 0:
                finish(b, 3 + j, j - 1)
        act(b, N1).wait()
        act(b, INV1).wait()

        def norm_one(i):
            r = tile_of(i, ROWS)
            gradient = acc[r, :]
            normed = norm_buf[r, :]
            dr = norm_back(gradient * small[6:7, :], normed, inv_buf[r, 0:1])
            acc[r, :] = dr
            dz_buf[r, :] = dr.astype(BF)
            dsmall[b, 6:7, :] += column_sum(gradient * normed)
            dsmall[b, 3:4, :] += column_sum(gradient)
            dsmall[b, 2:3, :] += column_sum(dr)

        loop(rows // ROWS, norm_one, 2)
        finish(b, 7, 3)
        point()
        for j in range(count):
            ring(b, G, j).wait()
            turned[...] = gring[j % wide].T
            if j + wide < count:
                ring(b, G, j + wide).start()
            product(low_buf, 0, lambda piece: (piece % count, j * (PARTS // count) + piece // count))
            point()
        for c in range(count):
            hand_over(b, 8 + c, c)
        mixer = weight_next()

        def mix(t):
            cols = tile_of(t)
            cot_buf[:, cols] = dot_nt(dz_buf[...], mixer[cols, :]).astype(BF)

        loop(width // TILE, mix, width // TILE)
        weight_done()
        act(b, QKV).wait()
        act(b, LSE).wait()
        point()

        def attend(pair):
            here = tile_of(pair, 128)
            key_cols = pl.ds(pl.multiple_of(width + pair * 128, 128), 128)
            value_cols = pl.ds(pl.multiple_of(2 * width + pair * 128, 128), 128)
            queries, keys, values = qkv_buf[:, here], qkv_buf[:, key_cols], qkv_buf[:, value_cols]
            grad = cot_buf[:, here]
            masks = lane_masks((rows, 128))
            dq, dk, dv = [], 0.0, 0.0
            for h in range(2):
                head_queries = jnp.where(masks[h], queries, jnp.zeros_like(queries))
                head_grad = jnp.where(masks[h], grad, jnp.zeros_like(grad))
                scores = dot_nt(keys, head_queries) + mask_ref[...]
                weight = jnp.exp(scores - lse_buf[pair, pl.ds(h, 1), :])
                dweight = dot_nt(values, head_grad)
                delta = jnp.sum(weight * dweight, axis=0, keepdims=True)
                dscore = (weight * (dweight - delta)).astype(BF)
                dq.append(dot_tn(keys, dscore)[h * HEAD : (h + 1) * HEAD])
                dk = dk + dot_nn(dscore, head_queries)
                dv = dv + dot_nn(weight.astype(BF), head_grad)
            dq = jnp.concatenate(dq, axis=0).T * (HEAD ** -0.5)
            dsmall[b, 0:1, here] = column_sum(dq)
            dsmall[b, 1:2, here] = column_sum(dv)
            qkv_buf[:, here] = dq.astype(BF)
            qkv_buf[:, key_cols] = dk.astype(BF)
            qkv_buf[:, value_cols] = dv.astype(BF)

        for third in range(3):
            loop(HEADS // 6, lambda i: attend(third * (HEADS // 6) + i), 2)
            if third == 0:
                finish(b, 8, 0)
                finish(b, 9, 1)
                point()
                act(b, O).wait()
                turned[...] = lhs[...].T
                act(b, X).start()
                product(dz_buf, 0, lambda piece: (0, piece))
                hand_over(b, 3, 0)
                point()
            elif third == 1:
                finish(b, 10, 2)
                finish(b, 11, 3)
                point()
            else:
                finish(b, 3, 0)
                point()
        act(b, X).wait()
        turned[...] = lhs[...].T
        if b == 1:
            act(0, HLOW).start()
            first_loads(0)
        point()

        for j in range(3):
            product(qkv_buf, j * width, lambda piece: (1 + j, piece))
            hand_over(b, j, 1 + j)
            point()
            block_weight = weight_next()

            def project(t):
                cols = tile_of(t)
                dx = acc[:, cols] + dot_nt(qkv_buf[:, j * width : (j + 1) * width], block_weight[cols, :])
                if j < 2:
                    acc[:, cols] = dx
                elif b == 1:
                    dx_ref[:, cols] = dx
                else:
                    dx_ref[:, cols] = dx + jnp.where(first_ref[:, 0:1] > 0.5, 0.0, dx_ref[:, cols])

            loop(width // TILE, project, width // TILE)
            weight_done()
            point()
            if j > 0:
                finish(b, j - 1, j)
        finish(b, 2, 3)

    def own_grad():
        return pltpu.make_async_copy(dx_ref, grad_input.at[mine], grad_sem.at[0])

    def sent_grad():
        return pltpu.make_async_remote_copy(
            src_ref=dx_ref, dst_ref=grad_input.at[mine], send_sem=grad_sem.at[1], recv_sem=grad_sem.at[2],
            device_id={"section": 1 - sec}, device_id_type=MESH,
        )

    own_grad().start()
    sent_grad().start()

    def small_exchange(phase):
        target = {"section": 1 - sec} if phase == 0 else {"dp": me ^ (1 << (phase - 1))}
        source = dsmall.at[1 - sec] if phase == 0 else small_sum.at[phase]
        return pltpu.make_async_remote_copy(
            src_ref=source, dst_ref=small_in.at[phase], send_sem=small_send.at[phase], recv_sem=small_recv.at[phase],
            device_id=target, device_id_type=MESH,
        )

    def small_take(phase):
        small_exchange(phase).wait()
        before = dsmall[sec] if phase == 0 else small_sum[phase]
        if phase < BITS:
            small_sum[phase + 1] = before + small_in[phase]
            small_exchange(phase + 1).start()
        else:
            sums = before + small_in[phase]
            for part in range(PARTS):
                cut = slice(part * share, (part + 1) * share)
                line, start = part * count // PARTS, (part % (PARTS // count)) * count * share

                @pl.when(me == part)
                def _():
                    for k in range(out_biases.shape[0]):
                        out_biases[k] = sums[k : k + 1, cut]
                    out_gains[...] = sums[6:8, cut]
                    out_upb[...] = sums[8 + line : 9 + line, start : start + count * share]

    small_exchange(0).start()
    left = [[step for step in steps if step[0] >= points[0] and owner(step[1], step[2]) == core] for core in range(2)]
    for phase in range(BITS + 1):
        run_steps(left[0][:3] + left[1][:3])
        left = [left[0][3:], left[1][3:]]
        small_take(phase)
    run_steps(left[0] + left[1])
    for chunk in SEQUENCE[1::2]:
        bring(chunk).wait()
    own_grad().wait()
    sent_grad().wait()


def backward_sum(kept, hidden, x1, cotangent, cot_theirs, weights, theirs, seg, smalls):
    rows, width = x1.shape
    hidden_width = kept[6].shape[2]
    share = width // PARTS
    chunks = 2 * hidden_width // width + 4
    return pl.pallas_call(
        backward_sum_kernel,
        out_shape=(
            shaped((share, 3 * width)), shaped((share, width)), shaped((share, hidden_width)),
            shaped((hidden_width // PARTS, width)), shaped((6, 1, share)), shaped((2, share)),
            shaped((1, hidden_width // PARTS)), shaped((2 * rows, width)),
        ),
        in_specs=in_hbm(19) + in_vmem(2),
        out_specs=tuple(in_vmem(7) + in_hbm(1)),
        scratch_shapes=[
            pltpu.VMEM((chunks, 2, 2, 2, 2, share, width), BF),
            pltpu.VMEM((SLOTS, 2, 2, 2, 2, share, width), BF),
            pltpu.VMEM((chunks // 2, share, width), F32),
            pltpu.VMEM((chunks, 2, 2, 2, share, width), BF),
            pltpu.VMEM((chunks, 2, 2, share, width), BF),
            pltpu.VMEM((chunks, 2, share, width), BF),
            pltpu.VMEM((chunks, share, width), BF),
            pltpu.VMEM((3, width, width), BF),
            pltpu.VMEM((2, rows, width), BF),
            pltpu.VMEM((2, rows, width), BF),
            pltpu.VMEM((rows, width), BF),
            pltpu.VMEM((width, rows), BF),
            pltpu.VMEM((rows, width), F32),
            pltpu.VMEM((rows, 128), F32),
            pltpu.VMEM((rows, width), BF),
            pltpu.VMEM((rows, 3 * width), BF),
            pltpu.VMEM((HEADS // 2, 2, rows), F32),
            pltpu.VMEM((rows, width), BF),
            pltpu.VMEM((rows, width), BF),
            pltpu.VMEM((rows, width), F32),
            pltpu.VMEM((rows, width), F32),
            pltpu.VMEM((rows, rows), F32),
            pltpu.VMEM((rows, 128), F32),
            pltpu.VMEM((2, 16, width), F32),
            pltpu.VMEM((BITS + 1, 16, width), F32),
            pltpu.VMEM((BITS + 1, 16, width), F32),
            pltpu.SemaphoreType.DMA((chunks,)),
            pltpu.SemaphoreType.DMA((chunks,)),
            pltpu.SemaphoreType.DMA((chunks,)),
            pltpu.SemaphoreType.DMA((chunks,)),
            pltpu.SemaphoreType.DMA((chunks, BITS)),
            pltpu.SemaphoreType.DMA((chunks, BITS)),
            pltpu.SemaphoreType.DMA((BITS + 1,)),
            pltpu.SemaphoreType.DMA((BITS + 1,)),
            pltpu.SemaphoreType.DMA((3,)),
            pltpu.SemaphoreType.DMA((2,)),
            pltpu.SemaphoreType.DMA((2,)),
            pltpu.SemaphoreType.DMA((6,)),
            pltpu.SemaphoreType.DMA((3,)),
        ],
        compiler_params=pltpu.CompilerParams(
            collective_id=0, has_side_effects=True, vmem_limit_bytes=VMEM_BYTES
        ),
        name="backward_sum",
    )(*kept, hidden, x1, cotangent, cot_theirs, *weights, theirs, seg, smalls)


def sum_plainly(pieces, small):
    def scattered(names):
        both = jnp.stack([dot_tn(pieces[b][names[0]], pieces[b][names[1]]) for b in range(2)])
        own = lax.psum_scatter(both, "section", scatter_dimension=0, tiled=False)
        return lax.psum_scatter(own, "dp", scatter_dimension=0, tiled=True)

    own_small = lax.psum(lax.psum_scatter(small, "section", scatter_dimension=0, tiled=False), "dp")
    return tuple(scattered(names) for names in ((0, 1), (2, 3), (4, 5), (6, 7))) + (own_small,)


def hand_out_kernel(cuts, *refs):
    count = len(cuts)
    given, results, held, sems = refs[:count], refs[count : 2 * count], refs[2 * count : 3 * count], refs[3 * count]
    loads, stores = [], []
    for i, cut in enumerate(cuts):
        size = given[i].shape[0] // cut
        for part in range(cut):
            at = pl.ds(part * size, size)
            loads.append(pltpu.make_async_copy(given[i].at[at], held[i].at[at], sems.at[0, len(loads)]))
            stores.append(pltpu.make_async_copy(held[i].at[at], results[i].at[at], sems.at[1, len(stores)]))
    for load in loads:
        load.start()
    for load, store in zip(loads, stores):
        load.wait()
        store.start()
    for store in stores:
        store.wait()


def hand_out(results):
    count = len(results)
    cuts = [1] * count
    return pl.pallas_call(
        functools.partial(hand_out_kernel, cuts),
        out_shape=tuple(shaped(result.shape, result.dtype) for result in results),
        in_specs=in_hbm(count),
        out_specs=tuple(in_hbm(count)),
        scratch_shapes=[pltpu.VMEM(result.shape, result.dtype) for result in results] + [
            pltpu.SemaphoreType.DMA((2, sum(cuts)))
        ],
        compiler_params=pltpu.CompilerParams(vmem_limit_bytes=VMEM_BYTES),
        name="hand_out",
    )(*results)


def swap(value):
    return lax.ppermute(value, "section", [(0, 1), (1, 0)])


def backward_plainly(kept, hidden, x1, cotangent, cot_theirs, weights, theirs, seg, smalls):
    sec, me = lax.axis_index("section"), lax.axis_index("dp")
    share = hidden.shape[1] // lax.axis_size("dp")
    rows, width = x1.shape
    inputs = (lax.dynamic_slice_in_dim(hidden, sec * rows, rows, 0), x1)
    cot_own = lax.dynamic_slice_in_dim(cotangent[0], sec * rows, rows, 0)
    segments = lax.dynamic_index_in_dim(seg, sec, 0, False)
    segr, segc = segments.reshape(1, rows), segments.reshape(rows, 1)
    first = jnp.concatenate([jnp.ones((1,), F32), (segments[1:] != segments[:-1]).astype(F32)]).reshape(rows, 1)
    pairs = []
    for own in weights:
        pairs += [own[0], swap(own[0])]
    pieces, dsmalls, dnext = [None, None], [None, None], x1
    for block in (1, 0):
        qkv, o, lse, n1, inv1, hlow, g, slope, n2, inv2 = (member[block] for member in kept)
        cot = jnp.where(sec == block, cot_own, cot_theirs)
        dnext, dproj, da, dz, df, dsmall, dup = block_backward(
            block, cot, dnext, segr, segc, first, smalls[block], (qkv, o, lse, n1, inv1, slope, n2, inv2), pairs,
        )
        pieces[block] = (inputs[block], dproj, o, da, hlow, dz, g, df)
        dsmalls[block] = jnp.concatenate([dsmall[:8], dup.reshape(-1, width), jnp.zeros((4, width), F32)], axis=0)
    *sums, small = sum_plainly(pieces, jnp.stack(dsmalls))
    columns = lax.dynamic_slice_in_dim(small[:8], me * share, share, 1)
    up_share = kept[6].shape[2] // lax.axis_size("dp")
    upb = lax.dynamic_slice_in_dim(small[8:12].reshape(1, -1), me * up_share, up_share, 1)
    other = swap(dnext)
    grad_input = jnp.concatenate([jnp.where(sec == 0, dnext, other), jnp.where(sec == 0, other, dnext)], axis=0)
    return (*sums, columns[:6][:, None], columns[6:], upb, grad_input)


def local(hidden, segment_ids, cotangent, w_qkv, w_out, w_up, w_down, biases, gains, up_bias):
    width = hidden.shape[1]
    assert hidden.shape[0] == 2 * segment_ids.shape[1]
    weights = (w_qkv, w_out, w_up, w_down)
    *kept, x1, states, theirs, cot_theirs, smalls = both_forward(
        hidden, segment_ids, cotangent, weights, biases, gains, up_bias
    )
    fits = lax.axis_size("dp") == PARTS and width % (16 * PARTS) == 0
    backward = backward_sum if fits else backward_plainly
    *totals, upb, grad_input = backward(
        kept, hidden, x1, cotangent, cot_theirs, weights, theirs, segment_ids, smalls
    )
    results = (states, grad_input, *totals, upb)
    if fits:
        results = hand_out(results)
    states, grad_input, *products, bias_sums, gain_sums, upb = results
    products = tuple(member[None] for member in products)
    return (states[None], grad_input) + products + (jnp.swapaxes(bias_sums, 0, 1), gain_sums[None], upb)


def solution(mesh):
    placed = (
        P("dp", None),
        P("dp", None),
        P("section", "dp", None),
        P("section", None, None),
        P("section", None, None),
        P("section", None, None),
        P("section", None, None),
        P("section", None, None),
        P("section", None, None),
        P("section", None),
    )
    return jax.shard_map(
        local,
        mesh=mesh,
        in_specs=placed,
        out_specs=(
            P("section", "dp", None),
            P("dp", None),
            P("section", "dp", None),
            P("section", "dp", None),
            P("section", "dp", None),
            P("section", "dp", None),
            P("section", None, "dp"),
            P("section", None, "dp"),
            P("section", "dp"),
        ),
        check_vma=False,
    )
```
